32 devices in a mesh: groups: 2 (over y), row: 4 (over z), col: 4 (over x, core).
Axes of the slice: x: 2, y: 2, z: 4, core: 2. Of those that a mesh axis runs over, the one named last changes fastest.
Arguments:
- positions: float32 [4096, 3, 128], P(('groups', 'row', 'col')), parts along dimension 0, may hold values from -6 to 6
- normals: float32 [4096, 3, 128], P(('groups', 'row', 'col')), parts along dimension 0, may hold values from -6 to 6
- curvature: float32 [4096, 128], P(('groups', 'row', 'col')), parts along dimension 0, may hold values from 0.5 to 3
- pair_targets: int32 [32, 512], P(('groups', 'row', 'col')), parts along dimension 0, may hold values from 0 to 511, as said below
- pair_sources: int32 [32, 512], P(('groups', 'row', 'col')), parts along dimension 0, may hold values from 0 to 511
- pair_count: int32 [32], P(('groups', 'row', 'col')), parts along dimension 0, may hold values from 64 to 512, as said below
- node_counts: int32 [512, 8], P('groups'), parts along dimension 0, may hold values from 1 to 128, 642 in all within a row
- drop_clusters: int32 [512, 8], P('groups'), parts along dimension 0, may hold values from 0 to 2047, as said below
- drop_owner: int32 [512], P('groups'), parts along dimension 0, may hold values from 0 to 15, as said below
Outputs:
- drop_velocity: float32 [4096, 3, 128], P(('groups', 'row', 'col')), parts along dimension 0
The draws below stay inside these ranges and needn't reach their ends.
There are 2 independent parts, one for each index of `groups`. The reference program is written for one: setup_inputs(seed, part) draws one part's arguments, and reference() takes and returns one part's arrays. A program takes and returns all parts, laid end to end along the dimension named above; each array names one. Nothing has to cross between parts.
Inputs may be any that keep to these rules, and one draw needn't show every extreme that they name: `drop_clusters`: every cluster of 0 to 2047 appears exactly once. Of the 128 clusters of one device, at most 16 belong to drops of any one owner, and this many is reached. `drop_owner`: every device owns exactly 16 drops. `pair_count`: the largest count is reached on some device; list entries past a device's count are not pairs. In each device's list, at most 256 entries have the same value of pair_targets // 128, and every device's list reaches this many for some value. `node_counts`: each drop's counts sum to 642.
All inputs are finite; a program needn't handle non-finite values.
Results may differ from the reference program's by a relative error of at most 0.0003.
Values sent between devices are 32-bit elements; how exact they have to be, the bound alone decides.
No kernel may reach another device: no remote copies, remote signals or barrier semaphores. Data moves between devices by JAX's collectives and lax.ppermute only.
A program may use at most 64 MiB of HBM per device.

```python
import math
import jax
import jax.numpy as jnp
import numpy as np
from jax import lax

P_SIZE = 128
CPD = 8
NODES_DROP = 642
CL_DEV = 128
PAIRS_DEV = 512
DEVS = 16
CLUSTERS = 2048
DROP_DEV = 16
DROPS = 256
CAP = 16
TCAP = 256
N_ROW = 4
N_COL = 4


def cluster_layout(key):
    base = jax.random.fold_in(key, 7)
    first_key, second_key, third_key = jax.random.split(base, 3)
    group_count = CL_DEV // CAP
    ranking = jax.random.permutation(first_key, DEVS).astype(jnp.int32)
    ranking = ranking.at[1].set(-2)
    ranking = ranking.at[DEVS // 2].set(-1)
    offsets = jnp.argsort(ranking, stable=True)[:group_count].astype(jnp.int32)
    owners = jnp.arange(DEVS, dtype=jnp.int32)[:, None]
    arrival = jnp.arange(CL_DEV, dtype=jnp.int32)[None, :]
    group_of = arrival // CAP
    anchor = (owners - offsets[group_of]) % DEVS
    homes = anchor * CL_DEV + arrival
    shuffle_keys = jax.random.split(second_key, DEVS)
    shuffles = jax.vmap(lambda one_key: jax.random.permutation(one_key, CL_DEV))(shuffle_keys)
    homes = jnp.take_along_axis(homes, shuffles.astype(jnp.int32), axis=1)
    grouped = homes.reshape(DEVS * DROP_DEV, CPD)
    labels = jax.random.permutation(third_key, DROPS).astype(jnp.int32)
    clusters = jnp.zeros((DROPS, CPD), jnp.int32).at[labels].set(grouped)
    owner_of = jnp.zeros((DROPS,), jnp.int32).at[labels].set(jnp.arange(DROPS, dtype=jnp.int32) // DROP_DEV)
    return (clusters, owner_of)


def draw_drop_clusters(key, part):
    return cluster_layout(key)[0]


def draw_drop_owner(key, part):
    return cluster_layout(key)[1]


def draw_pair_count(key, part):
    base = jax.random.fold_in(key, 11)
    first_key, second_key = jax.random.split(base, 2)
    counts = jax.random.randint(first_key, (DEVS,), PAIRS_DEV // 8, PAIRS_DEV // 2 + 1, dtype=jnp.int32)
    busiest = jax.random.randint(second_key, (), 0, DEVS, dtype=jnp.int32)
    return counts.at[busiest].set(PAIRS_DEV)


def draw_pair_targets(key, part):
    base = jax.random.fold_in(key, 13)
    first_key, second_key, third_key = jax.random.split(base, 3)
    perm_keys = jax.random.split(first_key, DEVS)
    orders = jax.vmap(lambda one_key: jax.random.permutation(one_key, PAIRS_DEV))(perm_keys).astype(jnp.int32)
    shifts = jax.random.randint(second_key, (DEVS, 1), 0, N_COL, dtype=jnp.int32)
    home_col = (orders // TCAP + shifts) % N_COL
    within = jax.random.randint(third_key, (DEVS, PAIRS_DEV), 0, CL_DEV, dtype=jnp.int32)
    return home_col * CL_DEV + within


def place_ends(values, stream_key, low, largest):
    index_at = [jax.random.randint(jax.random.fold_in(stream_key, axis), (), 0, length) for axis, length in enumerate(values.shape)]
    main_axis = values.shape.index(max(values.shape))
    neighbour = index_at[:main_axis] + [(index_at[main_axis] + 1) % values.shape[main_axis]] + index_at[main_axis + 1:]
    return values.at[tuple(index_at)].set(low).at[tuple(neighbour)].set(largest)


def level_of(own_key, shape, pieces, smallest, high):
    def one(axis_at, shards_of):
        steps = jax.random.uniform(jax.random.fold_in(jax.random.fold_in(own_key, 6), axis_at), (shards_of,), jnp.float32, smallest / len(pieces), high / len(pieces))
        return jnp.repeat(jnp.exp(steps), shape[axis_at] // shards_of).reshape((-1,) + (1,) * (len(shape) - axis_at - 1))

    loudness = one(*pieces[0])
    for cut in pieces[1:]:
        loudness = loudness * one(*cut)
    return loudness


def length_profile(count, total, most, slope):
    portions = [(1 << 20) // math.isqrt(grade ** slope) + 1 for grade in range(2, count + 1)]
    surplus, given = total - most - (count - 1), [1] * (count - 1)
    while surplus > 0:
        free = [i for i in range(count - 1) if given[i] < most]
        mass, left = sum([portions[i] for i in free]), surplus
        for i in free:
            more = min(most - given[i], max(1, left * portions[i] // mass), surplus)
            given[i] = given[i] + more
            surplus = surplus - more
    return np.array([most] + given)


def uneven_parts(stream_key, number_of, total, most, skew):
    if number_of == 2:
        one = jax.random.randint(stream_key, (), max(1, total - most), min(most, total - 1) + 1)
        return jnp.stack([one, total - one])
    tallies = jnp.asarray(length_profile(number_of, total, most, skew), jnp.int32)
    pairs = (number_of - 1) // 2
    source_of, sink = tallies[1:1 + 2 * pairs:2], tallies[2:2 + 2 * pairs:2]
    slack = jnp.minimum(source_of - 1, most - sink)
    moved = jax.random.randint(jax.random.fold_in(stream_key, 1), (pairs,), 0, 1 << 20) % (slack + 1)
    tallies = tallies.at[1:1 + 2 * pairs:2].set(source_of - moved).at[2:2 + 2 * pairs:2].set(sink + moved)
    return tallies[jax.random.permutation(jax.random.fold_in(stream_key, 2), number_of)]


def gaussian(key, extent, deviation, bound, pieces=(), kind=jnp.bfloat16):
    factor_of = level_of(key, extent, pieces, -0.22, 0.18) if pieces else 1.0
    drawn = jax.random.normal(key, extent, jnp.float32) * deviation * factor_of
    return jnp.minimum(jnp.maximum(drawn, -bound), bound).astype(kind)


def setup_inputs(seed: int = 0, part: int = 0) -> dict:
    splits = jax.random.split(jax.random.key(seed), 10)
    part_keys = jax.random.split(jax.random.fold_in(splits[9], part), 10)
    return {
        "positions": gaussian(part_keys[0], (CLUSTERS, 3, P_SIZE), 1.0, 6.0, ((0, 16),), jnp.float32),
        "normals": gaussian(part_keys[1], (CLUSTERS, 3, P_SIZE), 1.0, 6.0, ((0, 16),), jnp.float32),
        "curvature": jnp.clip(0.5 + 2.5 * jax.random.uniform(part_keys[2], (CLUSTERS, P_SIZE), jnp.float32) ** level_of(part_keys[2], (CLUSTERS, P_SIZE), ((0, 16),), -0.2, 0.2), 0.5, 3.0),
        "pair_targets": draw_pair_targets(jax.random.fold_in(jax.random.fold_in(splits[9], part), 71), part),
        "pair_sources": place_ends(jax.random.randint(part_keys[4], (DEVS, PAIRS_DEV), 0, N_ROW * CL_DEV), jax.random.fold_in(part_keys[4], 1), 0, (N_ROW * CL_DEV) - 1).astype(jnp.int32),
        "pair_count": draw_pair_count(jax.random.fold_in(jax.random.fold_in(splits[9], part), 71), part),
        "node_counts": jax.vmap(lambda own: uneven_parts(own, CPD, NODES_DROP, P_SIZE, 1))(jax.random.split(part_keys[6], DROPS)).reshape((DROPS, CPD)).astype(jnp.int32),
        "drop_clusters": draw_drop_clusters(jax.random.fold_in(jax.random.fold_in(splits[9], part), 71), part),
        "drop_owner": draw_drop_owner(jax.random.fold_in(jax.random.fold_in(splits[9], part), 71), part),
    }


pair_block = 32
regular_sq = 0.0025
stokes_scale = 1.0 / (8.0 * math.pi)

def stokeslet(target_pos, source_pos, source_force):
    delta_x = target_pos[:, 0, :, None] - source_pos[:, 0, None, :]
    delta_y = target_pos[:, 1, :, None] - source_pos[:, 1, None, :]
    delta_z = target_pos[:, 2, :, None] - source_pos[:, 2, None, :]
    dist_sq = delta_x * delta_x + delta_y * delta_y + delta_z * delta_z
    inverse = lax.rsqrt(dist_sq + regular_sq)
    weight = inverse * inverse * inverse
    isotropic = (dist_sq + 2.0 * regular_sq) * weight
    force_x = source_force[:, 0, None, :]
    force_y = source_force[:, 1, None, :]
    force_z = source_force[:, 2, None, :]
    project = (delta_x * force_x + delta_y * force_y + delta_z * force_z) * weight
    speed_x = lax.optimization_barrier(jnp.sum(isotropic * force_x + project * delta_x, axis=2))
    speed_y = lax.optimization_barrier(jnp.sum(isotropic * force_y + project * delta_y, axis=2))
    speed_z = lax.optimization_barrier(jnp.sum(isotropic * force_z + project * delta_z, axis=2))
    return stokes_scale * jnp.stack([speed_x, speed_y, speed_z], axis=1)

def reference(positions, normals, curvature, pair_targets, pair_sources, pair_count, node_counts, drop_clusters, drop_owner):
    entries = DROPS * CPD
    flat_clusters = drop_clusters.reshape(-1)
    flat_counts = node_counts.reshape(-1)
    home_counts = jnp.zeros((entries,), jnp.int32).at[flat_clusters].set(flat_counts)
    slot_index = jnp.arange(P_SIZE, dtype=jnp.int32)
    home_live = (slot_index[None, :] < home_counts[:, None]).astype(jnp.float32)
    forces = (curvature * home_live)[:, None, :] * normals
    devices = jnp.arange(DEVS, dtype=jnp.int32)
    row_of = devices // N_COL
    col_of = devices % N_COL
    target_global = row_of[:, None] * (N_COL * CL_DEV) + pair_targets
    source_global = (pair_sources // CL_DEV * N_COL + col_of[:, None]) * CL_DEV + pair_sources % CL_DEV

    def per_device(speeds, items):
        target_row, source_row, limit = items
        blocks = (limit + pair_block - 1) // pair_block

        def accumulate(block_number, totals):
            picked = block_number * pair_block + jnp.arange(pair_block, dtype=jnp.int32)
            active = picked < limit
            picked = jnp.minimum(picked, PAIRS_DEV - 1)
            target_ids = target_row[picked]
            source_ids = source_row[picked]
            contrib = stokeslet(positions[target_ids], positions[source_ids], forces[source_ids])
            contrib = contrib * active.astype(jnp.float32)[:, None, None]
            return totals.at[target_ids].add(contrib)
        return (lax.fori_loop(0, blocks, accumulate, speeds), None)
    speeds, unused = lax.scan(per_device, jnp.zeros((entries, 3, P_SIZE), jnp.float32), (target_global, source_global, pair_count))
    owner_order = jnp.argsort(drop_owner, stable=True)
    ordered_clusters = drop_clusters[owner_order].reshape(-1)
    ordered_counts = node_counts[owner_order].reshape(-1)
    owned_live = (slot_index[None, :] < ordered_counts[:, None]).astype(jnp.float32)
    return speeds[ordered_clusters] * owned_live[:, None, :]
```

```python
import functools
import math

import jax
import jax.numpy as jnp
from jax import lax
from jax.experimental import pallas as pl
from jax.experimental.pallas import tpu as pltpu
from jax.sharding import PartitionSpec as P

f32 = jnp.float32
bf16 = jnp.bfloat16
i32 = jnp.int32
regular_sq = 0.0025
length_scale = 1.0 / math.sqrt(regular_sq)
force_scale = length_scale / (8.0 * math.pi)
unroll = 8
vmem_limit = 48 * 2**20
vmem = pl.BlockSpec(memory_space=pltpu.VMEM)
smem = pl.BlockSpec(memory_space=pltpu.SMEM)


def split3(value):
    high = value.astype(bf16)
    rest = value - high.astype(f32)
    mid = rest.astype(bf16)
    low = (rest - mid.astype(f32)).astype(bf16)
    return high.astype(f32), mid.astype(f32), low.astype(f32)


def rows16(upper, lower):
    return jnp.concatenate([upper, lower], axis=0).astype(bf16)


def pair_velocity(slots, target_ref, source_ref, force_ref, target, source):
    row = lax.broadcasted_iota(i32, (8, slots), 0)
    zero = jnp.zeros((8, slots), f32)
    tile = source_ref[pl.ds(pl.multiple_of(source * 8, 8), 8), :]
    high, mid, low = split3(tile)
    left = jnp.concatenate([rows16(high, mid), rows16(low, zero)], axis=0)
    base = (target // slots) * (3 * slots) + target % slots
    columns = []
    for k in range(3):
        coord = jnp.broadcast_to(target_ref[pl.ds(base + slots * k, 1), :], (8, slots))
        x_high, x_mid, x_low = split3(coord)
        minus = jnp.where(row == k, -1.0, 0.0).astype(f32)
        top = jnp.where(row == 3, x_high, jnp.where(row == 4, x_mid, jnp.where(row == 5, x_low, minus)))
        columns.append(jnp.concatenate([rows16(top, minus), rows16(minus, zero)], axis=0))
    right = jnp.concatenate(columns, axis=1)
    delta = lax.dot_general(left, right, (((0,), (0,)), ((), ())), preferred_element_type=f32)
    block = (source // slots) * (3 * slots) + source % slots
    force = [
        jnp.broadcast_to(force_ref[pl.ds(block + slots * k, 1), :], (slots, slots)).T for k in range(3)
    ]
    total = None
    for g in range(slots // 8):
        w = delta[8 * g : 8 * g + 8]
        wx, wy, wz = w[:, :slots], w[:, slots : 2 * slots], w[:, 2 * slots :]
        fx, fy, fz = [part[8 * g : 8 * g + 8] for part in force]
        inverse = lax.rsqrt(wx * wx + wy * wy + (wz * wz + 1.0))
        cube = inverse * inverse * inverse
        isotropic = inverse + cube
        project = (wx * fx + wy * fy + wz * fz) * cube
        terms = (isotropic * fx + project * wx, isotropic * fy + project * wy, isotropic * fz + project * wz)
        total = terms if total is None else tuple(a + b for a, b in zip(total, terms))
    sums = [jnp.broadcast_to(jnp.sum(part, axis=0, keepdims=True), (8, slots)) for part in total]
    return jnp.where(row == 0, sums[0], jnp.where(row == 1, sums[1], jnp.where(row == 2, sums[2], zero)))


def hop_kernel(slots, hop, blocks, homes, has_input, pairs_ref, bounds_ref, *refs):
    refs = list(refs)
    target_refs = [refs.pop(0) for _ in range(homes)]
    source_refs = [(refs.pop(0), refs.pop(0)) for _ in range(blocks)]
    before_ref = refs.pop(0) if has_input else None
    out_ref, target_ref, source_ref, force_ref, total_ref = refs
    clusters = homes * slots
    for h in range(homes):
        target_ref[3 * slots * h : 3 * slots * (h + 1), :] = target_refs[h][...]
    tiles = source_ref.reshape(blocks * slots, 8, slots)
    for b, (position, force) in enumerate(source_refs):
        for k in range(8):
            if k < 3:
                value = position[slots * k : slots * (k + 1), :]
            else:
                value = jnp.full((slots, slots), 1.0 if k < 6 else 0.0, f32)
            tiles[slots * b : slots * (b + 1), k, :] = value
        force_ref[3 * slots * b : 3 * slots * (b + 1), :] = force[...]
    total_ref[...] = jnp.zeros_like(total_ref)
    start = bounds_ref[hop]
    stop = bounds_ref[hop + 1]
    last = pairs_ref.shape[0] - 1

    def step(i, carry):
        results = []
        for u in range(unroll):
            index = start + i * unroll + u
            packed = pairs_ref[jnp.minimum(index, last)]
            live = index < stop
            target = jnp.where(live, packed & 0xFFFF, 0)
            source = jnp.where(live, packed >> 16, 0)
            result = pair_velocity(slots, target_ref, source_ref, force_ref, target, source)
            results.append((jnp.where(live, target, clusters), result))
        for target, result in results:
            total_ref[pl.ds(pl.multiple_of(target * 8, 8), 8), :] += result
        return carry

    lax.fori_loop(0, (stop - start + unroll - 1) // unroll, step, 0)
    totals = total_ref.reshape(total_ref.shape[0] // 8, 8, slots)
    for h in range(homes):
        for k in range(3):
            rows = slice(slots * (3 * h + k), slots * (3 * h + k + 1))
            value = totals[slots * h : slots * (h + 1), k, :]
            out_ref[rows, :] = value if before_ref is None else value + before_ref[rows, :]


def hop_call(hop, pairs, bounds, targets, sources, before):
    slots = targets[0].shape[1]
    homes, blocks = len(targets), len(sources)
    operands = [pairs, bounds, *targets]
    for position, force in sources:
        operands += [position, force]
    if before is not None:
        operands.append(before)
    return pl.pallas_call(
        functools.partial(hop_kernel, slots, hop, blocks, homes, before is not None),
        out_shape=jax.ShapeDtypeStruct((homes * 3 * slots, slots), f32),
        in_specs=[smem, smem] + [vmem] * (len(operands) - 2),
        out_specs=vmem,
        scratch_shapes=[
            pltpu.VMEM((homes * 3 * slots, slots), f32),
            pltpu.VMEM((blocks * slots * 8, slots), f32),
            pltpu.VMEM((blocks * 3 * slots, slots), f32),
            pltpu.VMEM((homes * slots * 8 + 8, slots), f32),
        ],
        compiler_params=pltpu.CompilerParams(vmem_limit_bytes=vmem_limit),
        cost_estimate=pl.CostEstimate(flops=10**8, bytes_accessed=4 * 10**6, transcendentals=10**6),
        name=f"pairs_hop{hop}",
    )(*operands)


def pack_kernel(slots, capacity, place_ref, *refs):
    *speed_refs, out_ref, speed_ref = refs
    total = speed_refs[0][...]
    for part in speed_refs[1:]:
        total = total + part[...]
    speed_ref[...] = total
    out_ref[...] = jnp.zeros_like(out_ref)

    def step(i, carry):
        for u in range(8):
            cluster = i * 8 + u
            place = place_ref[cluster]
            for k in range(3):
                out_ref[pl.ds(place + capacity * k, 1), :] = speed_ref[pl.ds(cluster + slots * k, 1), :]
        return carry

    lax.fori_loop(0, place_ref.shape[0] // 8, step, 0)


def pack_call(places, speeds, capacity, devices):
    slots = speeds[0].shape[1]
    return pl.pallas_call(
        functools.partial(pack_kernel, places.shape[0], capacity),
        out_shape=jax.ShapeDtypeStruct((devices * capacity * 3, slots), f32),
        in_specs=[smem] + [vmem] * len(speeds),
        out_specs=vmem,
        scratch_shapes=[pltpu.VMEM(speeds[0].shape, f32)],
        compiler_params=pltpu.CompilerParams(vmem_limit_bytes=vmem_limit),
        name="pack_owners",
    )(places, *speeds)


def unpack_kernel(capacity, place_ref, count_ref, arrived_ref, out_ref):
    slots = arrived_ref.shape[1]
    lane = lax.broadcasted_iota(i32, (1, slots), 1)

    def step(i, carry):
        for u in range(8):
            cluster = i * 8 + u
            place = place_ref[cluster]
            live = lane < count_ref[cluster]
            for k in range(3):
                value = arrived_ref[pl.ds(place + capacity * k, 1), :]
                out_ref[cluster, k : k + 1, :] = jnp.where(live, value, 0.0)
        return carry

    lax.fori_loop(0, place_ref.shape[0] // 8, step, 0)


def unpack_call(places, counts, arrived, capacity):
    slots = arrived.shape[1]
    return pl.pallas_call(
        functools.partial(unpack_kernel, capacity),
        out_shape=jax.ShapeDtypeStruct((places.shape[0], 3, slots), f32),
        in_specs=[smem, smem, vmem],
        out_specs=vmem,
        compiler_params=pltpu.CompilerParams(vmem_limit_bytes=vmem_limit),
        name="unpack_drops",
    )(places, counts, arrived)


def per_device(
    positions,
    normals,
    curvature,
    pair_targets,
    pair_sources,
    pair_count,
    node_counts,
    drop_clusters,
    drop_owner,
):
    local_count = positions.shape[0]
    slots = positions.shape[2]
    rows = lax.axis_size("row")
    cols = lax.axis_size("col")
    devices = rows * cols
    my_row = lax.axis_index("row")
    my_col = lax.axis_index("col")
    device = my_row * cols + my_col
    capacity = max(2, 2 * local_count // devices)
    per_drop = drop_clusters.shape[1]
    drops = drop_clusters.shape[0]
    drops_here = local_count // per_drop
    hypercube = cols == 4

    def swap(value, bit):
        return lax.ppermute(value, "col", [(c, c ^ bit) for c in range(cols)])

    position = (jnp.transpose(positions, (1, 0, 2)) * length_scale).reshape(3 * local_count, slots)

    to_right = [(r, r + 1) for r in range(rows - 1)]
    to_left = [(r + 1, r) for r in range(rows - 1)]
    right_position = lax.ppermute(position, "row", to_right)
    left_position = lax.ppermute(position, "row", to_left)

    if hypercube:
        core_mate = swap(position, 1)
        chip_mate = swap(position, 2)
        targets = [position, core_mate, chip_mate, swap(chip_mate, 1)]
    else:
        gathered = lax.all_gather(position, "col", axis=0, tiled=True)
        targets = [gathered[3 * local_count * h : 3 * local_count * (h + 1)] for h in range(cols)]

    flat_clusters = drop_clusters.reshape(-1)
    flat_facts = (node_counts + (drop_owner[:, None] << 16)).reshape(-1)
    mine = device * local_count + jnp.arange(local_count, dtype=i32)
    home_facts = jnp.sum(
        jnp.where(flat_clusters[:, None] == mine[None, :], flat_facts[:, None], 0), axis=0
    )
    home_counts = home_facts & 0xFFFF
    home_owner = home_facts >> 16
    slot_index = jnp.arange(slots, dtype=i32)
    strength = jnp.where(slot_index[None, :] < home_counts[:, None], curvature * force_scale, 0.0)
    force = (jnp.transpose(normals, (1, 0, 2)) * strength[None]).reshape(3 * local_count, slots)

    right_force = lax.ppermute(force, "row", to_right)
    left_force = lax.ppermute(force, "row", to_left)

    pair_slots = pair_targets.shape[1]
    entry = jnp.arange(pair_slots, dtype=i32)
    source_row = pair_sources[0] // local_count
    distance = jnp.abs(source_row - my_row)
    key = jnp.where(entry < pair_count[0], distance, rows)
    home = pair_targets[0] // local_count
    home = home ^ my_col if hypercube else home
    target = home * local_count + pair_targets[0] % local_count
    side = jnp.where(source_row > my_row, local_count, 0)
    packed = target | ((side + pair_sources[0] % local_count) << 16)
    ahead = (key[None, :] < key[:, None]) | ((key[None, :] == key[:, None]) & (entry[None, :] < entry[:, None]))
    place = jnp.sum(ahead.astype(i32), axis=1)
    pairs = jnp.sum(jnp.where(place[:, None] == entry[None, :], packed[:, None], 0), axis=0)
    bounds = jnp.sum((key[None, :] < jnp.arange(rows + 1, dtype=i32)[:, None]).astype(i32), axis=1)

    speed = hop_call(0, pairs, bounds, targets, [(position, force)], None)
    for hop in range(1, rows):
        if hop + 1 < rows:
            next_position = (
                lax.ppermute(right_position, "row", to_right),
                lax.ppermute(left_position, "row", to_left),
            )
            next_force = (
                lax.ppermute(right_force, "row", to_right),
                lax.ppermute(left_force, "row", to_left),
            )
        speed = hop_call(
            hop, pairs, bounds, targets, [(right_position, right_force), (left_position, left_force)], speed
        )
        if hop + 1 < rows:
            right_position, left_position = next_position
            right_force, left_force = next_force

    block = 3 * local_count
    if hypercube:
        parts = [speed[block * h : block * (h + 1)] for h in range(4)]
        from_mate = swap(jnp.concatenate([parts[1], parts[3]], axis=0), 1)
        across = swap(parts[2] + from_mate[block:], 2)
        home_speed = [parts[0], from_mate[:block], across]
    else:
        home_speed = [lax.psum_scatter(speed, "col", scatter_dimension=0, tiled=True)]

    local = jnp.arange(local_count, dtype=i32)
    earlier = (home_owner[None, :] == home_owner[:, None]) & (local[None, :] < local[:, None])
    send_rank = jnp.sum(earlier.astype(i32), axis=1)
    outgoing = pack_call(home_owner * (3 * capacity) + send_rank, home_speed, capacity, devices)
    arrived = lax.all_to_all(outgoing, ("row", "col"), split_axis=0, concat_axis=0, tiled=True)

    owned = drop_owner == device
    drop_index = jnp.arange(drops, dtype=i32)
    order = jnp.sum((owned[None, :] & (drop_index[None, :] < drop_index[:, None])).astype(i32), axis=1)
    chosen = owned[None, :] & (order[None, :] == jnp.arange(drops_here, dtype=i32)[:, None])
    drop_facts = drop_clusters | (node_counts << 16)
    owned_facts = jnp.sum(jnp.where(chosen[:, :, None], drop_facts[None], 0), axis=1).reshape(-1)
    owned_clusters = owned_facts & 0xFFFF
    owned_counts = owned_facts >> 16
    anchor = owned_clusters // local_count
    before = (anchor[None, :] == anchor[:, None]) & (owned_clusters[None, :] < owned_clusters[:, None])
    arrive_rank = jnp.sum(before.astype(i32), axis=1)
    return unpack_call(anchor * (3 * capacity) + arrive_rank, owned_counts, arrived, capacity)


def solution(mesh):
    in_specs = (
        P(("groups", "row", "col"), None, None),
        P(("groups", "row", "col"), None, None),
        P(("groups", "row", "col"), None),
        P(("groups", "row", "col"), None),
        P(("groups", "row", "col"), None),
        P(("groups", "row", "col")),
        P("groups", None),
        P("groups", None),
        P("groups"),
    )
    out_specs = P(("groups", "row", "col"), None, None)
    return jax.shard_map(
        per_device, mesh=mesh, in_specs=in_specs, out_specs=out_specs, check_vma=False
    )
```

```python
import functools
import math

import jax
import jax.numpy as jnp
from jax import lax
from jax.experimental import pallas as pl
from jax.experimental.pallas import tpu as pltpu
from jax.sharding import PartitionSpec as P

f32 = jnp.float32
bf16 = jnp.bfloat16
i32 = jnp.int32
regular_sq = 0.0025
length_scale = 1.0 / math.sqrt(regular_sq)
force_scale = length_scale / (8.0 * math.pi)
unroll = 8
vmem_limit = 24 * 2**20
kernel_flops = 2 * 10**10
vmem = pl.BlockSpec(memory_space=pltpu.VMEM)
smem = pl.BlockSpec(memory_space=pltpu.SMEM)


def split3(value):
    high = value.astype(bf16)
    rest = value - high.astype(f32)
    mid = rest.astype(bf16)
    low = (rest - mid.astype(f32)).astype(bf16)
    return high.astype(f32), mid.astype(f32), low.astype(f32)


def rows16(upper, lower):
    return jnp.concatenate([upper, lower], axis=0).astype(bf16)


def transposed_left(y, f, slots):
    row = lax.broadcasted_iota(i32, (8, slots), 0)
    dot = -(y[0] * f[0] + y[1] * f[1] + y[2] * f[2])
    tile = jnp.where(row == 7, dot, 0.0)
    for k in range(3):
        tile = jnp.where(row == k, y[k], jnp.where(row == 3 + k, f[k], tile))
    high, mid, low = split3(tile)
    first = row < 3
    high_one = jnp.where(first, 1.0, high)
    left = jnp.concatenate(
        [rows16(high, mid), rows16(low, high_one), rows16(high_one, jnp.where(first, 1.0, mid))], axis=0
    )
    return left.T


def products(left, x, slots):
    row = lax.broadcasted_iota(i32, (8, slots), 0)
    zero = jnp.zeros((8, slots), f32)
    tile = jnp.where(row == 7, 1.0, zero)
    for k in range(3):
        tile = jnp.where((row == k) | (row == 3 + k), x[k], tile)
    high, mid, low = split3(tile)
    columns = []
    for k in range(3):
        mine = row == k
        minus = jnp.where(mine, -1.0, zero)
        columns.append(
            [
                rows16(minus, minus),
                rows16(minus, jnp.where(mine, high, 0.0)),
                rows16(jnp.where(mine, mid, 0.0), jnp.where(mine, low, 0.0)),
            ]
        )
    first = row < 3
    high, mid, low = [jnp.where(first, 0.0, part) for part in (high, mid, low)]
    columns.append([rows16(high, high), rows16(high, mid), rows16(low, mid)])
    for k in range(2):
        pick = jnp.where(row == 3 + k, 1.0, zero)
        columns.append([rows16(pick, pick), rows16(pick, zero), rows16(zero, zero)])
    right = jnp.concatenate([jnp.concatenate(column, axis=0) for column in columns], axis=1)
    return lax.dot_general(left, right, (((1,), (0,)), ((), ())), preferred_element_type=f32)


def node_sums(product, force_z, slots):
    row = lax.broadcasted_iota(i32, (8, slots), 0)
    total = None
    for g in range(slots // 8):
        part = product[8 * g : 8 * g + 8]
        wx, wy, wz, dot, fx, fy = [part[:, slots * k : slots * (k + 1)] for k in range(6)]
        fz = force_z[8 * g : 8 * g + 8]
        inverse = lax.rsqrt(wx * wx + wy * wy + (wz * wz + 1.0))
        cube = inverse * inverse * inverse
        isotropic = inverse + cube
        project = dot * cube
        terms = (isotropic * fx + project * wx, isotropic * fy + project * wy, isotropic * fz + project * wz)
        total = terms if total is None else tuple(a + b for a, b in zip(total, terms))
    sums = [jnp.broadcast_to(jnp.sum(part, axis=0, keepdims=True), (8, slots)) for part in total]
    return jnp.where(row == 0, sums[0], jnp.where(row == 1, sums[1], jnp.where(row == 2, sums[2], 0.0)))


def hop_kernel(spec, pairs_ref, *refs):
    n, slots, hop, hops, homes, own, mate, first, last, split = spec
    refs = list(refs)
    if first:
        target_refs = [refs.pop(0) for _ in range(homes)]
    else:
        target_ref, before_ref = refs.pop(0), refs.pop(0)
    own_refs = [refs.pop(0) for _ in range(own)]
    mate_refs = [refs.pop(0) for _ in range(mate)]
    if first:
        total_ref, target_ref = refs.pop(0), refs.pop(0)
    else:
        total_ref = refs.pop(0)
        out_refs = [refs.pop(0) for _ in range((2 if split else 1) if last else 0)]
    source_ref, left_ref = refs
    clusters = homes * n
    shift = n.bit_length() - 1
    if first:
        for h in range(homes):
            target_ref[3 * n * h : 3 * n * (h + 1), :] = target_refs[h][: 3 * n, :]
        total_ref[...] = jnp.zeros_like(total_ref)
    for place, block in list(enumerate(own_refs)) + [(2 + b, block) for b, block in enumerate(mate_refs)]:
        source_ref[6 * n * place : 6 * n * (place + 1), :] = block[...]

    width = pairs_ref.shape[0] // 2
    slots_of = width - 128
    own_start, own_count, mate_start, mate_count = 0, 0, 0, 0
    if own:
        own_start = pairs_ref[slots_of + hop]
        own_count = (pairs_ref[slots_of + hop + 1] - own_start + 1) >> 1
    if mate:
        begin = pairs_ref[width + slots_of + hop - 1]
        end = pairs_ref[width + slots_of + hop]
        mate_start = width + begin + ((end - begin + 1) >> 1)
        mate_count = width + end - mate_start
    count = own_count + mate_count
    mate_start = mate_start - own_count

    def entry(index):
        live = index < count
        index = jnp.where(live, index, 0)
        place = index + jnp.where(index < own_count, own_start, mate_start)
        packed = pairs_ref[jnp.where(live, place, 0)]
        target = jnp.where(live, packed & 0xFFFF, 0)
        source = jnp.where(live, packed >> 16, 0)
        return live, target, source

    def source_rows(source):
        base = source + (source >> shift) * (5 * n)
        return [source_ref[pl.ds(base + n * k, 1), :] for k in range(6)]

    def wide(value):
        return jnp.broadcast_to(value, (8, slots))

    def fetch(index, u):
        _, _, source = entry(index)
        values = [wide(value) for value in source_rows(source)]
        left_ref[u] = transposed_left(values[:3], values[3:], slots)

    @pl.when(count > 0)
    def _():
        for u in range(unroll):
            fetch(u, u)

    def step(i, carry):
        results = []
        lefts = [left_ref[u] for u in range(unroll)]
        for u in range(unroll):
            live, target, source = entry(i * unroll + u)
            base = target + (target >> shift) * (2 * n)
            x = [wide(target_ref[pl.ds(base + n * k, 1), :]) for k in range(3)]
            product = products(lefts[u], x, slots)
            force_z = source_ref[pl.ds(source + (source >> shift) * (5 * n) + 5 * n, 1), :]
            force_z = jnp.broadcast_to(force_z, (slots, slots)).T
            results.append((jnp.where(live, target, clusters), node_sums(product, force_z, slots)))
        for u in range(unroll):
            fetch((i + 1) * unroll + u, u)
        for target, result in results:
            total_ref[pl.ds(pl.multiple_of(target * 8, 8), 8), :] += result
        return carry

    lax.fori_loop(0, (count + unroll - 1) // unroll, step, 0)
    if last:
        totals = total_ref.reshape(total_ref.shape[0] // 8, 8, slots)
        for h in range(homes):
            out_ref = out_refs[h % 2] if split else out_refs[0]
            place = h // 2 if split else h
            for k in range(3):
                rows = slice(n * (3 * place + k), n * (3 * place + k + 1))
                out_ref[rows, :] = totals[n * h : n * (h + 1), k, :]


def hop_call(n, hop, hops, pairs, targets, total, own, mate, split):
    first, last = hop == 0, hop == hops
    slots = own[0].shape[1] if own else mate[0].shape[1]
    homes = len(targets) if first else targets[0].shape[0] // (3 * n)
    total_shape = jax.ShapeDtypeStruct((homes * n * 8 + 8, slots), f32)
    aliases = {}
    operands = [pairs, *targets]
    if not first:
        operands.append(total)
    if first:
        out_shape = [total_shape, jax.ShapeDtypeStruct((homes * 3 * n, slots), f32)]
    elif last:
        parts = 2 if split else 1
        out_shape = [total_shape] + [jax.ShapeDtypeStruct((homes * 3 * n // parts, slots), f32)] * parts
    else:
        out_shape = [total_shape]
    if not first:
        aliases = {len(operands) - 1: 0}
    operands += [*own, *mate]
    spec = (n, slots, hop, hops, homes, len(own), len(mate), first, last, split)
    return pl.pallas_call(
        functools.partial(hop_kernel, spec),
        out_shape=out_shape,
        in_specs=[smem] + [vmem] * (len(operands) - 1),
        out_specs=[vmem] * len(out_shape),
        scratch_shapes=[
            pltpu.VMEM((4 * 6 * n, slots), f32),
            pltpu.VMEM((unroll, slots, 48), bf16),
        ],
        input_output_aliases=aliases,
        compiler_params=pltpu.CompilerParams(vmem_limit_bytes=vmem_limit),
        cost_estimate=pl.CostEstimate(flops=kernel_flops, bytes_accessed=10**6, transcendentals=10**6),
        name=f"pairs_hop{hop}",
    )(*operands)


def prep_kernel(n, base_ref, position_ref, normal_ref, curvature_ref, cluster_ref, count_ref, out_ref, own_ref):
    slots = position_ref.shape[1]
    scaled = position_ref[...] * length_scale
    out_ref[: 3 * n, :] = scaled
    own_ref[...] = scaled
    mine = base_ref[0] + lax.broadcasted_iota(i32, (n, 128), 0)
    total = jnp.zeros((n, 128), f32)
    for k in range(cluster_ref.shape[0]):
        for j in range(cluster_ref.shape[1] // 128):
            part = slice(128 * j, 128 * (j + 1))
            cluster = jnp.broadcast_to(cluster_ref[k : k + 1, part], (n, 128))
            count = jnp.broadcast_to(count_ref[k : k + 1, part].astype(f32), (n, 128))
            total = total + jnp.where(cluster == mine, count, 0.0)
    live_count = jnp.sum(total, axis=1, keepdims=True)
    lane = lax.broadcasted_iota(i32, (n, slots), 1).astype(f32)
    strength = jnp.where(lane < live_count, curvature_ref[...] * force_scale, 0.0)
    for k in range(3):
        out_ref[n * (3 + k) : n * (4 + k), :] = normal_ref[n * k : n * (k + 1), :] * strength


def prep_call(base, position, normal, curvature, clusters, counts):
    n, slots = curvature.shape
    return pl.pallas_call(
        functools.partial(prep_kernel, n),
        out_shape=[jax.ShapeDtypeStruct((6 * n, slots), f32), jax.ShapeDtypeStruct((3 * n, slots), f32)],
        in_specs=[smem] + [vmem] * 5,
        out_specs=[vmem, vmem],
        compiler_params=pltpu.CompilerParams(vmem_limit_bytes=vmem_limit),
        name="prep_sources",
    )(base, position, normal, curvature, clusters, counts)


def pack_kernel(n, capacity, place_ref, *refs):
    *speed_refs, out_ref, speed_ref = refs
    total = speed_refs[0][: 3 * n, :]
    for part in speed_refs[1:]:
        total = total + part[: 3 * n, :]
    speed_ref[...] = total
    out_ref[...] = jnp.zeros_like(out_ref)

    def step(i, carry):
        for u in range(16):
            cluster = i * 16 + u
            place = place_ref[cluster]
            for k in range(3):
                out_ref[pl.ds(place + capacity * k, 1), :] = speed_ref[pl.ds(cluster + n * k, 1), :]
        return carry

    lax.fori_loop(0, n // 16, step, 0)


def pack_call(places, speeds, capacity, devices):
    n = places.shape[0]
    slots = speeds[0].shape[1]
    return pl.pallas_call(
        functools.partial(pack_kernel, n, capacity),
        out_shape=jax.ShapeDtypeStruct((devices * capacity * 3, slots), f32),
        in_specs=[smem] + [vmem] * len(speeds),
        out_specs=vmem,
        scratch_shapes=[pltpu.VMEM((3 * n, slots), f32)],
        compiler_params=pltpu.CompilerParams(vmem_limit_bytes=vmem_limit),
        name="pack_owners",
    )(places, *speeds)


def unpack_kernel(n, capacity, place_ref, count_ref, arrived_ref, out_ref):
    slots = arrived_ref.shape[1]
    lane = lax.broadcasted_iota(i32, (1, slots), 1)

    def step(i, carry):
        for u in range(16):
            cluster = i * 16 + u
            place = place_ref[cluster]
            live = lane < count_ref[cluster]
            for k in range(3):
                value = arrived_ref[pl.ds(place + capacity * k, 1), :]
                out_ref[pl.ds(cluster + n * k, 1), :] = jnp.where(live, value, 0.0)
        return carry

    lax.fori_loop(0, n // 16, step, 0)


def unpack_call(places, counts, arrived, capacity):
    n, slots = places.shape[0], arrived.shape[1]
    return pl.pallas_call(
        functools.partial(unpack_kernel, n, capacity),
        out_shape=jax.ShapeDtypeStruct((3 * n, slots), f32),
        in_specs=[smem, smem, vmem],
        out_specs=vmem,
        compiler_params=pltpu.CompilerParams(vmem_limit_bytes=vmem_limit),
        name="unpack_drops",
    )(places, counts, arrived)


def per_device(
    positions,
    normals,
    curvature,
    pair_targets,
    pair_sources,
    pair_count,
    node_counts,
    drop_clusters,
    drop_owner,
):
    n, slots = curvature.shape
    rows = lax.axis_size("row")
    cols = lax.axis_size("col")
    devices = rows * cols
    my_row = lax.axis_index("row")
    my_col = lax.axis_index("col")
    device = my_row * cols + my_col
    capacity = max(2, 2 * n // devices)
    drops, per_drop = drop_clusters.shape
    drops_here = n // per_drop
    hypercube = cols == 4

    def swap(value, bit):
        return lax.ppermute(value, "col", [(c, c ^ bit) for c in range(cols)])

    def component_major(value):
        return jnp.transpose(value, (1, 0, 2)).reshape(3 * n, slots)

    block, position = prep_call(
        (device * n).reshape(1),
        component_major(positions),
        component_major(normals),
        curvature,
        drop_clusters.T,
        node_counts.T,
    )
    to_right = [(r, r + 1) for r in range(rows - 1)]
    to_left = [(r + 1, r) for r in range(rows - 1)]
    right = lax.ppermute(block, "row", to_right)
    left = lax.ppermute(block, "row", to_left)
    mate_block = swap(block, 1)
    if hypercube:
        across = swap(position, 2)
        targets = [position, mate_block, across, swap(across, 1)]
    else:
        gathered = lax.all_gather(position, "col", axis=0, tiled=True)
        targets = [gathered[3 * n * h : 3 * n * (h + 1)] for h in range(cols)]

    pair_slots = pair_targets.shape[1]
    entry = jnp.arange(pair_slots, dtype=i32)
    source_row = pair_sources[0] // n
    key = jnp.where(entry < pair_count[0], jnp.abs(source_row - my_row), rows)
    home = pair_targets[0] // n
    home = home ^ my_col if hypercube else home
    target = home * n + pair_targets[0] % n
    packed = target | ((jnp.where(source_row > my_row, n, 0) + pair_sources[0] % n) << 16)
    ahead = (key[None, :] < key[:, None]) | ((key[None, :] == key[:, None]) & (entry[None, :] < entry[:, None]))
    place = jnp.sum(ahead.astype(i32), axis=1)
    ordered = jnp.sum(jnp.where(place[:, None] == entry[None, :], packed[:, None], 0), axis=0)
    bounds = jnp.sum((key[None, :] < jnp.arange(128, dtype=i32)[:, None]).astype(i32), axis=1)
    listed = jnp.concatenate([ordered, bounds])
    mate_listed = swap(listed, 1)
    flip = n if hypercube else 0
    mate_pairs = jnp.where(
        jnp.arange(pair_slots + 128) < pair_slots, (mate_listed ^ flip) + ((2 * n) << 16), mate_listed
    )
    pairs = jnp.concatenate([listed, mate_pairs])

    total, all_targets = hop_call(n, 0, rows, pairs, targets, None, [block], [], hypercube)
    mate = [mate_block]
    for hop in range(1, rows):
        right, left, total = lax.optimization_barrier((right, left, total))
        own = [right, left]
        if hop + 1 < rows:
            right = lax.ppermute(right, "row", to_right)
            left = lax.ppermute(left, "row", to_left)
        next_mate = [swap(own[0], 1), swap(own[1], 1)]
        (total,) = hop_call(n, hop, rows, pairs, [all_targets], total, own, mate, hypercube)
        mate = next_mate
    _, *speed = hop_call(n, rows, rows, pairs, [all_targets], total, [], mate, hypercube)

    if hypercube:
        kept, sent = speed
        from_mate = swap(sent, 1)
        across = swap(kept[3 * n :] + from_mate[3 * n :], 2)
        home_speed = [kept, from_mate, across]
    else:
        home_speed = [lax.psum_scatter(speed[0], "col", scatter_dimension=0, tiled=True)]

    flat_clusters = drop_clusters.reshape(-1)
    flat_owner = jnp.broadcast_to(drop_owner[:, None], drop_clusters.shape).reshape(-1)
    local = jnp.arange(n, dtype=i32)
    home_owner = jnp.sum(
        jnp.where(flat_clusters[:, None] == (device * n + local)[None, :], flat_owner[:, None], 0), axis=0
    )
    earlier = (home_owner[None, :] == home_owner[:, None]) & (local[None, :] < local[:, None])
    send_rank = jnp.sum(earlier.astype(i32), axis=1)
    outgoing = pack_call(home_owner * (3 * capacity) + send_rank, home_speed, capacity, devices)
    arrived = lax.all_to_all(outgoing, ("row", "col"), split_axis=0, concat_axis=0, tiled=True)

    owned = drop_owner == device
    drop_index = jnp.arange(drops, dtype=i32)
    order = jnp.sum((owned[None, :] & (drop_index[None, :] < drop_index[:, None])).astype(i32), axis=1)
    chosen = owned[None, :] & (order[None, :] == jnp.arange(drops_here, dtype=i32)[:, None])
    drop_facts = drop_clusters | (node_counts << 16)
    owned_facts = jnp.sum(jnp.where(chosen[:, :, None], drop_facts[None], 0), axis=1).reshape(-1)
    owned_clusters = owned_facts & 0xFFFF
    owned_counts = owned_facts >> 16
    anchor = owned_clusters // n
    before = (anchor[None, :] == anchor[:, None]) & (owned_clusters[None, :] < owned_clusters[:, None])
    arrive_rank = jnp.sum(before.astype(i32), axis=1)
    result = unpack_call(anchor * (3 * capacity) + arrive_rank, owned_counts, arrived, capacity)
    return jnp.transpose(result.reshape(3, n, slots), (1, 0, 2))


def solution(mesh):
    in_specs = (
        P(("groups", "row", "col"), None, None),
        P(("groups", "row", "col"), None, None),
        P(("groups", "row", "col"), None),
        P(("groups", "row", "col"), None),
        P(("groups", "row", "col"), None),
        P(("groups", "row", "col")),
        P("groups", None),
        P("groups", None),
        P("groups"),
    )
    out_specs = P(("groups", "row", "col"), None, None)
    return jax.shard_map(
        per_device, mesh=mesh, in_specs=in_specs, out_specs=out_specs, check_vma=False
    )
```

```python
import functools
import math

import jax
import jax.numpy as jnp
from jax import lax
from jax.experimental import pallas as pl
from jax.experimental.pallas import tpu as pltpu
from jax.sharding import PartitionSpec as P

f32 = jnp.float32
bf16 = jnp.bfloat16
i32 = jnp.int32
regular_sq = 0.0025
length_scale = 1.0 / math.sqrt(regular_sq)
force_scale = length_scale / (8.0 * math.pi)
unroll = 8
vmem_limit = 24 * 2**20
kernel_flops = 2 * 10**10
vmem = pl.BlockSpec(memory_space=pltpu.VMEM)
smem = pl.BlockSpec(memory_space=pltpu.SMEM)
hbm = pl.BlockSpec(memory_space=pltpu.HBM)


def split3(value):
    high = value.astype(bf16)
    rest = value - high.astype(f32)
    mid = rest.astype(bf16)
    low = (rest - mid.astype(f32)).astype(bf16)
    return high.astype(f32), mid.astype(f32), low.astype(f32)


def rows16(upper, lower):
    return jnp.concatenate([upper, lower], axis=0).astype(bf16)


def transposed_left(y, f, slots):
    row = lax.broadcasted_iota(i32, (8, slots), 0)
    dot = -(y[0] * f[0] + y[1] * f[1] + y[2] * f[2])
    tile = jnp.where(row == 7, dot, 0.0)
    for k in range(3):
        tile = jnp.where(row == k, y[k], jnp.where(row == 3 + k, f[k], tile))
    high, mid, low = split3(tile)
    first = row < 3
    high_one = jnp.where(first, 1.0, high)
    left = jnp.concatenate(
        [rows16(high, mid), rows16(low, high_one), rows16(high_one, jnp.where(first, 1.0, mid))], axis=0
    )
    return left.T


def products(left, x, slots):
    row = lax.broadcasted_iota(i32, (8, slots), 0)
    zero = jnp.zeros((8, slots), f32)
    tile = jnp.where(row == 7, 1.0, zero)
    for k in range(3):
        tile = jnp.where((row == k) | (row == 3 + k), x[k], tile)
    high, mid, low = split3(tile)
    columns = []
    for k in range(3):
        mine = row == k
        minus = jnp.where(mine, -1.0, zero)
        columns.append(
            [
                rows16(minus, minus),
                rows16(minus, jnp.where(mine, high, 0.0)),
                rows16(jnp.where(mine, mid, 0.0), jnp.where(mine, low, 0.0)),
            ]
        )
    first = row < 3
    high, mid, low = [jnp.where(first, 0.0, part) for part in (high, mid, low)]
    columns.append([rows16(high, high), rows16(high, mid), rows16(low, mid)])
    for k in range(2):
        pick = jnp.where(row == 3 + k, 1.0, zero)
        columns.append([rows16(pick, pick), rows16(pick, zero), rows16(zero, zero)])
    right = jnp.concatenate([jnp.concatenate(column, axis=0) for column in columns], axis=1)
    return lax.dot_general(left, right, (((1,), (0,)), ((), ())), preferred_element_type=f32)


def node_sums(product, force_z, slots):
    row = lax.broadcasted_iota(i32, (8, slots), 0)
    total = None
    for g in range(slots // 8):
        part = product[8 * g : 8 * g + 8]
        wx, wy, wz, dot, fx, fy = [part[:, slots * k : slots * (k + 1)] for k in range(6)]
        fz = force_z[8 * g : 8 * g + 8]
        inverse = lax.rsqrt(wx * wx + wy * wy + (wz * wz + 1.0))
        cube = inverse * inverse * inverse
        isotropic = inverse + cube
        project = dot * cube
        terms = (isotropic * fx + project * wx, isotropic * fy + project * wy, isotropic * fz + project * wz)
        total = terms if total is None else tuple(a + b for a, b in zip(total, terms))
    sums = [jnp.broadcast_to(jnp.sum(part, axis=0, keepdims=True), (8, slots)) for part in total]
    return jnp.where(row == 0, sums[0], jnp.where(row == 1, sums[1], jnp.where(row == 2, sums[2], 0.0)))


def hop_kernel(spec, list_ref, mate_list_ref, *refs):
    n, slots, hop, homes, own, mate, first, last, split = spec
    refs = list(refs)
    if first:
        target_refs = [refs.pop(0) for _ in range(homes)]
    else:
        target_ref, before_ref = refs.pop(0), refs.pop(0)
    own_refs = [refs.pop(0) for _ in range(own)]
    mate_refs = [refs.pop(0) for _ in range(mate)]
    if first:
        total_ref, target_ref = refs.pop(0), refs.pop(0)
    else:
        total_ref = refs.pop(0)
        out_refs = [refs.pop(0) for _ in range((2 if split else 1) if last else 0)]
    source_ref, left_ref = refs
    clusters = homes * n
    shift = n.bit_length() - 1
    if first:
        for h in range(homes):
            target_ref[3 * n * h : 3 * n * (h + 1), :] = target_refs[h][: 3 * n, :]
        total_ref[...] = jnp.zeros_like(total_ref)
    for place, block in list(enumerate(own_refs)) + [(2 + b, block) for b, block in enumerate(mate_refs)]:
        source_ref[6 * n * place : 6 * n * (place + 1), :] = block[...]

    bound_row = list_ref.shape[0] - 1
    own_start, own_count, mate_start, mate_count = 0, 0, 0, 0
    if own:
        own_start = list_ref[bound_row, hop]
        own_count = (list_ref[bound_row, hop + 1] - own_start + 1) >> 1
    if mate:
        begin = mate_list_ref[bound_row, hop - 1]
        end = mate_list_ref[bound_row, hop]
        mate_start = begin + ((end - begin + 1) >> 1)
        mate_count = end - mate_start
    count = own_count + mate_count
    mate_start = mate_start - own_count

    def entry(index):
        live = index < count
        mine = index < own_count
        place = jnp.where(live, index + jnp.where(mine, own_start, mate_start), 0)
        row, lane = place >> 7, place & 127
        target, source = 0, 0
        if own:
            packed = list_ref[row, lane]
            target, source = packed & 0xFFF, packed >> 12
        if mate:
            packed = mate_list_ref[row, lane]
            flip = n if split else 0
            mate_target, mate_source = (packed & 0xFFF) ^ flip, (packed >> 12) + 2 * n
            target = jnp.where(mine, target, mate_target)
            source = jnp.where(mine, source, mate_source)
        return live, jnp.where(live, target, 0), jnp.where(live, source, 0)

    def source_rows(source):
        base = source + (source >> shift) * (5 * n)
        return [source_ref[pl.ds(base + n * k, 1), :] for k in range(6)]

    def wide(value):
        return jnp.broadcast_to(value, (8, slots))

    def fetch(index, u):
        _, _, source = entry(index)
        values = [wide(value) for value in source_rows(source)]
        left_ref[u] = transposed_left(values[:3], values[3:], slots)

    @pl.when(count > 0)
    def _():
        for u in range(unroll):
            fetch(u, u)

    def step(i, carry):
        results = []
        lefts = [left_ref[u] for u in range(unroll)]
        for u in range(unroll):
            live, target, source = entry(i * unroll + u)
            base = target + (target >> shift) * (2 * n)
            x = [wide(target_ref[pl.ds(base + n * k, 1), :]) for k in range(3)]
            product = products(lefts[u], x, slots)
            force_z = source_ref[pl.ds(source + (source >> shift) * (5 * n) + 5 * n, 1), :]
            force_z = jnp.broadcast_to(force_z, (slots, slots)).T
            results.append((jnp.where(live, target, clusters), node_sums(product, force_z, slots)))
        for u in range(unroll):
            fetch((i + 1) * unroll + u, u)
        for target, result in results:
            total_ref[pl.ds(pl.multiple_of(target * 8, 8), 8), :] += result
        return carry

    lax.fori_loop(0, (count + unroll - 1) // unroll, step, 0)
    if last:
        for h in range(homes):
            out_ref = out_refs[h % 2] if split else out_refs[0]
            first_row = 3 * n * (h // 2 if split else h)

            def move(i, carry, h=h, out_ref=out_ref, first_row=first_row):
                for u in range(8):
                    tile = total_ref[pl.ds(pl.multiple_of((n * h + i * 8 + u) * 8, 8), 8), :]
                    out_ref[pl.ds(first_row + i * 24 + 3 * u, 3), :] = tile[:3]
                return carry

            lax.fori_loop(0, n // 8, move, 0)


def hop_call(n, hop, hops, lists, targets, total, own, mate, split):
    first, last = hop == 0, hop == hops
    slots = own[0].shape[1] if own else mate[0].shape[1]
    homes = len(targets) if first else targets[0].shape[0] // (3 * n)
    total_shape = jax.ShapeDtypeStruct((homes * n * 8 + 8, slots), f32)
    aliases = {}
    operands = [*lists, *targets]
    if not first:
        operands.append(total)
    if first:
        out_shape = [total_shape, jax.ShapeDtypeStruct((homes * 3 * n, slots), f32)]
    elif last:
        parts = 2 if split else 1
        out_shape = [total_shape] + [jax.ShapeDtypeStruct((homes * 3 * n // parts, slots), f32)] * parts
    else:
        out_shape = [total_shape]
    if not first:
        aliases = {len(operands) - 1: 0}
    operands += [*own, *mate]
    spec = (n, slots, hop, homes, len(own), len(mate), first, last, split)
    return pl.pallas_call(
        functools.partial(hop_kernel, spec),
        out_shape=out_shape,
        in_specs=[smem, smem] + [vmem] * (len(operands) - 2),
        out_specs=[vmem] * len(out_shape),
        scratch_shapes=[
            pltpu.VMEM((4 * 6 * n, slots), f32),
            pltpu.VMEM((unroll, slots, 48), bf16),
        ],
        input_output_aliases=aliases,
        compiler_params=pltpu.CompilerParams(vmem_limit_bytes=vmem_limit),
        cost_estimate=pl.CostEstimate(flops=kernel_flops, bytes_accessed=10**6, transcendentals=10**6),
        name=f"pairs_hop{hop}",
    )(*operands)


def fetch_all(pairs, sems):
    copies = [pltpu.make_async_copy(a, b, sems.at[k]) for k, (a, b) in enumerate(pairs)]
    for copy in copies:
        copy.start()
    for copy in copies:
        copy.wait()


def column(row, rows):
    return jnp.broadcast_to(row, (rows, 128)).T


def prep_kernel(n, base_ref, *refs):
    ins, (out_ref, own_ref), held, sems = refs[:5], refs[5:7], refs[7:12], refs[12]
    fetch_all(list(zip(ins, held)), sems)
    position_ref, normal_ref, curvature_ref, cluster_ref, count_ref = held
    slots = position_ref.shape[1]
    scaled = position_ref[...] * length_scale
    out_ref[: 3 * n, :] = scaled
    own_ref[...] = scaled
    mine = base_ref[0] + lax.broadcasted_iota(i32, (n, 128), 0)
    total = jnp.zeros((n, 128), f32)
    for k in range(cluster_ref.shape[0]):
        for j in range(cluster_ref.shape[1] // 128):
            part = slice(128 * j, 128 * (j + 1))
            cluster = jnp.broadcast_to(cluster_ref[k : k + 1, part], (n, 128))
            count = jnp.broadcast_to(count_ref[k : k + 1, part].astype(f32), (n, 128))
            total = total + jnp.where(cluster == mine, count, 0.0)
    live_count = jnp.sum(total, axis=1, keepdims=True)
    lane = lax.broadcasted_iota(i32, (n, slots), 1).astype(f32)
    strength = jnp.where(lane < live_count, curvature_ref[...] * force_scale, 0.0)
    for k in range(3):
        out_ref[n * (3 + k) : n * (4 + k), :] = normal_ref[n * k : n * (k + 1), :] * strength


def prep_call(base, *operands):
    n, slots = operands[2].shape
    return pl.pallas_call(
        functools.partial(prep_kernel, n),
        out_shape=[jax.ShapeDtypeStruct((6 * n, slots), f32), jax.ShapeDtypeStruct((3 * n, slots), f32)],
        in_specs=[smem] + [hbm] * 5,
        out_specs=[vmem, vmem],
        scratch_shapes=[pltpu.VMEM(x.shape, x.dtype) for x in operands] + [pltpu.SemaphoreType.DMA((5,))],
        compiler_params=pltpu.CompilerParams(vmem_limit_bytes=vmem_limit),
        name="prep_sources",
    )(base, *operands)


def index_kernel(spec, facts_ref, *refs):
    n, rows, cols, capacity, split = spec
    ins, (list_ref, place_ref), held, sems = refs[:5], refs[5:7], refs[7:12], refs[12]
    fetch_all(list(zip(ins, held)), sems)
    target_ref, source_ref, cluster_ref, count_ref, owner_ref = held
    my_row, my_col, device, live_pairs = [facts_ref[k] for k in range(4)]
    shift = n.bit_length() - 1
    wide = (128, 128)
    lane_row = lax.broadcasted_iota(i32, (1, 128), 1)
    sub = lax.broadcasted_iota(i32, wide, 0)
    lane = lax.broadcasted_iota(i32, wide, 1)

    blocks = target_ref.shape[1] // 128
    keys, packs = [], []
    for b in range(blocks):
        target = target_ref[:, 128 * b : 128 * (b + 1)]
        source = source_ref[:, 128 * b : 128 * (b + 1)]
        source_row = source >> shift
        index = lane_row + 128 * b
        key = jnp.where(index < live_pairs, jnp.abs(source_row - my_row), rows)
        keys.append(key * (128 * blocks) + index)
        home = target >> shift
        if split:
            home = home ^ my_col
        side = jnp.where(source_row > my_row, n, 0)
        packs.append((home * n + (target & (n - 1)) + (side + (source & (n - 1))) * 4096).astype(f32))
    key_columns = [column(key, 128) for key in keys]
    order_columns = []
    for b in range(blocks):
        before = jnp.zeros(wide, f32)
        for c in range(blocks):
            before = before + jnp.where(key_columns[c] < jnp.broadcast_to(keys[b], wide), 1.0, 0.0)
        order_columns.append(column(jnp.sum(before, axis=0, keepdims=True), 128))
    pack_columns = [column(pack, 128) for pack in packs]
    lanes = lane.astype(f32)
    for b in range(blocks):
        ordered = jnp.zeros(wide, f32)
        for c in range(blocks):
            ordered = ordered + jnp.where(order_columns[c] == lanes + 128.0 * b, pack_columns[c], 0.0)
        list_ref[b : b + 1, :] = jnp.sum(ordered, axis=0, keepdims=True).astype(i32)
    below = jnp.zeros(wide, f32)
    for c in range(blocks):
        below = below + jnp.where(key_columns[c] < lane * (128 * blocks), 1.0, 0.0)
    list_ref[blocks : blocks + 1, :] = jnp.sum(below, axis=0, keepdims=True).astype(i32)

    per_drop = cluster_ref.shape[0]
    mine = device * n + sub
    drop_blocks = owner_ref.shape[1] // 128

    def scan(j, carry):
        owner_sum, chosen, owned_before = carry
        part = pl.ds(pl.multiple_of(j * 128, 128), 128)
        owner = owner_ref[:, part]
        is_mine = jnp.where(owner == device, 1.0, 0.0)
        mine_column = column(is_mine, 128)
        rank = jnp.sum(jnp.where(sub < lane, mine_column, 0.0), axis=0, keepdims=True) + owned_before
        slot = jnp.where(owner == device, rank, -1.0)
        picked = column(slot, 128) == (lane // per_drop).astype(f32)
        for k in range(per_drop):
            cluster = cluster_ref[k : k + 1, part]
            fact = (cluster + count_ref[k : k + 1, part] * 16384).astype(f32)
            chosen = chosen + jnp.where(picked & (lane % per_drop == k), column(fact, 128), 0.0)
            wide_owner = jnp.broadcast_to(owner.astype(f32), wide)
            owner_sum = owner_sum + jnp.where(jnp.broadcast_to(cluster, wide) == mine, wide_owner, 0.0)
        return owner_sum, chosen, owned_before + jnp.sum(is_mine, axis=1, keepdims=True)

    start = (jnp.zeros(wide, f32), jnp.zeros(wide, f32), jnp.zeros((1, 1), f32))
    owner_sum, chosen, _ = lax.fori_loop(0, drop_blocks, scan, start)
    home_owner = jnp.broadcast_to(jnp.sum(owner_sum, axis=1, keepdims=True), wide)
    owner_lanes = home_owner.T
    rank = jnp.sum(jnp.where((home_owner == owner_lanes) & (sub < lane), 1.0, 0.0), axis=0, keepdims=True)
    place_ref[0:1, :] = ((owner_lanes[0:1] * capacity + rank) * 3.0).astype(i32)
    fact = jnp.sum(chosen, axis=0, keepdims=True).astype(i32)
    cluster = fact & 16383
    anchor = cluster >> shift
    cluster_column = column(cluster, 128)
    cluster_wide = jnp.broadcast_to(cluster, wide)
    same = (cluster_column >> shift) == (cluster_wide >> shift)
    rank = jnp.sum(jnp.where(same & (cluster_column < cluster_wide), 1.0, 0.0), axis=0, keepdims=True)
    place_ref[1:2, :] = (anchor * capacity + rank.astype(i32)) * 3
    place_ref[2:3, :] = fact >> 14


def index_call(spec, facts, *operands):
    blocks = operands[0].shape[1] // 128
    return pl.pallas_call(
        functools.partial(index_kernel, spec),
        out_shape=[jax.ShapeDtypeStruct((blocks + 1, 128), i32), jax.ShapeDtypeStruct((3, 128), i32)],
        in_specs=[smem] + [hbm] * 5,
        out_specs=[vmem, vmem],
        scratch_shapes=[pltpu.VMEM(x.shape, x.dtype) for x in operands] + [pltpu.SemaphoreType.DMA((5,))],
        compiler_params=pltpu.CompilerParams(vmem_limit_bytes=vmem_limit),
        name="index_work",
    )(facts, *operands)


def pack_kernel(n, place_ref, *refs):
    *speed_refs, out_ref, speed_ref = refs
    total = speed_refs[0][: 3 * n, :]
    for part in speed_refs[1:]:
        total = total + part[: 3 * n, :]
    speed_ref[...] = total
    out_ref[...] = jnp.zeros_like(out_ref)

    def step(i, carry):
        for u in range(16):
            cluster = i * 16 + u
            out_ref[pl.ds(place_ref[0, cluster], 3), :] = speed_ref[pl.ds(3 * cluster, 3), :]
        return carry

    lax.fori_loop(0, n // 16, step, 0)


def pack_call(places, speeds, n, capacity, devices):
    slots = speeds[0].shape[1]
    return pl.pallas_call(
        functools.partial(pack_kernel, n),
        out_shape=jax.ShapeDtypeStruct((devices * capacity * 3, slots), f32),
        in_specs=[smem] + [vmem] * len(speeds),
        out_specs=vmem,
        scratch_shapes=[pltpu.VMEM((3 * n, slots), f32)],
        compiler_params=pltpu.CompilerParams(vmem_limit_bytes=vmem_limit),
        name="pack_owners",
    )(places, *speeds)


def unpack_kernel(n, place_ref, arrived_ref, out_ref, tile_ref):
    slots = arrived_ref.shape[1]
    lane = lax.broadcasted_iota(i32, (3, slots), 1)

    def step(i, carry):
        for u in range(16):
            cluster = i * 16 + u
            value = arrived_ref[pl.ds(place_ref[1, cluster], 3), :]
            tile_ref[cluster, :3, :] = jnp.where(lane < place_ref[2, cluster], value, 0.0)
        return carry

    lax.fori_loop(0, n // 16, step, 0)
    for k in range(3):
        out_ref[n * k : n * (k + 1), :] = tile_ref[:, k, :]


def unpack_call(places, arrived, n):
    slots = arrived.shape[1]
    return pl.pallas_call(
        functools.partial(unpack_kernel, n),
        out_shape=jax.ShapeDtypeStruct((3 * n, slots), f32),
        in_specs=[smem, vmem],
        out_specs=vmem,
        scratch_shapes=[pltpu.VMEM((n, 8, slots), f32)],
        compiler_params=pltpu.CompilerParams(vmem_limit_bytes=vmem_limit),
        name="unpack_drops",
    )(places, arrived)


def per_device(
    positions,
    normals,
    curvature,
    pair_targets,
    pair_sources,
    pair_count,
    node_counts,
    drop_clusters,
    drop_owner,
):
    n, slots = curvature.shape
    rows = lax.axis_size("row")
    cols = lax.axis_size("col")
    devices = rows * cols
    my_row = lax.axis_index("row")
    my_col = lax.axis_index("col")
    device = my_row * cols + my_col
    capacity = max(2, 2 * n // devices)
    hypercube = cols == 4

    def swap(value, bit):
        return lax.ppermute(value, "col", [(c, c ^ bit) for c in range(cols)])

    def component_major(value):
        return jnp.transpose(value, (1, 0, 2)).reshape(3 * n, slots)

    clusters, counts = drop_clusters.T, node_counts.T
    block, position = prep_call(
        (device * n).reshape(1),
        component_major(positions),
        component_major(normals),
        curvature,
        clusters,
        counts,
    )
    mate_block = swap(block, 1)
    if hypercube:
        across = swap(position, 2)
    to_right = [(r, r + 1) for r in range(rows - 1)]
    to_left = [(r + 1, r) for r in range(rows - 1)]
    right = lax.ppermute(block, "row", to_right)
    left = lax.ppermute(block, "row", to_left)
    if hypercube:
        targets = [position, mate_block, across, swap(across, 1)]
    else:
        gathered = lax.all_gather(position, "col", axis=0, tiled=True)
        targets = [gathered[3 * n * h : 3 * n * (h + 1)] for h in range(cols)]
    listed, places = index_call(
        (n, rows, cols, capacity, hypercube),
        jnp.stack([my_row, my_col, device, pair_count[0]]),
        pair_targets,
        pair_sources,
        clusters,
        counts,
        drop_owner.reshape(1, -1),
    )
    lists = [listed, swap(listed, 1)]

    total, all_targets = hop_call(n, 0, rows, lists, targets, None, [block], [], hypercube)
    mate = [mate_block]
    for hop in range(1, rows):
        right_here, left_here = right, left
        if hop + 1 < rows:
            right, total = lax.optimization_barrier((right, total))
            right = lax.ppermute(right, "row", to_right)
            left, total = lax.optimization_barrier((left, total))
            left = lax.ppermute(left, "row", to_left)
        next_mate = [swap(right_here, 1), swap(left_here, 1)]
        (total,) = hop_call(n, hop, rows, lists, [all_targets], total, [right_here, left_here], mate, hypercube)
        mate = next_mate
    _, *speed = hop_call(n, rows, rows, lists, [all_targets], total, [], mate, hypercube)

    if hypercube:
        kept, sent = speed
        from_mate = swap(sent, 1)
        across = swap(kept[3 * n :] + from_mate[3 * n :], 2)
        home_speed = [kept, from_mate, across]
    else:
        home_speed = [lax.psum_scatter(speed[0], "col", scatter_dimension=0, tiled=True)]

    outgoing = pack_call(places, home_speed, n, capacity, devices)
    arrived = lax.all_to_all(outgoing, ("row", "col"), split_axis=0, concat_axis=0, tiled=True)
    result = unpack_call(places, arrived, n)
    return jnp.transpose(result.reshape(3, n, slots), (1, 0, 2))


def solution(mesh):
    in_specs = (
        P(("groups", "row", "col"), None, None),
        P(("groups", "row", "col"), None, None),
        P(("groups", "row", "col"), None),
        P(("groups", "row", "col"), None),
        P(("groups", "row", "col"), None),
        P(("groups", "row", "col")),
        P("groups", None),
        P("groups", None),
        P("groups"),
    )
    out_specs = P(("groups", "row", "col"), None, None)
    return jax.shard_map(
        per_device, mesh=mesh, in_specs=in_specs, out_specs=out_specs, check_vma=False
    )
```

```python
import functools
import math

import jax
import jax.numpy as jnp
from jax import lax
from jax.experimental import pallas as pl
from jax.experimental.pallas import tpu as pltpu
from jax.sharding import PartitionSpec as P

f32 = jnp.float32
bf16 = jnp.bfloat16
i32 = jnp.int32
regular_sq = 0.0025
length_scale = 1.0 / math.sqrt(regular_sq)
force_scale = length_scale / (8.0 * math.pi)
unroll = 8
vmem_limit = 24 * 2**20
kernel_flops = 8 * 10**9
whole_vmem = 60 * 2**20
vmem = pl.BlockSpec(memory_space=pltpu.VMEM)
smem = pl.BlockSpec(memory_space=pltpu.SMEM)
hbm = pl.BlockSpec(memory_space=pltpu.HBM)


def split3(value):
    high = value.astype(bf16)
    rest = value - high.astype(f32)
    mid = rest.astype(bf16)
    low = (rest - mid.astype(f32)).astype(bf16)
    return high.astype(f32), mid.astype(f32), low.astype(f32)


def rows16(upper, lower):
    return jnp.concatenate([upper, lower], axis=0).astype(bf16)


def transposed_left(y, f, slots):
    row = lax.broadcasted_iota(i32, (8, slots), 0)
    dot = -(y[0] * f[0] + y[1] * f[1] + y[2] * f[2])
    tile = jnp.where(row == 7, dot, 0.0)
    for k in range(3):
        tile = jnp.where(row == k, y[k], jnp.where(row == 3 + k, f[k], tile))
    high, mid, low = split3(tile)
    first = row < 3
    high_one = jnp.where(first, 1.0, high)
    left = jnp.concatenate(
        [rows16(high, mid), rows16(low, high_one), rows16(high_one, jnp.where(first, 1.0, mid))], axis=0
    )
    return left.T


def products(left, x, slots):
    row = lax.broadcasted_iota(i32, (8, slots), 0)
    zero = jnp.zeros((8, slots), f32)
    tile = jnp.where(row == 7, 1.0, zero)
    for k in range(3):
        tile = jnp.where((row == k) | (row == 3 + k), x[k], tile)
    high, mid, low = split3(tile)
    columns = []
    for k in range(3):
        mine = row == k
        minus = jnp.where(mine, -1.0, zero)
        columns.append(
            [
                rows16(minus, minus),
                rows16(minus, jnp.where(mine, high, 0.0)),
                rows16(jnp.where(mine, mid, 0.0), jnp.where(mine, low, 0.0)),
            ]
        )
    first = row < 3
    high, mid, low = [jnp.where(first, 0.0, part) for part in (high, mid, low)]
    columns.append([rows16(high, high), rows16(high, mid), rows16(low, mid)])
    for k in range(2):
        pick = jnp.where(row == 3 + k, 1.0, zero)
        columns.append([rows16(pick, pick), rows16(pick, zero), rows16(zero, zero)])
    right = jnp.concatenate([jnp.concatenate(column, axis=0) for column in columns], axis=1)
    return lax.dot_general(left, right, (((1,), (0,)), ((), ())), preferred_element_type=f32)


def node_sums(product, force_z, slots):
    row = lax.broadcasted_iota(i32, (8, slots), 0)
    total = None
    for g in range(slots // 8):
        part = product[8 * g : 8 * g + 8]
        wx, wy, wz, dot, fx, fy = [part[:, slots * k : slots * (k + 1)] for k in range(6)]
        fz = force_z[8 * g : 8 * g + 8]
        inverse = lax.rsqrt(wx * wx + wy * wy + (wz * wz + 1.0))
        cube = inverse * inverse * inverse
        isotropic = inverse + cube
        project = dot * cube
        terms = (isotropic * fx + project * wx, isotropic * fy + project * wy, isotropic * fz + project * wz)
        total = terms if total is None else tuple(a + b for a, b in zip(total, terms))
    sums = [jnp.broadcast_to(jnp.sum(part, axis=0, keepdims=True), (8, slots)) for part in total]
    return jnp.where(row == 0, sums[0], jnp.where(row == 1, sums[1], jnp.where(row == 2, sums[2], 0.0)))


def hop_kernel(spec, list_ref, mate_list_ref, *refs):
    n, slots, hop, homes, own, mate, first, last, split = spec
    refs = list(refs)
    if first:
        target_refs = [refs.pop(0) for _ in range(homes)]
    else:
        target_ref, before_ref = refs.pop(0), refs.pop(0)
    own_refs = [refs.pop(0) for _ in range(own)]
    mate_refs = [refs.pop(0) for _ in range(mate)]
    if first:
        total_ref, target_ref = refs.pop(0), refs.pop(0)
    else:
        total_ref = refs.pop(0)
        out_refs = [refs.pop(0) for _ in range((2 if split else 1) if last else 0)]
    source_ref, left_ref = refs
    clusters = homes * n
    shift = n.bit_length() - 1
    if first:
        for h in range(homes):
            target_ref[3 * n * h : 3 * n * (h + 1), :] = target_refs[h][: 3 * n, :]
        total_ref[...] = jnp.zeros_like(total_ref)
    for place, block in list(enumerate(own_refs)) + [(2 + b, block) for b, block in enumerate(mate_refs)]:
        source_ref[6 * n * place : 6 * n * (place + 1), :] = block[...]

    bound_row = list_ref.shape[0] - 1
    own_start, own_count, mate_start, mate_count = 0, 0, 0, 0
    if own:
        own_start = list_ref[bound_row, hop]
        own_count = (list_ref[bound_row, hop + 1] - own_start + 1) >> 1
    if mate:
        begin = mate_list_ref[bound_row, hop - 1]
        end = mate_list_ref[bound_row, hop]
        mate_start = begin + ((end - begin + 1) >> 1)
        mate_count = end - mate_start
    count = own_count + mate_count
    mate_start = mate_start - own_count

    def entry(index):
        live = index < count
        mine = index < own_count
        place = jnp.where(live, index + jnp.where(mine, own_start, mate_start), 0)
        row, lane = place >> 7, place & 127
        target, source = 0, 0
        if own:
            packed = list_ref[row, lane]
            target, source = packed & 0xFFF, packed >> 12
        if mate:
            packed = mate_list_ref[row, lane]
            flip = n if split else 0
            mate_target, mate_source = (packed & 0xFFF) ^ flip, (packed >> 12) + 2 * n
            target = jnp.where(mine, target, mate_target)
            source = jnp.where(mine, source, mate_source)
        return live, jnp.where(live, target, 0), jnp.where(live, source, 0)

    def source_rows(source):
        base = source + (source >> shift) * (5 * n)
        return [source_ref[pl.ds(base + n * k, 1), :] for k in range(6)]

    def wide(value):
        return jnp.broadcast_to(value, (8, slots))

    def fetch(index, u):
        _, _, source = entry(index)
        values = [wide(value) for value in source_rows(source)]
        left_ref[u] = transposed_left(values[:3], values[3:], slots)

    @pl.when(count > 0)
    def _():
        for u in range(unroll):
            fetch(u, u)

    def step(i, carry):
        results = []
        lefts = [left_ref[u] for u in range(unroll)]
        for u in range(unroll):
            live, target, source = entry(i * unroll + u)
            base = target + (target >> shift) * (2 * n)
            x = [wide(target_ref[pl.ds(base + n * k, 1), :]) for k in range(3)]
            product = products(lefts[u], x, slots)
            force_z = source_ref[pl.ds(source + (source >> shift) * (5 * n) + 5 * n, 1), :]
            force_z = jnp.broadcast_to(force_z, (slots, slots)).T
            results.append((jnp.where(live, target, clusters), node_sums(product, force_z, slots)))
        for u in range(unroll):
            fetch((i + 1) * unroll + u, u)
        for target, result in results:
            total_ref[pl.ds(pl.multiple_of(target * 8, 8), 8), :] += result
        return carry

    lax.fori_loop(0, (count + unroll - 1) // unroll, step, 0)
    if last:
        for h in range(homes):
            out_ref = out_refs[h % 2] if split else out_refs[0]
            first_row = 3 * n * (h // 2 if split else h)

            def move(i, carry, h=h, out_ref=out_ref, first_row=first_row):
                for u in range(8):
                    tile = total_ref[pl.ds(pl.multiple_of((n * h + i * 8 + u) * 8, 8), 8), :]
                    out_ref[pl.ds(first_row + i * 24 + 3 * u, 3), :] = tile[:3]
                return carry

            lax.fori_loop(0, n // 8, move, 0)


def hop_call(n, hop, hops, lists, targets, total, own, mate, split):
    first, last = hop == 0, hop == hops
    slots = own[0].shape[1] if own else mate[0].shape[1]
    homes = len(targets) if first else targets[0].shape[0] // (3 * n)
    total_shape = jax.ShapeDtypeStruct((homes * n * 8 + 8, slots), f32)
    aliases = {}
    operands = [*lists, *targets]
    if not first:
        operands.append(total)
    if first:
        out_shape = [total_shape, jax.ShapeDtypeStruct((homes * 3 * n, slots), f32)]
    elif last:
        parts = 2 if split else 1
        out_shape = [total_shape] + [jax.ShapeDtypeStruct((homes * 3 * n // parts, slots), f32)] * parts
    else:
        out_shape = [total_shape]
    if not first:
        aliases = {len(operands) - 1: 0}
    operands += [*own, *mate]
    spec = (n, slots, hop, homes, len(own), len(mate), first, last, split)
    return pl.pallas_call(
        functools.partial(hop_kernel, spec),
        out_shape=out_shape,
        in_specs=[smem, smem] + [vmem] * (len(operands) - 2),
        out_specs=[vmem] * len(out_shape),
        scratch_shapes=[
            pltpu.VMEM((4 * 6 * n, slots), f32),
            pltpu.VMEM((unroll, slots, 48), bf16),
        ],
        input_output_aliases=aliases,
        compiler_params=pltpu.CompilerParams(vmem_limit_bytes=vmem_limit),
        cost_estimate=pl.CostEstimate(flops=kernel_flops if hop else kernel_flops // 8, bytes_accessed=10**6, transcendentals=10**6),
        name=f"pairs_hop{hop}",
    )(*operands)


def column(row, rows):
    return jnp.broadcast_to(row, (rows, 128)).T


def prep_kernel(n, base_ref, *refs):
    ins, (out_ref, own_ref, small_ref), held, sems = refs[:8], refs[8:11], refs[11:19], refs[19]
    copies = [pltpu.make_async_copy(a, b, sems.at[k]) for k, (a, b) in enumerate(zip(ins, held))]
    for copy in copies:
        copy.start()
    for copy in copies:
        copy.wait()
    position_ref, normal_ref, curvature_ref, cluster_ref, count_ref, owner_ref, target_ref, source_ref = held
    slots = position_ref.shape[1]
    scaled = position_ref[...] * length_scale
    out_ref[: 3 * n, :] = scaled
    own_ref[...] = scaled
    mine = base_ref[0] + lax.broadcasted_iota(i32, (n, 128), 0)
    total = jnp.zeros((n, 128), f32)
    for k in range(cluster_ref.shape[0]):
        for j in range(cluster_ref.shape[1] // 128):
            part = slice(128 * j, 128 * (j + 1))
            cluster = jnp.broadcast_to(cluster_ref[k : k + 1, part], (n, 128))
            count = jnp.broadcast_to(count_ref[k : k + 1, part].astype(f32), (n, 128))
            total = total + jnp.where(cluster == mine, count, 0.0)
    live_count = jnp.sum(total, axis=1, keepdims=True)
    lane = lax.broadcasted_iota(i32, (n, slots), 1).astype(f32)
    strength = jnp.where(lane < live_count, curvature_ref[...] * force_scale, 0.0)
    for k in range(3):
        out_ref[n * (3 + k) : n * (4 + k), :] = normal_ref[n * k : n * (k + 1), :] * strength
    per_drop, drops = cluster_ref.shape
    pairs = target_ref.shape[1]
    small_ref[:per_drop, :drops] = cluster_ref[...] + (count_ref[...] << 14)
    small_ref[per_drop : per_drop + 1, :drops] = owner_ref[...]
    small_ref[per_drop + 1 : per_drop + 2, :pairs] = target_ref[...]
    small_ref[per_drop + 2 : per_drop + 3, :pairs] = source_ref[...]


def prep_call(base, *operands):
    n, slots = operands[2].shape
    per_drop, drops = operands[3].shape
    small = (per_drop + 8, max(drops, operands[6].shape[1]))
    shapes = [((6 * n, slots), f32), ((3 * n, slots), f32), (small, i32)]
    return pl.pallas_call(
        functools.partial(prep_kernel, n),
        out_shape=[jax.ShapeDtypeStruct(*shape) for shape in shapes],
        in_specs=[smem] + [hbm] * 8,
        out_specs=[vmem] * 3,
        scratch_shapes=[pltpu.VMEM(x.shape, x.dtype) for x in operands] + [pltpu.SemaphoreType.DMA((8,))],
        compiler_params=pltpu.CompilerParams(vmem_limit_bytes=whole_vmem),
        name="prep_sources",
    )(base, *operands)


def index_kernel(spec, facts_ref, *refs):
    n, rows, capacity, per_drop, drops, pair_slots, split = spec
    small_ref, list_ref, place_ref = refs
    my_row, my_col, device, live_pairs = [facts_ref[k] for k in range(4)]
    shift = n.bit_length() - 1
    wide = (128, 128)
    lane_row = lax.broadcasted_iota(i32, (1, 128), 1)
    sub = lax.broadcasted_iota(i32, wide, 0)
    lane = lax.broadcasted_iota(i32, wide, 1)

    blocks = pair_slots // 128
    keys, packs = [], []
    for b in range(blocks):
        target = small_ref[per_drop + 1 : per_drop + 2, 128 * b : 128 * (b + 1)]
        source = small_ref[per_drop + 2 : per_drop + 3, 128 * b : 128 * (b + 1)]
        source_row = source >> shift
        index = lane_row + 128 * b
        key = jnp.where(index < live_pairs, jnp.abs(source_row - my_row), rows)
        keys.append(key * (128 * blocks) + index)
        home = target >> shift
        if split:
            home = home ^ my_col
        side = jnp.where(source_row > my_row, n, 0)
        packs.append((home * n + (target & (n - 1)) + (side + (source & (n - 1))) * 4096).astype(f32))
    key_columns = [column(key, 128) for key in keys]
    order_columns = []
    for b in range(blocks):
        before = jnp.zeros(wide, f32)
        for c in range(blocks):
            before = before + jnp.where(key_columns[c] < jnp.broadcast_to(keys[b], wide), 1.0, 0.0)
        order_columns.append(column(jnp.sum(before, axis=0, keepdims=True), 128))
    pack_columns = [column(pack, 128) for pack in packs]
    lanes = lane.astype(f32)
    for b in range(blocks):
        ordered = jnp.zeros(wide, f32)
        for c in range(blocks):
            ordered = ordered + jnp.where(order_columns[c] == lanes + 128.0 * b, pack_columns[c], 0.0)
        list_ref[b : b + 1, :] = jnp.sum(ordered, axis=0, keepdims=True).astype(i32)
    below = jnp.zeros(wide, f32)
    for c in range(blocks):
        below = below + jnp.where(key_columns[c] < lane * (128 * blocks), 1.0, 0.0)
    list_ref[blocks : blocks + 1, :] = jnp.sum(below, axis=0, keepdims=True).astype(i32)

    mine = device * n + sub

    def scan(j, carry):
        owner_sum, chosen, owned_before = carry
        part = pl.ds(pl.multiple_of(j * 128, 128), 128)
        owner = small_ref[per_drop : per_drop + 1, part]
        is_mine = jnp.where(owner == device, 1.0, 0.0)
        mine_column = column(is_mine, 128)
        rank = jnp.sum(jnp.where(sub < lane, mine_column, 0.0), axis=0, keepdims=True) + owned_before
        slot = jnp.where(owner == device, rank, -1.0)
        picked = column(slot, 128) == (lane // per_drop).astype(f32)
        for k in range(per_drop):
            fact = small_ref[k : k + 1, part]
            cluster = fact & 16383
            chosen = chosen + jnp.where(picked & (lane % per_drop == k), column(fact.astype(f32), 128), 0.0)
            wide_owner = jnp.broadcast_to(owner.astype(f32), wide)
            owner_sum = owner_sum + jnp.where(jnp.broadcast_to(cluster, wide) == mine, wide_owner, 0.0)
        return owner_sum, chosen, owned_before + jnp.sum(is_mine, axis=1, keepdims=True)

    start = (jnp.zeros(wide, f32), jnp.zeros(wide, f32), jnp.zeros((1, 1), f32))
    owner_sum, chosen, _ = lax.fori_loop(0, drops // 128, scan, start)
    home_owner = jnp.broadcast_to(jnp.sum(owner_sum, axis=1, keepdims=True), wide)
    owner_lanes = home_owner.T
    rank = jnp.sum(jnp.where((home_owner == owner_lanes) & (sub < lane), 1.0, 0.0), axis=0, keepdims=True)
    place_ref[0:1, :] = ((owner_lanes[0:1] * capacity + rank) * 3.0).astype(i32)
    fact = jnp.sum(chosen, axis=0, keepdims=True).astype(i32)
    cluster = fact & 16383
    anchor = cluster >> shift
    cluster_column = column(cluster, 128)
    cluster_wide = jnp.broadcast_to(cluster, wide)
    same = (cluster_column >> shift) == (cluster_wide >> shift)
    rank = jnp.sum(jnp.where(same & (cluster_column < cluster_wide), 1.0, 0.0), axis=0, keepdims=True)
    place_ref[1:2, :] = (anchor * capacity + rank.astype(i32)) * 3
    place_ref[2:3, :] = fact >> 14


def index_call(spec, facts, small):
    return pl.pallas_call(
        functools.partial(index_kernel, spec),
        out_shape=[jax.ShapeDtypeStruct((spec[5] // 128 + 1, 128), i32), jax.ShapeDtypeStruct((3, 128), i32)],
        in_specs=[smem, vmem],
        out_specs=[vmem, vmem],
        compiler_params=pltpu.CompilerParams(vmem_limit_bytes=vmem_limit),
        name="index_work",
    )(facts, small)


def pack_kernel(n, place_ref, *refs):
    *speed_refs, out_ref, speed_ref = refs
    total = speed_refs[0][: 3 * n, :]
    for part in speed_refs[1:]:
        total = total + part[: 3 * n, :]
    speed_ref[...] = total
    out_ref[...] = jnp.zeros_like(out_ref)

    def step(i, carry):
        for u in range(16):
            cluster = i * 16 + u
            out_ref[pl.ds(place_ref[0, cluster], 3), :] = speed_ref[pl.ds(3 * cluster, 3), :]
        return carry

    lax.fori_loop(0, n // 16, step, 0)


def pack_call(places, speeds, n, capacity, devices):
    slots = speeds[0].shape[1]
    return pl.pallas_call(
        functools.partial(pack_kernel, n),
        out_shape=jax.ShapeDtypeStruct((devices * capacity * 3, slots), f32),
        in_specs=[smem] + [vmem] * len(speeds),
        out_specs=vmem,
        scratch_shapes=[pltpu.VMEM((3 * n, slots), f32)],
        compiler_params=pltpu.CompilerParams(vmem_limit_bytes=vmem_limit),
        name="pack_owners",
    )(places, *speeds)


def unpack_kernel(n, place_ref, arrived_ref, out_ref, tile_ref):
    slots = arrived_ref.shape[1]
    lane = lax.broadcasted_iota(i32, (3, slots), 1)

    def step(i, carry):
        for u in range(16):
            cluster = i * 16 + u
            value = arrived_ref[pl.ds(place_ref[1, cluster], 3), :]
            tile_ref[cluster, :3, :] = jnp.where(lane < place_ref[2, cluster], value, 0.0)
        return carry

    lax.fori_loop(0, n // 16, step, 0)
    for k in range(3):
        out_ref[n * k : n * (k + 1), :] = tile_ref[:, k, :]


def unpack_call(places, arrived, n):
    slots = arrived.shape[1]
    return pl.pallas_call(
        functools.partial(unpack_kernel, n),
        out_shape=jax.ShapeDtypeStruct((3 * n, slots), f32),
        in_specs=[smem, vmem],
        out_specs=vmem,
        scratch_shapes=[pltpu.VMEM((n, 8, slots), f32)],
        compiler_params=pltpu.CompilerParams(vmem_limit_bytes=vmem_limit),
        name="unpack_drops",
    )(places, arrived)


def per_device(
    positions,
    normals,
    curvature,
    pair_targets,
    pair_sources,
    pair_count,
    node_counts,
    drop_clusters,
    drop_owner,
):
    n, slots = curvature.shape
    rows = lax.axis_size("row")
    cols = lax.axis_size("col")
    devices = rows * cols
    my_row = lax.axis_index("row")
    my_col = lax.axis_index("col")
    device = my_row * cols + my_col
    capacity = max(2, 2 * n // devices)
    hypercube = cols == 4

    def swap(value, bit):
        return lax.ppermute(value, "col", [(c, c ^ bit) for c in range(cols)])

    def component_major(value):
        return jnp.transpose(value, (1, 0, 2)).reshape(3 * n, slots)

    block, position, small = prep_call(
        (device * n).reshape(1),
        component_major(positions),
        component_major(normals),
        curvature,
        drop_clusters.T,
        node_counts.T,
        drop_owner.reshape(1, -1),
        pair_targets,
        pair_sources,
    )
    mate_block = swap(block, 1)
    if hypercube:
        across = swap(position, 2)
    to_right = [(r, r + 1) for r in range(rows - 1)]
    to_left = [(r + 1, r) for r in range(rows - 1)]
    right = lax.ppermute(block, "row", to_right)
    left = lax.ppermute(block, "row", to_left)
    if hypercube:
        targets = [position, mate_block, across, swap(across, 1)]
    else:
        gathered = lax.all_gather(position, "col", axis=0, tiled=True)
        targets = [gathered[3 * n * h : 3 * n * (h + 1)] for h in range(cols)]
    listed, places = index_call(
        (n, rows, capacity, drop_clusters.shape[1], drop_clusters.shape[0], pair_targets.shape[1], hypercube),
        jnp.stack([my_row, my_col, device, pair_count[0]]),
        small,
    )
    lists = [listed, swap(listed, 1)]

    total, all_targets = hop_call(n, 0, rows, lists, targets, None, [block], [], hypercube)
    mate = [mate_block]
    for hop in range(1, rows):
        right_here, left_here = right, left
        if hop + 1 < rows:
            right, total = lax.optimization_barrier((right, total))
            right = lax.ppermute(right, "row", to_right)
            left, total = lax.optimization_barrier((left, total))
            left = lax.ppermute(left, "row", to_left)
        next_mate = [swap(right_here, 1), swap(left_here, 1)]
        (total,) = hop_call(n, hop, rows, lists, [all_targets], total, [right_here, left_here], mate, hypercube)
        mate = next_mate
    _, *speed = hop_call(n, rows, rows, lists, [all_targets], total, [], mate, hypercube)

    if hypercube:
        kept, sent = speed
        from_mate = swap(sent, 1)
        across = swap(kept[3 * n :] + from_mate[3 * n :], 2)
        home_speed = [kept, from_mate, across]
    else:
        home_speed = [lax.psum_scatter(speed[0], "col", scatter_dimension=0, tiled=True)]

    outgoing = pack_call(places, home_speed, n, capacity, devices)
    arrived = lax.all_to_all(outgoing, ("row", "col"), split_axis=0, concat_axis=0, tiled=True)
    result = unpack_call(places, arrived, n)
    return jnp.transpose(result.reshape(3, n, slots), (1, 0, 2))


def solution(mesh):
    in_specs = (
        P(("groups", "row", "col"), None, None),
        P(("groups", "row", "col"), None, None),
        P(("groups", "row", "col"), None),
        P(("groups", "row", "col"), None),
        P(("groups", "row", "col"), None),
        P(("groups", "row", "col")),
        P("groups", None),
        P("groups", None),
        P("groups"),
    )
    out_specs = P(("groups", "row", "col"), None, None)
    return jax.shard_map(
        per_device, mesh=mesh, in_specs=in_specs, out_specs=out_specs, check_vma=False
    )
```

```python
import functools
import math

import jax
import jax.numpy as jnp
from jax import lax
from jax.experimental import pallas as pl
from jax.experimental.pallas import tpu as pltpu
from jax.sharding import PartitionSpec as P

f32 = jnp.float32
bf16 = jnp.bfloat16
i32 = jnp.int32
regular_sq = 0.0025
length_scale = 1.0 / math.sqrt(regular_sq)
force_scale = length_scale / (8.0 * math.pi)
unroll = 8
vmem_limit = 24 * 2**20
kernel_flops = 8 * 10**9
whole_vmem = 60 * 2**20
vmem = pl.BlockSpec(memory_space=pltpu.VMEM)
smem = pl.BlockSpec(memory_space=pltpu.SMEM)
hbm = pl.BlockSpec(memory_space=pltpu.HBM)


def split3(value):
    high = value.astype(bf16)
    rest = value - high.astype(f32)
    mid = rest.astype(bf16)
    low = (rest - mid.astype(f32)).astype(bf16)
    return high.astype(f32), mid.astype(f32), low.astype(f32)


def rows16(upper, lower):
    return jnp.concatenate([upper, lower], axis=0).astype(bf16)


def transposed_left(y, f, slots):
    row = lax.broadcasted_iota(i32, (8, slots), 0)
    dot = -(y[0] * f[0] + y[1] * f[1] + y[2] * f[2])
    tile = jnp.where(row == 7, dot, 0.0)
    for k in range(3):
        tile = jnp.where(row == k, y[k], jnp.where(row == 3 + k, f[k], tile))
    high, mid, low = split3(tile)
    first = row < 3
    high_one = jnp.where(first, 1.0, high)
    left = jnp.concatenate(
        [rows16(high, mid), rows16(low, high_one), rows16(high_one, jnp.where(first, 1.0, mid))], axis=0
    )
    return left.T


def products(left, x, slots):
    row = lax.broadcasted_iota(i32, (8, slots), 0)
    zero = jnp.zeros((8, slots), f32)
    tile = jnp.where(row == 7, 1.0, zero)
    for k in range(3):
        tile = jnp.where((row == k) | (row == 3 + k), x[k], tile)
    high, mid, low = split3(tile)
    columns = []
    for k in range(3):
        mine = row == k
        minus = jnp.where(mine, -1.0, zero)
        columns.append(
            [
                rows16(minus, minus),
                rows16(minus, jnp.where(mine, high, 0.0)),
                rows16(jnp.where(mine, mid, 0.0), jnp.where(mine, low, 0.0)),
            ]
        )
    first = row < 3
    high, mid, low = [jnp.where(first, 0.0, part) for part in (high, mid, low)]
    columns.append([rows16(high, high), rows16(high, mid), rows16(low, mid)])
    for k in range(2):
        pick = jnp.where(row == 3 + k, 1.0, zero)
        columns.append([rows16(pick, pick), rows16(pick, zero), rows16(zero, zero)])
    right = jnp.concatenate([jnp.concatenate(column, axis=0) for column in columns], axis=1)
    return lax.dot_general(left, right, (((1,), (0,)), ((), ())), preferred_element_type=f32)


def node_sums(product, force_z, slots):
    row = lax.broadcasted_iota(i32, (8, slots), 0)
    total = None
    for g in range(slots // 8):
        part = product[8 * g : 8 * g + 8]
        wx, wy, wz, dot, fx, fy = [part[:, slots * k : slots * (k + 1)] for k in range(6)]
        fz = force_z[8 * g : 8 * g + 8]
        inverse = lax.rsqrt(wx * wx + wy * wy + (wz * wz + 1.0))
        cube = inverse * inverse * inverse
        isotropic = inverse + cube
        project = dot * cube
        terms = (isotropic * fx + project * wx, isotropic * fy + project * wy, isotropic * fz + project * wz)
        total = terms if total is None else tuple(a + b for a, b in zip(total, terms))
    sums = [jnp.broadcast_to(jnp.sum(part, axis=0, keepdims=True), (8, slots)) for part in total]
    return jnp.where(row == 0, sums[0], jnp.where(row == 1, sums[1], jnp.where(row == 2, sums[2], 0.0)))


def hop_kernel(spec, list_ref, mate_list_ref, *refs):
    n, slots, hop, homes, own, mate, first, last, split = spec
    refs = list(refs)
    if first:
        target_refs = [refs.pop(0) for _ in range(homes)]
    else:
        target_ref, before_ref = refs.pop(0), refs.pop(0)
    own_refs = [refs.pop(0) for _ in range(own)]
    mate_refs = [refs.pop(0) for _ in range(mate)]
    if first:
        total_ref, target_ref = refs.pop(0), refs.pop(0)
    else:
        total_ref = refs.pop(0)
        out_refs = [refs.pop(0) for _ in range((2 if split else 1) if last else 0)]
    source_ref, left_ref = refs
    clusters = homes * n
    shift = n.bit_length() - 1
    if first:
        for h in range(homes):
            target_ref[3 * n * h : 3 * n * (h + 1), :] = target_refs[h][: 3 * n, :]
        total_ref[...] = jnp.zeros_like(total_ref)
    for place, block in list(enumerate(own_refs)) + [(2 + b, block) for b, block in enumerate(mate_refs)]:
        source_ref[6 * n * place : 6 * n * (place + 1), :] = block[...]

    bound_row = list_ref.shape[0] - 1
    own_start, own_count, mate_start, mate_count = 0, 0, 0, 0
    if own:
        own_start = list_ref[bound_row, hop]
        own_count = (list_ref[bound_row, hop + 1] - own_start + 1) >> 1
    if mate:
        begin = mate_list_ref[bound_row, hop]
        end = mate_list_ref[bound_row, hop + 1]
        mate_start = begin + ((end - begin + 1) >> 1)
        mate_count = end - mate_start
    count = own_count + mate_count
    mate_start = mate_start - own_count

    def entry(index):
        live = index < count
        mine = index < own_count
        place = jnp.where(live, index + jnp.where(mine, own_start, mate_start), 0)
        row, lane = place >> 7, place & 127
        target, source = 0, 0
        if own:
            packed = list_ref[row, lane]
            target, source = packed & 0xFFF, packed >> 12
        if mate:
            packed = mate_list_ref[row, lane]
            flip = n if split else 0
            mate_target, mate_source = (packed & 0xFFF) ^ flip, (packed >> 12) + 2 * n
            target = jnp.where(mine, target, mate_target)
            source = jnp.where(mine, source, mate_source)
        return live, jnp.where(live, target, 0), jnp.where(live, source, 0)

    def source_rows(source):
        base = source + (source >> shift) * (5 * n)
        return [source_ref[pl.ds(base + n * k, 1), :] for k in range(6)]

    def wide(value):
        return jnp.broadcast_to(value, (8, slots))

    def fetch(index, u):
        _, _, source = entry(index)
        values = [wide(value) for value in source_rows(source)]
        left_ref[u] = transposed_left(values[:3], values[3:], slots)

    @pl.when(count > 0)
    def _():
        for u in range(unroll):
            fetch(u, u)

    def step(i, carry):
        results = []
        lefts = [left_ref[u] for u in range(unroll)]
        for u in range(unroll):
            live, target, source = entry(i * unroll + u)
            base = target + (target >> shift) * (2 * n)
            x = [wide(target_ref[pl.ds(base + n * k, 1), :]) for k in range(3)]
            product = products(lefts[u], x, slots)
            force_z = source_ref[pl.ds(source + (source >> shift) * (5 * n) + 5 * n, 1), :]
            force_z = jnp.broadcast_to(force_z, (slots, slots)).T
            results.append((jnp.where(live, target, clusters), node_sums(product, force_z, slots)))
        for u in range(unroll):
            fetch((i + 1) * unroll + u, u)
        for target, result in results:
            total_ref[pl.ds(pl.multiple_of(target * 8, 8), 8), :] += result
        return carry

    lax.fori_loop(0, (count + unroll - 1) // unroll, step, 0)
    if last:
        for h in range(homes):
            out_ref = out_refs[h % 2] if split else out_refs[0]
            first_row = 3 * n * (h // 2 if split else h)

            def move(i, carry, h=h, out_ref=out_ref, first_row=first_row):
                for u in range(8):
                    tile = total_ref[pl.ds(pl.multiple_of((n * h + i * 8 + u) * 8, 8), 8), :]
                    out_ref[pl.ds(first_row + i * 24 + 3 * u, 3), :] = tile[:3]
                return carry

            lax.fori_loop(0, n // 8, move, 0)


def hop_call(n, hop, hops, lists, targets, total, own, mate, split):
    first, last = hop == 0, hop == hops - 1
    slots = own[0].shape[1]
    homes = len(targets) if first else targets[0].shape[0] // (3 * n)
    total_shape = jax.ShapeDtypeStruct((homes * n * 8 + 8, slots), f32)
    aliases = {}
    operands = [*lists, *targets]
    if not first:
        operands.append(total)
    if first:
        out_shape = [total_shape, jax.ShapeDtypeStruct((homes * 3 * n, slots), f32)]
    elif last:
        parts = 2 if split else 1
        out_shape = [total_shape] + [jax.ShapeDtypeStruct((homes * 3 * n // parts, slots), f32)] * parts
    else:
        out_shape = [total_shape]
    if not first:
        aliases = {len(operands) - 1: 0}
    operands += [*own, *mate]
    spec = (n, slots, hop, homes, len(own), len(mate), first, last, split)
    return pl.pallas_call(
        functools.partial(hop_kernel, spec),
        out_shape=out_shape,
        in_specs=[smem, smem] + [vmem] * (len(operands) - 2),
        out_specs=[vmem] * len(out_shape),
        scratch_shapes=[
            pltpu.VMEM((4 * 6 * n, slots), f32),
            pltpu.VMEM((unroll, slots, 48), bf16),
        ],
        input_output_aliases=aliases,
        compiler_params=pltpu.CompilerParams(vmem_limit_bytes=vmem_limit),
        cost_estimate=pl.CostEstimate(flops=kernel_flops if hop else kernel_flops // 8, bytes_accessed=10**6, transcendentals=10**6),
        name=f"pairs_hop{hop}",
    )(*operands)


def column(row, rows):
    return jnp.broadcast_to(row, (rows, 128)).T


def prep_kernel(n, base_ref, *refs):
    ins, (out_ref, own_ref, small_ref), held, sems = refs[:8], refs[8:11], refs[11:19], refs[19]
    copies = [pltpu.make_async_copy(a, b, sems.at[k]) for k, (a, b) in enumerate(zip(ins, held))]
    for copy in copies:
        copy.start()
    for copy in copies:
        copy.wait()
    position_ref, normal_ref, curvature_ref, cluster_ref, count_ref, owner_ref, target_ref, source_ref = held
    slots = position_ref.shape[1]
    scaled = position_ref[...] * length_scale
    out_ref[: 3 * n, :] = scaled
    own_ref[...] = scaled
    mine = base_ref[0] + lax.broadcasted_iota(i32, (n, 128), 0)
    total = jnp.zeros((n, 128), f32)
    for k in range(cluster_ref.shape[0]):
        for j in range(cluster_ref.shape[1] // 128):
            part = slice(128 * j, 128 * (j + 1))
            cluster = jnp.broadcast_to(cluster_ref[k : k + 1, part], (n, 128))
            count = jnp.broadcast_to(count_ref[k : k + 1, part].astype(f32), (n, 128))
            total = total + jnp.where(cluster == mine, count, 0.0)
    live_count = jnp.sum(total, axis=1, keepdims=True)
    lane = lax.broadcasted_iota(i32, (n, slots), 1).astype(f32)
    strength = jnp.where(lane < live_count, curvature_ref[...] * force_scale, 0.0)
    for k in range(3):
        out_ref[n * (3 + k) : n * (4 + k), :] = normal_ref[n * k : n * (k + 1), :] * strength
    per_drop, drops = cluster_ref.shape
    pairs = target_ref.shape[1]
    small_ref[:per_drop, :drops] = cluster_ref[...] + (count_ref[...] << 14)
    small_ref[per_drop : per_drop + 1, :drops] = owner_ref[...]
    small_ref[per_drop + 1 : per_drop + 2, :pairs] = target_ref[...]
    small_ref[per_drop + 2 : per_drop + 3, :pairs] = source_ref[...]


def prep_call(base, *operands):
    n, slots = operands[2].shape
    per_drop, drops = operands[3].shape
    small = (per_drop + 8, max(drops, operands[6].shape[1]))
    shapes = [((6 * n, slots), f32), ((3 * n, slots), f32), (small, i32)]
    return pl.pallas_call(
        functools.partial(prep_kernel, n),
        out_shape=[jax.ShapeDtypeStruct(*shape) for shape in shapes],
        in_specs=[smem] + [hbm] * 8,
        out_specs=[vmem] * 3,
        scratch_shapes=[pltpu.VMEM(x.shape, x.dtype) for x in operands] + [pltpu.SemaphoreType.DMA((8,))],
        compiler_params=pltpu.CompilerParams(vmem_limit_bytes=whole_vmem),
        name="prep_sources",
    )(base, *operands)


def index_kernel(spec, facts_ref, *refs):
    n, rows, capacity, per_drop, drops, pair_slots, split = spec
    small_ref, list_ref, place_ref = refs
    my_row, my_col, device, live_pairs = [facts_ref[k] for k in range(4)]
    shift = n.bit_length() - 1
    wide = (128, 128)
    lane_row = lax.broadcasted_iota(i32, (1, 128), 1)
    sub = lax.broadcasted_iota(i32, wide, 0)
    lane = lax.broadcasted_iota(i32, wide, 1)

    blocks = pair_slots // 128
    keys, packs = [], []
    for b in range(blocks):
        target = small_ref[per_drop + 1 : per_drop + 2, 128 * b : 128 * (b + 1)]
        source = small_ref[per_drop + 2 : per_drop + 3, 128 * b : 128 * (b + 1)]
        ahead = ((source >> shift) - my_row) & (rows - 1)
        hop = jnp.minimum(ahead, rows - ahead)
        index = lane_row + 128 * b
        key = jnp.where(index < live_pairs, hop, rows)
        keys.append(key * (128 * blocks) + index)
        home = target >> shift
        if split:
            home = home ^ my_col
        side = jnp.where((ahead > 0) & (ahead * 2 < rows), n, 0)
        packs.append((home * n + (target & (n - 1)) + (side + (source & (n - 1))) * 4096).astype(f32))
    key_columns = [column(key, 128) for key in keys]
    order_columns = []
    for b in range(blocks):
        before = jnp.zeros(wide, f32)
        for c in range(blocks):
            before = before + jnp.where(key_columns[c] < jnp.broadcast_to(keys[b], wide), 1.0, 0.0)
        order_columns.append(column(jnp.sum(before, axis=0, keepdims=True), 128))
    pack_columns = [column(pack, 128) for pack in packs]
    lanes = lane.astype(f32)
    for b in range(blocks):
        ordered = jnp.zeros(wide, f32)
        for c in range(blocks):
            ordered = ordered + jnp.where(order_columns[c] == lanes + 128.0 * b, pack_columns[c], 0.0)
        list_ref[b : b + 1, :] = jnp.sum(ordered, axis=0, keepdims=True).astype(i32)
    below = jnp.zeros(wide, f32)
    for c in range(blocks):
        below = below + jnp.where(key_columns[c] < lane * (128 * blocks), 1.0, 0.0)
    list_ref[blocks : blocks + 1, :] = jnp.sum(below, axis=0, keepdims=True).astype(i32)

    mine = device * n + sub

    def scan(j, carry):
        owner_sum, chosen, owned_before = carry
        part = pl.ds(pl.multiple_of(j * 128, 128), 128)
        owner = small_ref[per_drop : per_drop + 1, part]
        is_mine = jnp.where(owner == device, 1.0, 0.0)
        mine_column = column(is_mine, 128)
        rank = jnp.sum(jnp.where(sub < lane, mine_column, 0.0), axis=0, keepdims=True) + owned_before
        slot = jnp.where(owner == device, rank, -1.0)
        picked = column(slot, 128) == (lane // per_drop).astype(f32)
        for k in range(per_drop):
            fact = small_ref[k : k + 1, part]
            cluster = fact & 16383
            chosen = chosen + jnp.where(picked & (lane % per_drop == k), column(fact.astype(f32), 128), 0.0)
            wide_owner = jnp.broadcast_to(owner.astype(f32), wide)
            owner_sum = owner_sum + jnp.where(jnp.broadcast_to(cluster, wide) == mine, wide_owner, 0.0)
        return owner_sum, chosen, owned_before + jnp.sum(is_mine, axis=1, keepdims=True)

    start = (jnp.zeros(wide, f32), jnp.zeros(wide, f32), jnp.zeros((1, 1), f32))
    owner_sum, chosen, _ = lax.fori_loop(0, drops // 128, scan, start)
    home_owner = jnp.broadcast_to(jnp.sum(owner_sum, axis=1, keepdims=True), wide)
    owner_lanes = home_owner.T
    rank = jnp.sum(jnp.where((home_owner == owner_lanes) & (sub < lane), 1.0, 0.0), axis=0, keepdims=True)
    place_ref[0:1, :] = ((owner_lanes[0:1] * capacity + rank) * 3.0).astype(i32)
    fact = jnp.sum(chosen, axis=0, keepdims=True).astype(i32)
    cluster = fact & 16383
    anchor = cluster >> shift
    cluster_column = column(cluster, 128)
    cluster_wide = jnp.broadcast_to(cluster, wide)
    same = (cluster_column >> shift) == (cluster_wide >> shift)
    rank = jnp.sum(jnp.where(same & (cluster_column < cluster_wide), 1.0, 0.0), axis=0, keepdims=True)
    place_ref[1:2, :] = (anchor * capacity + rank.astype(i32)) * 3
    place_ref[2:3, :] = fact >> 14


def index_call(spec, facts, small):
    return pl.pallas_call(
        functools.partial(index_kernel, spec),
        out_shape=[jax.ShapeDtypeStruct((spec[5] // 128 + 1, 128), i32), jax.ShapeDtypeStruct((3, 128), i32)],
        in_specs=[smem, vmem],
        out_specs=[vmem, vmem],
        compiler_params=pltpu.CompilerParams(vmem_limit_bytes=vmem_limit),
        name="index_work",
    )(facts, small)


def pack_kernel(n, place_ref, *refs):
    *speed_refs, out_ref, speed_ref = refs
    total = speed_refs[0][: 3 * n, :]
    for part in speed_refs[1:]:
        total = total + part[: 3 * n, :]
    speed_ref[...] = total
    out_ref[...] = jnp.zeros_like(out_ref)

    def step(i, carry):
        for u in range(16):
            cluster = i * 16 + u
            out_ref[pl.ds(place_ref[0, cluster], 3), :] = speed_ref[pl.ds(3 * cluster, 3), :]
        return carry

    lax.fori_loop(0, n // 16, step, 0)


def pack_call(places, speeds, n, capacity, devices):
    slots = speeds[0].shape[1]
    return pl.pallas_call(
        functools.partial(pack_kernel, n),
        out_shape=jax.ShapeDtypeStruct((devices * capacity * 3, slots), f32),
        in_specs=[smem] + [vmem] * len(speeds),
        out_specs=vmem,
        scratch_shapes=[pltpu.VMEM((3 * n, slots), f32)],
        compiler_params=pltpu.CompilerParams(vmem_limit_bytes=vmem_limit),
        name="pack_owners",
    )(places, *speeds)


def unpack_kernel(n, place_ref, arrived_ref, out_ref, tile_ref):
    slots = arrived_ref.shape[1]
    lane = lax.broadcasted_iota(i32, (3, slots), 1)

    def step(i, carry):
        for u in range(16):
            cluster = i * 16 + u
            value = arrived_ref[pl.ds(place_ref[1, cluster], 3), :]
            tile_ref[cluster, :3, :] = jnp.where(lane < place_ref[2, cluster], value, 0.0)
        return carry

    lax.fori_loop(0, n // 16, step, 0)
    for k in range(3):
        out_ref[n * k : n * (k + 1), :] = tile_ref[:, k, :]


def unpack_call(places, arrived, n):
    slots = arrived.shape[1]
    return pl.pallas_call(
        functools.partial(unpack_kernel, n),
        out_shape=jax.ShapeDtypeStruct((3 * n, slots), f32),
        in_specs=[smem, vmem],
        out_specs=vmem,
        scratch_shapes=[pltpu.VMEM((n, 8, slots), f32)],
        compiler_params=pltpu.CompilerParams(vmem_limit_bytes=vmem_limit),
        name="unpack_drops",
    )(places, arrived)


def per_device(
    positions,
    normals,
    curvature,
    pair_targets,
    pair_sources,
    pair_count,
    node_counts,
    drop_clusters,
    drop_owner,
):
    n, slots = curvature.shape
    rows = lax.axis_size("row")
    cols = lax.axis_size("col")
    devices = rows * cols
    my_row = lax.axis_index("row")
    my_col = lax.axis_index("col")
    device = my_row * cols + my_col
    capacity = max(2, 2 * n // devices)
    hypercube = cols == 4
    hops = rows // 2 + 1

    def swap(value, bit):
        return lax.ppermute(value, "col", [(c, c ^ bit) for c in range(cols)])

    def component_major(value):
        return jnp.transpose(value, (1, 0, 2)).reshape(3 * n, slots)

    block, position, small = prep_call(
        (device * n).reshape(1),
        component_major(positions),
        component_major(normals),
        curvature,
        drop_clusters.T,
        node_counts.T,
        drop_owner.reshape(1, -1),
        pair_targets,
        pair_sources,
    )
    mate_block = swap(block, 1)
    if hypercube:
        across = swap(position, 2)
    to_right = [(r, (r + 1) % rows) for r in range(rows)]
    to_left = [((r + 1) % rows, r) for r in range(rows)]
    right = lax.ppermute(block, "row", to_right)
    left = lax.ppermute(block, "row", to_left)
    if hypercube:
        targets = [position, mate_block, across, swap(across, 1)]
    else:
        gathered = lax.all_gather(position, "col", axis=0, tiled=True)
        targets = [gathered[3 * n * h : 3 * n * (h + 1)] for h in range(cols)]
    listed, places = index_call(
        (n, rows, capacity, *drop_clusters.shape[::-1], pair_targets.shape[1], hypercube),
        jnp.stack([my_row, my_col, device, pair_count[0]]),
        small,
    )
    lists = [listed, swap(listed, 1)]

    total, all_targets = hop_call(n, 0, hops, lists, targets, None, [block], [mate_block], hypercube)
    for hop in range(1, hops):
        if hop + 1 < hops:
            own = [right, left]
        *own, total = lax.optimization_barrier((*own, total))
        mates = [swap(part, 1) for part in own]
        if rows == 4 and hop == 1:
            passed = jnp.where(my_row % 2 == 0, own[0], own[1])
            opposite = [lax.ppermute(passed, "row", [(0, 1), (1, 0), (2, 3), (3, 2)])]
        elif hop + 1 < hops:
            right = lax.ppermute(own[0], "row", to_right)
            left = lax.ppermute(own[1], "row", to_left)
            opposite = [right]
        total, *speed = hop_call(n, hop, hops, lists, [all_targets], total, own, mates, hypercube)
        own = opposite

    if hypercube:
        kept, sent = speed
        from_mate = swap(sent, 1)
        across = swap(kept[3 * n :] + from_mate[3 * n :], 2)
        home_speed = [kept, from_mate, across]
    else:
        home_speed = [lax.psum_scatter(speed[0], "col", scatter_dimension=0, tiled=True)]

    outgoing = pack_call(places, home_speed, n, capacity, devices)
    arrived = lax.all_to_all(outgoing, ("row", "col"), split_axis=0, concat_axis=0, tiled=True)
    result = unpack_call(places, arrived, n)
    return jnp.transpose(result.reshape(3, n, slots), (1, 0, 2))


def solution(mesh):
    in_specs = (
        P(("groups", "row", "col"), None, None),
        P(("groups", "row", "col"), None, None),
        P(("groups", "row", "col"), None),
        P(("groups", "row", "col"), None),
        P(("groups", "row", "col"), None),
        P(("groups", "row", "col")),
        P("groups", None),
        P("groups", None),
        P("groups"),
    )
    out_specs = P(("groups", "row", "col"), None, None)
    return jax.shard_map(
        per_device, mesh=mesh, in_specs=in_specs, out_specs=out_specs, check_vma=False
    )
```

```python
import functools
import math

import jax
import jax.numpy as jnp
from jax import lax
from jax.experimental import pallas as pl
from jax.experimental.pallas import tpu as pltpu
from jax.sharding import PartitionSpec as P

f32 = jnp.float32
bf16 = jnp.bfloat16
i32 = jnp.int32
regular_sq = 0.0025
length_scale = 1.0 / math.sqrt(regular_sq)
force_scale = length_scale / (8.0 * math.pi)
unroll = 8
group_levels = 3
vmem_limit = 24 * 2**20
kernel_flops = 8 * 10**9
whole_vmem = 60 * 2**20
vmem = pl.BlockSpec(memory_space=pltpu.VMEM)
smem = pl.BlockSpec(memory_space=pltpu.SMEM)
hbm = pl.BlockSpec(memory_space=pltpu.HBM)


def split3(value):
    high = value.astype(bf16)
    rest = value - high.astype(f32)
    mid = rest.astype(bf16)
    low = (rest - mid.astype(f32)).astype(bf16)
    return high.astype(f32), mid.astype(f32), low.astype(f32)


def rows16(upper, lower):
    return jnp.concatenate([upper, lower], axis=0).astype(bf16)


def transposed_left(y, f, slots):
    row = lax.broadcasted_iota(i32, (8, slots), 0)
    dot = -(y[0] * f[0] + y[1] * f[1] + y[2] * f[2])
    tile = jnp.where(row == 7, dot, 0.0)
    for k in range(3):
        tile = jnp.where(row == k, y[k], jnp.where(row == 3 + k, f[k], tile))
    high, mid, low = split3(tile)
    first = row < 3
    high_one = jnp.where(first, 1.0, high)
    left = jnp.concatenate(
        [rows16(high, mid), rows16(low, high_one), rows16(high_one, jnp.where(first, 1.0, mid))], axis=0
    )
    return left.T


def products(left, x, slots):
    row = lax.broadcasted_iota(i32, (8, slots), 0)
    zero = jnp.zeros((8, slots), f32)
    tile = jnp.where(row == 7, 1.0, zero)
    for k in range(3):
        tile = jnp.where((row == k) | (row == 3 + k), x[k], tile)
    high, mid, low = split3(tile)
    columns = []
    for k in range(3):
        mine = row == k
        minus = jnp.where(mine, -1.0, zero)
        columns.append(
            [
                rows16(minus, minus),
                rows16(minus, jnp.where(mine, high, 0.0)),
                rows16(jnp.where(mine, mid, 0.0), jnp.where(mine, low, 0.0)),
            ]
        )
    first = row < 3
    high, mid, low = [jnp.where(first, 0.0, part) for part in (high, mid, low)]
    columns.append([rows16(high, high), rows16(high, mid), rows16(low, mid)])
    for k in range(2):
        pick = jnp.where(row == 3 + k, 1.0, zero)
        columns.append([rows16(pick, pick), rows16(pick, zero), rows16(zero, zero)])
    right = jnp.concatenate([jnp.concatenate(column, axis=0) for column in columns], axis=1)
    return lax.dot_general(left, right, (((1,), (0,)), ((), ())), preferred_element_type=f32)


def node_sums(product, force_z, slots):
    row = lax.broadcasted_iota(i32, (8, slots), 0)
    total = None
    for g in range(product.shape[0] // 8):
        part = product[8 * g : 8 * g + 8]
        wx, wy, wz, dot, fx, fy = [part[:, slots * k : slots * (k + 1)] for k in range(6)]
        fz = force_z[8 * g : 8 * g + 8]
        inverse = lax.rsqrt(wx * wx + wy * wy + (wz * wz + 1.0))
        cube = inverse * inverse * inverse
        isotropic = inverse + cube
        project = dot * cube
        terms = (isotropic * fx + project * wx, isotropic * fy + project * wy, isotropic * fz + project * wz)
        total = terms if total is None else tuple(a + b for a, b in zip(total, terms))
    sums = [jnp.broadcast_to(jnp.sum(part, axis=0, keepdims=True), (8, slots)) for part in total]
    return jnp.where(row == 0, sums[0], jnp.where(row == 1, sums[1], jnp.where(row == 2, sums[2], 0.0)))


def hop_kernel(spec, list_ref, mate_list_ref, *refs):
    n, slots, hop, homes, own, mate, first, last, split = spec
    refs = list(refs)
    if first:
        target_refs = [refs.pop(0) for _ in range(homes)]
    else:
        target_ref, before_ref = refs.pop(0), refs.pop(0)
    own_refs = [refs.pop(0) for _ in range(own)]
    mate_refs = [refs.pop(0) for _ in range(mate)]
    if first:
        total_ref, token_ref, target_ref = refs.pop(0), refs.pop(0), refs.pop(0)
    else:
        total_ref, token_ref = refs.pop(0), refs.pop(0)
        out_refs = [refs.pop(0) for _ in range((2 if split else 1) if last else 0)]
    source_ref, left_ref = refs
    token_ref[...] = jnp.zeros_like(token_ref)
    clusters = homes * n
    shift = n.bit_length() - 1
    if first:
        for h in range(homes):
            target_ref[3 * n * h : 3 * n * (h + 1), :] = target_refs[h][: 3 * n, :]
        total_ref[...] = jnp.zeros_like(total_ref)
    for place, block in list(enumerate(own_refs)) + [(2 + b, block) for b, block in enumerate(mate_refs)]:
        source_ref[6 * n * place : 6 * n * (place + 1), :] = block[...]

    bound_row = list_ref.shape[0] - 1
    own_start, own_count, mate_start, mate_count = 0, 0, 0, 0
    if own:
        own_start = list_ref[bound_row, hop]
        own_count = (list_ref[bound_row, hop + 1] - own_start + 1) >> 1
    if mate:
        begin = mate_list_ref[bound_row, hop]
        end = mate_list_ref[bound_row, hop + 1]
        mate_count = (end - begin) >> 1
        mate_start = begin + 1
    count = own_count + mate_count
    mate_start = mate_start - 2 * own_count

    def entry(index):
        live = index < count
        mine = index < own_count
        place = jnp.where(live, 2 * index + jnp.where(mine, own_start, mate_start), 0)
        row, lane = place >> 7, place & 127
        flip = jnp.where(mine, 0, n if split else 0)
        packed = jnp.where(mine, list_ref[row, lane], mate_list_ref[row, lane])
        packed = jnp.where(live, packed, 0)
        source = (packed >> 12) & 0xFF
        source = jnp.where(mine, source, source + 2 * n)
        return live, (packed & 0xFFF) ^ flip, jnp.where(live, source, 0), packed >> 20

    def source_rows(source):
        base = source + (source >> shift) * (5 * n)
        return [source_ref[pl.ds(base + n * k, 1), :] for k in range(6)]

    def wide(value):
        return jnp.broadcast_to(value, (8, slots))

    def fetch(index, u):
        _, _, source, _ = entry(index)
        values = [wide(value) for value in source_rows(source)]
        left_ref[u] = transposed_left(values[:3], values[3:], slots)

    @pl.when(count > 0)
    def _():
        for u in range(unroll):
            fetch(u, u)

    def batch(i, entries, groups):
        results = []
        lefts = [left_ref[u, : 8 * groups] for u in range(unroll)]
        for u in range(unroll):
            live, target, source, _ = entries[u]
            base = target + (target >> shift) * (2 * n)
            x = [wide(target_ref[pl.ds(base + n * k, 1), :]) for k in range(3)]
            product = products(lefts[u], x, slots)
            force_z = source_ref[pl.ds(source + (source >> shift) * (5 * n) + 5 * n, 1), :]
            force_z = jnp.broadcast_to(force_z, (slots, slots)).T
            results.append((jnp.where(live, target, clusters), node_sums(product, force_z, slots)))
        for u in range(unroll):
            fetch((i + 1) * unroll + u, u)
        for target, result in results:
            total_ref[pl.ds(pl.multiple_of(target * 8, 8), 8), :] += result

    def step(i, carry):
        entries = [entry(i * unroll + u) for u in range(unroll)]
        level = entries[0][3]
        for one in entries[1:]:
            level = jnp.maximum(level, one[3])
        for k in range(group_levels):
            groups = slots // 8 * (k + 2) // (group_levels + 1)
            pl.when(level == k)(functools.partial(batch, i, entries, groups))
        return carry

    lax.fori_loop(0, (count + unroll - 1) // unroll, step, 0)
    if last:
        for h in range(homes):
            out_ref = out_refs[h % 2] if split else out_refs[0]
            first_row = 3 * n * (h // 2 if split else h)

            def move(i, carry, h=h, out_ref=out_ref, first_row=first_row):
                for u in range(8):
                    tile = total_ref[pl.ds(pl.multiple_of((n * h + i * 8 + u) * 8, 8), 8), :]
                    out_ref[pl.ds(first_row + i * 24 + 3 * u, 3), :] = tile[:3]
                return carry

            lax.fori_loop(0, n // 8, move, 0)


def hop_call(n, hop, hops, lists, targets, total, own, mate, split):
    first, last = hop == 0, hop == hops - 1
    slots = own[0].shape[1]
    homes = len(targets) if first else targets[0].shape[0] // (3 * n)
    total_shape = jax.ShapeDtypeStruct((homes * n * 8 + 8, slots), f32)
    aliases = {}
    operands = [*lists, *targets]
    if not first:
        operands.append(total)
    out_shape = [total_shape, jax.ShapeDtypeStruct((8, 128), f32)]
    if first:
        out_shape += [jax.ShapeDtypeStruct((homes * 3 * n, slots), f32)]
    elif last:
        parts = 2 if split else 1
        out_shape += [jax.ShapeDtypeStruct((homes * 3 * n // parts, slots), f32)] * parts
    if not first:
        aliases = {len(operands) - 1: 0}
    operands += [*own, *mate]
    spec = (n, slots, hop, homes, len(own), len(mate), first, last, split)
    return pl.pallas_call(
        functools.partial(hop_kernel, spec),
        out_shape=out_shape,
        in_specs=[smem, smem] + [vmem] * (len(operands) - 2),
        out_specs=[vmem] * len(out_shape),
        scratch_shapes=[
            pltpu.VMEM((4 * 6 * n, slots), f32),
            pltpu.VMEM((unroll, slots, 48), bf16),
        ],
        input_output_aliases=aliases,
        compiler_params=pltpu.CompilerParams(vmem_limit_bytes=vmem_limit),
        cost_estimate=pl.CostEstimate(flops=kernel_flops if hop else kernel_flops // 8, bytes_accessed=10**6, transcendentals=10**6),
        name=f"pairs_hop{hop}",
    )(*operands)


def column(row, rows):
    return jnp.broadcast_to(row, (rows, 128)).T


def prep_kernel(n, base_ref, *refs):
    ins, (out_ref, own_ref, small_ref), held, sems = refs[:8], refs[8:11], refs[11:19], refs[19]
    copies = [pltpu.make_async_copy(a, b, sems.at[k]) for k, (a, b) in enumerate(zip(ins, held))]
    for copy in copies:
        copy.start()
    for copy in copies:
        copy.wait()
    position_ref, normal_ref, curvature_ref, cluster_ref, count_ref, owner_ref, target_ref, source_ref = held
    slots = position_ref.shape[1]
    scaled = position_ref[...] * length_scale
    out_ref[: 3 * n, :] = scaled
    own_ref[...] = scaled
    mine = base_ref[0] + lax.broadcasted_iota(i32, (n, 128), 0)
    total = jnp.zeros((n, 128), f32)
    for k in range(cluster_ref.shape[0]):
        for j in range(cluster_ref.shape[1] // 128):
            part = slice(128 * j, 128 * (j + 1))
            cluster = jnp.broadcast_to(cluster_ref[k : k + 1, part], (n, 128))
            count = jnp.broadcast_to(count_ref[k : k + 1, part].astype(f32), (n, 128))
            total = total + jnp.where(cluster == mine, count, 0.0)
    live_count = jnp.sum(total, axis=1, keepdims=True)
    lane = lax.broadcasted_iota(i32, (n, slots), 1).astype(f32)
    strength = jnp.where(lane < live_count, curvature_ref[...] * force_scale, 0.0)
    for k in range(3):
        out_ref[n * (3 + k) : n * (4 + k), :] = normal_ref[n * k : n * (k + 1), :] * strength
    per_drop, drops = cluster_ref.shape
    pairs = target_ref.shape[1]
    small_ref[:per_drop, :drops] = cluster_ref[...] + (count_ref[...] << 14)
    small_ref[per_drop : per_drop + 1, :drops] = owner_ref[...]
    small_ref[per_drop + 1 : per_drop + 2, :pairs] = target_ref[...]
    small_ref[per_drop + 2 : per_drop + 3, :pairs] = source_ref[...]


def prep_call(base, *operands):
    n, slots = operands[2].shape
    per_drop, drops = operands[3].shape
    small = (per_drop + 8, max(drops, operands[6].shape[1]))
    shapes = [((6 * n, slots), f32), ((3 * n, slots), f32), (small, i32)]
    return pl.pallas_call(
        functools.partial(prep_kernel, n),
        out_shape=[jax.ShapeDtypeStruct(*shape) for shape in shapes],
        in_specs=[smem] + [hbm] * 8,
        out_specs=[vmem] * 3,
        scratch_shapes=[pltpu.VMEM(x.shape, x.dtype) for x in operands] + [pltpu.SemaphoreType.DMA((8,))],
        compiler_params=pltpu.CompilerParams(vmem_limit_bytes=whole_vmem),
        name="prep_sources",
    )(base, *operands)


def index_kernel(spec, facts_ref, *refs):
    n, rows, cols, capacity, per_drop, drops, pair_slots, split = spec
    small_ref, list_ref, place_ref = refs
    my_row, my_col, device, live_pairs = [facts_ref[k] for k in range(4)]
    shift = n.bit_length() - 1
    wide = (128, 128)
    lane_row = lax.broadcasted_iota(i32, (1, 128), 1)
    sub = lax.broadcasted_iota(i32, wide, 0)
    lane = lax.broadcasted_iota(i32, wide, 1)

    blocks = pair_slots // 128
    wide_source = []
    for b in range(blocks):
        source = small_ref[per_drop + 2 : per_drop + 3, 128 * b : 128 * (b + 1)]
        cluster = ((source >> shift) * cols + my_col) * n + (source & (n - 1))
        wide_source.append(jnp.broadcast_to(cluster, wide))

    def look_up(j, counts):
        part = pl.ds(pl.multiple_of(j * 128, 128), 128)
        for k in range(per_drop):
            fact = column(small_ref[k : k + 1, part], 128)
            cluster, count = fact & 16383, (fact >> 14).astype(f32)
            counts = [c + jnp.where(cluster == w, count, 0.0) for c, w in zip(counts, wide_source)]
        return counts

    counts = lax.fori_loop(0, drops // 128, look_up, [jnp.zeros(wide, f32)] * blocks)
    keys, packs = [], []
    for b in range(blocks):
        target = small_ref[per_drop + 1 : per_drop + 2, 128 * b : 128 * (b + 1)]
        source = small_ref[per_drop + 2 : per_drop + 3, 128 * b : 128 * (b + 1)]
        ahead = ((source >> shift) - my_row) & (rows - 1)
        hop = jnp.minimum(ahead, rows - ahead)
        index = lane_row + 128 * b
        key = jnp.where(index < live_pairs, hop, rows)
        count = jnp.sum(counts[b], axis=0, keepdims=True)
        level = jnp.zeros((1, 128), i32)
        for k in range(group_levels - 1):
            level = level + jnp.where(count > n * (k + 2) / (group_levels + 1), 1, 0)
        keys.append((key * group_levels + group_levels - 1 - level) * (128 * blocks) + index)
        home = target >> shift
        if split:
            home = home ^ my_col
        side = jnp.where((ahead > 0) & (ahead * 2 < rows), n, 0)
        packs.append((home * n + (target & (n - 1)) + (side + (source & (n - 1))) * 4096 + (level << 20)).astype(f32))
    key_columns = [column(key, 128) for key in keys]
    order_columns = []
    for b in range(blocks):
        before = jnp.zeros(wide, f32)
        for c in range(blocks):
            before = before + jnp.where(key_columns[c] < jnp.broadcast_to(keys[b], wide), 1.0, 0.0)
        order_columns.append(column(jnp.sum(before, axis=0, keepdims=True), 128))
    pack_columns = [column(pack, 128) for pack in packs]
    lanes = lane.astype(f32)
    for b in range(blocks):
        ordered = jnp.zeros(wide, f32)
        for c in range(blocks):
            ordered = ordered + jnp.where(order_columns[c] == lanes + 128.0 * b, pack_columns[c], 0.0)
        list_ref[b : b + 1, :] = jnp.sum(ordered, axis=0, keepdims=True).astype(i32)
    below = jnp.zeros(wide, f32)
    for c in range(blocks):
        below = below + jnp.where(key_columns[c] < lane * (128 * blocks * group_levels), 1.0, 0.0)
    list_ref[blocks : blocks + 1, :] = jnp.sum(below, axis=0, keepdims=True).astype(i32)

    mine = device * n + sub

    def scan(j, carry):
        owner_sum, chosen, owned_before = carry
        part = pl.ds(pl.multiple_of(j * 128, 128), 128)
        owner = small_ref[per_drop : per_drop + 1, part]
        is_mine = jnp.where(owner == device, 1.0, 0.0)
        mine_column = column(is_mine, 128)
        rank = jnp.sum(jnp.where(sub < lane, mine_column, 0.0), axis=0, keepdims=True) + owned_before
        slot = jnp.where(owner == device, rank, -1.0)
        picked = column(slot, 128) == (lane // per_drop).astype(f32)
        for k in range(per_drop):
            fact = small_ref[k : k + 1, part]
            cluster = fact & 16383
            chosen = chosen + jnp.where(picked & (lane % per_drop == k), column(fact.astype(f32), 128), 0.0)
            wide_owner = jnp.broadcast_to(owner.astype(f32), wide)
            owner_sum = owner_sum + jnp.where(jnp.broadcast_to(cluster, wide) == mine, wide_owner, 0.0)
        return owner_sum, chosen, owned_before + jnp.sum(is_mine, axis=1, keepdims=True)

    start = (jnp.zeros(wide, f32), jnp.zeros(wide, f32), jnp.zeros((1, 1), f32))
    owner_sum, chosen, _ = lax.fori_loop(0, drops // 128, scan, start)
    home_owner = jnp.broadcast_to(jnp.sum(owner_sum, axis=1, keepdims=True), wide)
    owner_lanes = home_owner.T
    rank = jnp.sum(jnp.where((home_owner == owner_lanes) & (sub < lane), 1.0, 0.0), axis=0, keepdims=True)
    place_ref[0:1, :] = ((owner_lanes[0:1] * capacity + rank) * 3.0).astype(i32)
    fact = jnp.sum(chosen, axis=0, keepdims=True).astype(i32)
    cluster = fact & 16383
    anchor = cluster >> shift
    cluster_column = column(cluster, 128)
    cluster_wide = jnp.broadcast_to(cluster, wide)
    same = (cluster_column >> shift) == (cluster_wide >> shift)
    rank = jnp.sum(jnp.where(same & (cluster_column < cluster_wide), 1.0, 0.0), axis=0, keepdims=True)
    place_ref[1:2, :] = (anchor * capacity + rank.astype(i32)) * 3
    place_ref[2:3, :] = fact >> 14


def index_call(spec, facts, small):
    return pl.pallas_call(
        functools.partial(index_kernel, spec),
        out_shape=[jax.ShapeDtypeStruct((spec[6] // 128 + 1, 128), i32), jax.ShapeDtypeStruct((3, 128), i32)],
        in_specs=[smem, vmem],
        out_specs=[vmem, vmem],
        compiler_params=pltpu.CompilerParams(vmem_limit_bytes=vmem_limit),
        name="index_work",
    )(facts, small)


def pack_kernel(n, place_ref, *refs):
    *speed_refs, out_ref, speed_ref = refs
    total = speed_refs[0][: 3 * n, :]
    for part in speed_refs[1:]:
        total = total + part[: 3 * n, :]
    speed_ref[...] = total
    out_ref[...] = jnp.zeros_like(out_ref)

    def step(i, carry):
        for u in range(16):
            cluster = i * 16 + u
            out_ref[pl.ds(place_ref[0, cluster], 3), :] = speed_ref[pl.ds(3 * cluster, 3), :]
        return carry

    lax.fori_loop(0, n // 16, step, 0)


def pack_call(places, speeds, n, capacity, devices):
    slots = speeds[0].shape[1]
    return pl.pallas_call(
        functools.partial(pack_kernel, n),
        out_shape=jax.ShapeDtypeStruct((devices * capacity * 3, slots), f32),
        in_specs=[smem] + [vmem] * len(speeds),
        out_specs=vmem,
        scratch_shapes=[pltpu.VMEM((3 * n, slots), f32)],
        compiler_params=pltpu.CompilerParams(vmem_limit_bytes=vmem_limit),
        name="pack_owners",
    )(places, *speeds)


def unpack_kernel(n, place_ref, arrived_ref, out_ref, tile_ref):
    slots = arrived_ref.shape[1]
    lane = lax.broadcasted_iota(i32, (3, slots), 1)

    def step(i, carry):
        for u in range(16):
            cluster = i * 16 + u
            value = arrived_ref[pl.ds(place_ref[1, cluster], 3), :]
            tile_ref[cluster, :3, :] = jnp.where(lane < place_ref[2, cluster], value, 0.0)
        return carry

    lax.fori_loop(0, n // 16, step, 0)
    for k in range(3):
        out_ref[n * k : n * (k + 1), :] = tile_ref[:, k, :]


def unpack_call(places, arrived, n):
    slots = arrived.shape[1]
    return pl.pallas_call(
        functools.partial(unpack_kernel, n),
        out_shape=jax.ShapeDtypeStruct((3 * n, slots), f32),
        in_specs=[smem, vmem],
        out_specs=vmem,
        scratch_shapes=[pltpu.VMEM((n, 8, slots), f32)],
        compiler_params=pltpu.CompilerParams(vmem_limit_bytes=vmem_limit),
        name="unpack_drops",
    )(places, arrived)


def per_device(
    positions,
    normals,
    curvature,
    pair_targets,
    pair_sources,
    pair_count,
    node_counts,
    drop_clusters,
    drop_owner,
):
    n, slots = curvature.shape
    rows = lax.axis_size("row")
    cols = lax.axis_size("col")
    devices = rows * cols
    my_row = lax.axis_index("row")
    my_col = lax.axis_index("col")
    device = my_row * cols + my_col
    capacity = max(2, 2 * n // devices)
    hypercube = cols == 4
    hops = rows // 2 + 1

    def swap(value, bit):
        return lax.ppermute(value, "col", [(c, c ^ bit) for c in range(cols)])

    def component_major(value):
        return jnp.transpose(value, (1, 0, 2)).reshape(3 * n, slots)

    block, position, small = prep_call(
        (device * n).reshape(1),
        component_major(positions),
        component_major(normals),
        curvature,
        drop_clusters.T,
        node_counts.T,
        drop_owner.reshape(1, -1),
        pair_targets,
        pair_sources,
    )
    mate_block = swap(block, 1)
    if hypercube:
        across = swap(position, 2)
    to_right = [(r, (r + 1) % rows) for r in range(rows)]
    to_left = [((r + 1) % rows, r) for r in range(rows)]
    right = lax.ppermute(block, "row", to_right)
    left = lax.ppermute(block, "row", to_left)
    if hypercube:
        targets = [block, mate_block, across, swap(across, 1)]
    else:
        gathered = lax.all_gather(position, "col", axis=0, tiled=True)
        targets = [gathered[3 * n * h : 3 * n * (h + 1)] for h in range(cols)]
    listed, places = index_call(
        (n, rows, cols, capacity, *drop_clusters.shape[::-1], pair_targets.shape[1], hypercube),
        jnp.stack([my_row, my_col, device, pair_count[0]]),
        small,
    )
    lists = [listed, swap(listed, 1)]

    total, token, all_targets = hop_call(n, 0, hops, lists, targets, None, [block], [mate_block], hypercube)
    for hop in range(1, hops):
        if hop + 1 < hops:
            own = [right, left]
        *own, token = lax.optimization_barrier((*own, token))
        mates = [swap(part, 1) for part in own]
        if rows == 4 and hop == 1:
            passed = jnp.where(my_row % 2 == 0, own[0], own[1])
            opposite = [lax.ppermute(passed, "row", [(0, 1), (1, 0), (2, 3), (3, 2)])]
        elif hop + 1 < hops:
            right = lax.ppermute(own[0], "row", to_right)
            left = lax.ppermute(own[1], "row", to_left)
            opposite = [right]
        total, token, *speed = hop_call(n, hop, hops, lists, [all_targets], total, own, mates, hypercube)
        own = opposite

    if hypercube:
        kept, sent = speed
        from_mate = swap(sent, 1)
        across = swap(kept[3 * n :] + from_mate[3 * n :], 2)
        home_speed = [kept, from_mate, across]
    else:
        home_speed = [lax.psum_scatter(speed[0], "col", scatter_dimension=0, tiled=True)]

    outgoing = pack_call(places, home_speed, n, capacity, devices)
    arrived = lax.all_to_all(outgoing, ("row", "col"), split_axis=0, concat_axis=0, tiled=True)
    result = unpack_call(places, arrived, n)
    return jnp.transpose(result.reshape(3, n, slots), (1, 0, 2))


def solution(mesh):
    in_specs = (
        P(("groups", "row", "col"), None, None),
        P(("groups", "row", "col"), None, None),
        P(("groups", "row", "col"), None),
        P(("groups", "row", "col"), None),
        P(("groups", "row", "col"), None),
        P(("groups", "row", "col")),
        P("groups", None),
        P("groups", None),
        P("groups"),
    )
    out_specs = P(("groups", "row", "col"), None, None)
    return jax.shard_map(
        per_device, mesh=mesh, in_specs=in_specs, out_specs=out_specs, check_vma=False
    )
```

```python
import functools
import math

import jax
import jax.numpy as jnp
from jax import lax
from jax.experimental import pallas as pl
from jax.experimental.pallas import tpu as pltpu
from jax.sharding import PartitionSpec as P

f32 = jnp.float32
bf16 = jnp.bfloat16
i32 = jnp.int32
regular_sq = 0.0025
length_scale = 1.0 / math.sqrt(regular_sq)
force_scale = length_scale / (8.0 * math.pi)
unroll = 8
vmem_limit = 24 * 2**20
kernel_flops = 8 * 10**9
whole_vmem = 60 * 2**20
vmem = pl.BlockSpec(memory_space=pltpu.VMEM)
smem = pl.BlockSpec(memory_space=pltpu.SMEM)
hbm = pl.BlockSpec(memory_space=pltpu.HBM)


def split3(value):
    high = value.astype(bf16)
    rest = value - high.astype(f32)
    mid = rest.astype(bf16)
    low = (rest - mid.astype(f32)).astype(bf16)
    return high.astype(f32), mid.astype(f32), low.astype(f32)


def rows16(upper, lower):
    return jnp.concatenate([upper, lower], axis=0).astype(bf16)


def transposed_left(y, f, slots):
    row = lax.broadcasted_iota(i32, (8, slots), 0)
    dot = -(y[0] * f[0] + y[1] * f[1] + y[2] * f[2])
    tile = jnp.where(row == 7, dot, 0.0)
    for k in range(3):
        tile = jnp.where(row == k, y[k], jnp.where(row == 3 + k, f[k], tile))
    high, mid, low = split3(tile)
    first = row < 3
    high_one = jnp.where(first, 1.0, high)
    left = jnp.concatenate(
        [rows16(high, mid), rows16(low, high_one), rows16(high_one, jnp.where(first, 1.0, mid))], axis=0
    )
    return left.T


def products(left, x, slots):
    row = lax.broadcasted_iota(i32, (8, slots), 0)
    zero = jnp.zeros((8, slots), f32)
    tile = jnp.where(row == 7, 1.0, zero)
    for k in range(3):
        tile = jnp.where((row == k) | (row == 3 + k), x[k], tile)
    high, mid, low = split3(tile)
    columns = []
    for k in range(3):
        mine = row == k
        minus = jnp.where(mine, -1.0, zero)
        columns.append(
            [
                rows16(minus, minus),
                rows16(minus, jnp.where(mine, high, 0.0)),
                rows16(jnp.where(mine, mid, 0.0), jnp.where(mine, low, 0.0)),
            ]
        )
    first = row < 3
    high, mid, low = [jnp.where(first, 0.0, part) for part in (high, mid, low)]
    columns.append([rows16(high, high), rows16(high, mid), rows16(low, mid)])
    for k in range(2):
        pick = jnp.where(row == 3 + k, 1.0, zero)
        columns.append([rows16(pick, pick), rows16(pick, zero), rows16(zero, zero)])
    right = jnp.concatenate([jnp.concatenate(column, axis=0) for column in columns], axis=1)
    return lax.dot_general(left, right, (((1,), (0,)), ((), ())), preferred_element_type=f32)


def node_sums(product, force_z, slots):
    row = lax.broadcasted_iota(i32, (8, slots), 0)
    total = None
    for g in range(slots // 8):
        part = product[8 * g : 8 * g + 8]
        wx, wy, wz, dot, fx, fy = [part[:, slots * k : slots * (k + 1)] for k in range(6)]
        fz = force_z[8 * g : 8 * g + 8]
        inverse = lax.rsqrt(wx * wx + wy * wy + (wz * wz + 1.0))
        cube = inverse * inverse * inverse
        isotropic = inverse + cube
        project = dot * cube
        terms = (isotropic * fx + project * wx, isotropic * fy + project * wy, isotropic * fz + project * wz)
        total = terms if total is None else tuple(a + b for a, b in zip(total, terms))
    sums = [jnp.broadcast_to(jnp.sum(part, axis=0, keepdims=True), (8, slots)) for part in total]
    return jnp.where(row == 0, sums[0], jnp.where(row == 1, sums[1], jnp.where(row == 2, sums[2], 0.0)))


def hop_kernel(spec, list_ref, mate_list_ref, *refs):
    n, slots, hop, homes, own, mate, first, last, split = spec
    refs = list(refs)
    if first:
        target_refs = [refs.pop(0) for _ in range(homes)]
    else:
        target_ref, _, _ = refs.pop(0), refs.pop(0), refs.pop(0)
    own_refs = [refs.pop(0) for _ in range(own)]
    mate_refs = [refs.pop(0) for _ in range(mate)]
    if first:
        total_ref, token_ref, target_ref = refs.pop(0), refs.pop(0), refs.pop(0)
    else:
        total_ref, token_ref = refs.pop(0), refs.pop(0)
        out_refs = [refs.pop(0) for _ in range((2 if split else 1) if last else 0)]
    source_ref, left_ref = refs
    token_ref[...] = jnp.zeros_like(token_ref)
    clusters = homes * n
    shift = n.bit_length() - 1
    if first:
        for h in range(homes):
            target_ref[3 * n * h : 3 * n * (h + 1), :] = target_refs[h][: 3 * n, :]
        total_ref[...] = jnp.zeros_like(total_ref)
    for place, block in list(enumerate(own_refs)) + [(2 + b, block) for b, block in enumerate(mate_refs)]:
        source_ref[6 * n * place : 6 * n * (place + 1), :] = block[...]

    bound_row = list_ref.shape[0] - 1
    own_start, own_count, mate_start, mate_count = 0, 0, 0, 0
    if own:
        own_start = list_ref[bound_row, hop]
        own_count = (list_ref[bound_row, hop + 1] - own_start + 1) >> 1
    if mate:
        begin = mate_list_ref[bound_row, hop]
        end = mate_list_ref[bound_row, hop + 1]
        mate_start = begin + ((end - begin + 1) >> 1)
        mate_count = end - mate_start
    count = own_count + mate_count
    mate_start = mate_start - own_count

    def entry(index):
        live = index < count
        mine = index < own_count
        place = jnp.where(live, index + jnp.where(mine, own_start, mate_start), 0)
        row, lane = place >> 7, place & 127
        target, source = 0, 0
        if own:
            packed = list_ref[row, lane]
            target, source = packed & 0xFFF, packed >> 12
        if mate:
            packed = mate_list_ref[row, lane]
            flip = n if split else 0
            mate_target, mate_source = (packed & 0xFFF) ^ flip, (packed >> 12) + 2 * n
            target = jnp.where(mine, target, mate_target)
            source = jnp.where(mine, source, mate_source)
        return live, jnp.where(live, target, 0), jnp.where(live, source, 0)

    def source_rows(source):
        base = source + (source >> shift) * (5 * n)
        return [source_ref[pl.ds(base + n * k, 1), :] for k in range(6)]

    def wide(value):
        return jnp.broadcast_to(value, (8, slots))

    def fetch(index, u):
        _, _, source = entry(index)
        values = [wide(value) for value in source_rows(source)]
        left_ref[u] = transposed_left(values[:3], values[3:], slots)

    @pl.when(count > 0)
    def _():
        for u in range(unroll):
            fetch(u, u)

    def step(i, carry):
        results = []
        lefts = [left_ref[u] for u in range(unroll)]
        for u in range(unroll):
            live, target, source = entry(i * unroll + u)
            base = target + (target >> shift) * (2 * n)
            x = [wide(target_ref[pl.ds(base + n * k, 1), :]) for k in range(3)]
            product = products(lefts[u], x, slots)
            force_z = source_ref[pl.ds(source + (source >> shift) * (5 * n) + 5 * n, 1), :]
            force_z = jnp.broadcast_to(force_z, (slots, slots)).T
            results.append((jnp.where(live, target, clusters), node_sums(product, force_z, slots)))
        for u in range(unroll):
            fetch((i + 1) * unroll + u, u)
        for target, result in results:
            total_ref[pl.ds(pl.multiple_of(target * 8, 8), 8), :] += result
        return carry

    lax.fori_loop(0, (count + unroll - 1) // unroll, step, 0)
    if last:
        for h in range(homes):
            out_ref = out_refs[h % 2] if split else out_refs[0]
            first_row = 3 * n * (h // 2 if split else h)

            def move(i, carry, h=h, out_ref=out_ref, first_row=first_row):
                for u in range(8):
                    tile = total_ref[pl.ds(pl.multiple_of((n * h + i * 8 + u) * 8, 8), 8), :]
                    out_ref[pl.ds(first_row + i * 24 + 3 * u, 3), :] = tile[:3]
                return carry

            lax.fori_loop(0, n // 8, move, 0)


def hop_call(n, hop, hops, lists, targets, token, total, own, mate, split):
    first, last = hop == 0, hop == hops - 1
    slots = own[0].shape[1]
    homes = len(targets) if first else targets[0].shape[0] // (3 * n)
    total_shape = jax.ShapeDtypeStruct((homes * n * 8 + 8, slots), f32)
    aliases = {}
    operands = [*lists, *targets]
    if not first:
        operands += [token, total]
    out_shape = [total_shape, jax.ShapeDtypeStruct((8, 128), f32)]
    if first:
        out_shape += [jax.ShapeDtypeStruct((homes * 3 * n, slots), f32)]
    elif last:
        parts = 2 if split else 1
        out_shape += [jax.ShapeDtypeStruct((homes * 3 * n // parts, slots), f32)] * parts
    if not first:
        aliases = {len(operands) - 1: 0}
    operands += [*own, *mate]
    spec = (n, slots, hop, homes, len(own), len(mate), first, last, split)
    return pl.pallas_call(
        functools.partial(hop_kernel, spec),
        out_shape=out_shape,
        in_specs=[smem, smem] + [vmem] * (len(operands) - 2),
        out_specs=[vmem] * len(out_shape),
        scratch_shapes=[
            pltpu.VMEM((4 * 6 * n, slots), f32),
            pltpu.VMEM((unroll, slots, 48), bf16),
        ],
        input_output_aliases=aliases,
        compiler_params=pltpu.CompilerParams(vmem_limit_bytes=vmem_limit),
        cost_estimate=pl.CostEstimate(flops=kernel_flops if hop else kernel_flops // 8, bytes_accessed=10**6, transcendentals=10**6),
        name=f"pairs_hop{hop}",
    )(*operands)


def column(row, rows):
    return jnp.broadcast_to(row, (rows, 128)).T


def prep_kernel(n, base_ref, *refs):
    ins, (out_ref, own_ref, small_ref), held, sems = refs[:8], refs[8:11], refs[11:19], refs[19]
    copies = [pltpu.make_async_copy(a, b, sems.at[k]) for k, (a, b) in enumerate(zip(ins, held))]
    for copy in copies:
        copy.start()
    for copy in copies:
        copy.wait()
    position_ref, normal_ref, curvature_ref, cluster_ref, count_ref, owner_ref, target_ref, source_ref = held
    slots = position_ref.shape[1]
    scaled = position_ref[...] * length_scale
    out_ref[: 3 * n, :] = scaled
    own_ref[...] = scaled
    mine = base_ref[0] + lax.broadcasted_iota(i32, (n, 128), 0)
    total = jnp.zeros((n, 128), f32)
    for k in range(cluster_ref.shape[0]):
        for j in range(cluster_ref.shape[1] // 128):
            part = slice(128 * j, 128 * (j + 1))
            cluster = jnp.broadcast_to(cluster_ref[k : k + 1, part], (n, 128))
            count = jnp.broadcast_to(count_ref[k : k + 1, part].astype(f32), (n, 128))
            total = total + jnp.where(cluster == mine, count, 0.0)
    live_count = jnp.sum(total, axis=1, keepdims=True)
    lane = lax.broadcasted_iota(i32, (n, slots), 1).astype(f32)
    strength = jnp.where(lane < live_count, curvature_ref[...] * force_scale, 0.0)
    for k in range(3):
        out_ref[n * (3 + k) : n * (4 + k), :] = normal_ref[n * k : n * (k + 1), :] * strength
    per_drop, drops = cluster_ref.shape
    pairs = target_ref.shape[1]
    small_ref[:per_drop, :drops] = cluster_ref[...] + (count_ref[...] << 14)
    small_ref[per_drop : per_drop + 1, :drops] = owner_ref[...]
    small_ref[per_drop + 1 : per_drop + 2, :pairs] = target_ref[...]
    small_ref[per_drop + 2 : per_drop + 3, :pairs] = source_ref[...]


def prep_call(base, *operands):
    n, slots = operands[2].shape
    per_drop, drops = operands[3].shape
    small = (per_drop + 8, max(drops, operands[6].shape[1]))
    shapes = [((6 * n, slots), f32), ((3 * n, slots), f32), (small, i32)]
    return pl.pallas_call(
        functools.partial(prep_kernel, n),
        out_shape=[jax.ShapeDtypeStruct(*shape) for shape in shapes],
        in_specs=[smem] + [hbm] * 8,
        out_specs=[vmem] * 3,
        scratch_shapes=[pltpu.VMEM(x.shape, x.dtype) for x in operands] + [pltpu.SemaphoreType.DMA((8,))],
        compiler_params=pltpu.CompilerParams(vmem_limit_bytes=whole_vmem),
        name="prep_sources",
    )(base, *operands)


def index_kernel(spec, facts_ref, *refs):
    n, rows, capacity, per_drop, drops, pair_slots, split = spec
    small_ref, list_ref, place_ref = refs
    my_row, my_col, device, live_pairs = [facts_ref[k] for k in range(4)]
    shift = n.bit_length() - 1
    wide = (128, 128)
    lane_row = lax.broadcasted_iota(i32, (1, 128), 1)
    sub = lax.broadcasted_iota(i32, wide, 0)
    lane = lax.broadcasted_iota(i32, wide, 1)

    blocks = pair_slots // 128
    keys, packs = [], []
    for b in range(blocks):
        target = small_ref[per_drop + 1 : per_drop + 2, 128 * b : 128 * (b + 1)]
        source = small_ref[per_drop + 2 : per_drop + 3, 128 * b : 128 * (b + 1)]
        ahead = ((source >> shift) - my_row) & (rows - 1)
        hop = jnp.minimum(ahead, rows - ahead)
        index = lane_row + 128 * b
        key = jnp.where(index < live_pairs, hop, rows)
        keys.append(key * (128 * blocks) + index)
        home = target >> shift
        if split:
            home = home ^ my_col
        side = jnp.where((ahead > 0) & (ahead * 2 < rows), n, 0)
        packs.append((home * n + (target & (n - 1)) + (side + (source & (n - 1))) * 4096).astype(f32))
    key_columns = [column(key, 128) for key in keys]
    order_columns = []
    for b in range(blocks):
        before = jnp.zeros(wide, f32)
        for c in range(blocks):
            before = before + jnp.where(key_columns[c] < jnp.broadcast_to(keys[b], wide), 1.0, 0.0)
        order_columns.append(column(jnp.sum(before, axis=0, keepdims=True), 128))
    pack_columns = [column(pack, 128) for pack in packs]
    lanes = lane.astype(f32)
    for b in range(blocks):
        ordered = jnp.zeros(wide, f32)
        for c in range(blocks):
            ordered = ordered + jnp.where(order_columns[c] == lanes + 128.0 * b, pack_columns[c], 0.0)
        list_ref[b : b + 1, :] = jnp.sum(ordered, axis=0, keepdims=True).astype(i32)
    below = jnp.zeros(wide, f32)
    for c in range(blocks):
        below = below + jnp.where(key_columns[c] < lane * (128 * blocks), 1.0, 0.0)
    list_ref[blocks : blocks + 1, :] = jnp.sum(below, axis=0, keepdims=True).astype(i32)

    mine = device * n + sub

    def scan(j, carry):
        owner_sum, chosen, owned_before = carry
        part = pl.ds(pl.multiple_of(j * 128, 128), 128)
        owner = small_ref[per_drop : per_drop + 1, part]
        is_mine = jnp.where(owner == device, 1.0, 0.0)
        mine_column = column(is_mine, 128)
        rank = jnp.sum(jnp.where(sub < lane, mine_column, 0.0), axis=0, keepdims=True) + owned_before
        slot = jnp.where(owner == device, rank, -1.0)
        picked = column(slot, 128) == (lane // per_drop).astype(f32)
        for k in range(per_drop):
            fact = small_ref[k : k + 1, part]
            cluster = fact & 16383
            chosen = chosen + jnp.where(picked & (lane % per_drop == k), column(fact.astype(f32), 128), 0.0)
            wide_owner = jnp.broadcast_to(owner.astype(f32), wide)
            owner_sum = owner_sum + jnp.where(jnp.broadcast_to(cluster, wide) == mine, wide_owner, 0.0)
        return owner_sum, chosen, owned_before + jnp.sum(is_mine, axis=1, keepdims=True)

    start = (jnp.zeros(wide, f32), jnp.zeros(wide, f32), jnp.zeros((1, 1), f32))
    owner_sum, chosen, _ = lax.fori_loop(0, drops // 128, scan, start)
    home_owner = jnp.broadcast_to(jnp.sum(owner_sum, axis=1, keepdims=True), wide)
    owner_lanes = home_owner.T
    rank = jnp.sum(jnp.where((home_owner == owner_lanes) & (sub < lane), 1.0, 0.0), axis=0, keepdims=True)
    place_ref[0:1, :] = ((owner_lanes[0:1] * capacity + rank) * 3.0).astype(i32)
    fact = jnp.sum(chosen, axis=0, keepdims=True).astype(i32)
    cluster = fact & 16383
    anchor = cluster >> shift
    cluster_column = column(cluster, 128)
    cluster_wide = jnp.broadcast_to(cluster, wide)
    same = (cluster_column >> shift) == (cluster_wide >> shift)
    rank = jnp.sum(jnp.where(same & (cluster_column < cluster_wide), 1.0, 0.0), axis=0, keepdims=True)
    place_ref[1:2, :] = (anchor * capacity + rank.astype(i32)) * 3
    place_ref[2:3, :] = fact >> 14


def index_call(spec, facts, small):
    return pl.pallas_call(
        functools.partial(index_kernel, spec),
        out_shape=[jax.ShapeDtypeStruct((spec[5] // 128 + 1, 128), i32), jax.ShapeDtypeStruct((3, 128), i32)],
        in_specs=[smem, vmem],
        out_specs=[vmem, vmem],
        compiler_params=pltpu.CompilerParams(vmem_limit_bytes=vmem_limit),
        name="index_work",
    )(facts, small)


def pack_kernel(n, place_ref, *refs):
    *speed_refs, out_ref, speed_ref = refs
    total = speed_refs[0][: 3 * n, :]
    for part in speed_refs[1:]:
        total = total + part[: 3 * n, :]
    speed_ref[...] = total
    out_ref[...] = jnp.zeros_like(out_ref)

    def step(i, carry):
        for u in range(16):
            cluster = i * 16 + u
            out_ref[pl.ds(place_ref[0, cluster], 3), :] = speed_ref[pl.ds(3 * cluster, 3), :]
        return carry

    lax.fori_loop(0, n // 16, step, 0)


def pack_call(places, speeds, n, capacity, devices):
    slots = speeds[0].shape[1]
    return pl.pallas_call(
        functools.partial(pack_kernel, n),
        out_shape=jax.ShapeDtypeStruct((devices * capacity * 3, slots), f32),
        in_specs=[smem] + [vmem] * len(speeds),
        out_specs=vmem,
        scratch_shapes=[pltpu.VMEM((3 * n, slots), f32)],
        compiler_params=pltpu.CompilerParams(vmem_limit_bytes=vmem_limit),
        name="pack_owners",
    )(places, *speeds)


def unpack_kernel(n, place_ref, arrived_ref, out_ref, tile_ref):
    slots = arrived_ref.shape[1]
    lane = lax.broadcasted_iota(i32, (3, slots), 1)

    def step(i, carry):
        for u in range(16):
            cluster = i * 16 + u
            value = arrived_ref[pl.ds(place_ref[1, cluster], 3), :]
            tile_ref[cluster, :3, :] = jnp.where(lane < place_ref[2, cluster], value, 0.0)
        return carry

    lax.fori_loop(0, n // 16, step, 0)
    for k in range(3):
        out_ref[n * k : n * (k + 1), :] = tile_ref[:, k, :]


def unpack_call(places, arrived, n):
    slots = arrived.shape[1]
    return pl.pallas_call(
        functools.partial(unpack_kernel, n),
        out_shape=jax.ShapeDtypeStruct((3 * n, slots), f32),
        in_specs=[smem, vmem],
        out_specs=vmem,
        scratch_shapes=[pltpu.VMEM((n, 8, slots), f32)],
        compiler_params=pltpu.CompilerParams(vmem_limit_bytes=vmem_limit),
        name="unpack_drops",
    )(places, arrived)


def per_device(
    positions,
    normals,
    curvature,
    pair_targets,
    pair_sources,
    pair_count,
    node_counts,
    drop_clusters,
    drop_owner,
):
    n, slots = curvature.shape
    rows = lax.axis_size("row")
    cols = lax.axis_size("col")
    devices = rows * cols
    my_row = lax.axis_index("row")
    my_col = lax.axis_index("col")
    device = my_row * cols + my_col
    capacity = max(2, 2 * n // devices)
    hypercube = cols == 4
    hops = rows // 2 + 1

    def swap(value, bit):
        return lax.ppermute(value, "col", [(c, c ^ bit) for c in range(cols)])

    def component_major(value):
        return jnp.transpose(value, (1, 0, 2)).reshape(3 * n, slots)

    block, position, small = prep_call(
        (device * n).reshape(1),
        component_major(positions),
        component_major(normals),
        curvature,
        drop_clusters.T,
        node_counts.T,
        drop_owner.reshape(1, -1),
        pair_targets,
        pair_sources,
    )
    mate_block = swap(block, 1)
    if hypercube:
        across = swap(position, 2)
    to_right = [(r, (r + 1) % rows) for r in range(rows)]
    to_left = [((r + 1) % rows, r) for r in range(rows)]
    right = lax.ppermute(block, "row", to_right)
    left = lax.ppermute(block, "row", to_left)
    if hypercube:
        targets = [block, mate_block, across, swap(across, 1)]
    else:
        gathered = lax.all_gather(position, "col", axis=0, tiled=True)
        targets = [gathered[3 * n * h : 3 * n * (h + 1)] for h in range(cols)]
    listed, places = index_call(
        (n, rows, capacity, *drop_clusters.shape[::-1], pair_targets.shape[1], hypercube),
        jnp.stack([my_row, my_col, device, pair_count[0]]),
        small,
    )
    lists = [listed, swap(listed, 1)]

    total, token, all_targets = hop_call(n, 0, hops, lists, targets, None, None, [block], [mate_block], hypercube)
    for hop in range(1, hops):
        if hop + 1 < hops:
            own = [right, left]
        *own, token = lax.optimization_barrier((*own, token))
        mates = [swap(part, 1) for part in own]
        if rows == 4 and hop == 1:
            passed = jnp.where(my_row % 2 == 0, own[0], own[1])
            opposite = [lax.ppermute(passed, "row", [(0, 1), (1, 0), (2, 3), (3, 2)])]
        elif hop + 1 < hops:
            right = lax.ppermute(own[0], "row", to_right)
            left = lax.ppermute(own[1], "row", to_left)
            opposite = [right]
        total, token, *speed = hop_call(n, hop, hops, lists, [all_targets], token, total, own, mates, hypercube)
        own = opposite

    if hypercube:
        kept, sent = speed
        from_mate = swap(sent, 1)
        across = swap(kept[3 * n :] + from_mate[3 * n :], 2)
        home_speed = [kept, from_mate, across]
    else:
        home_speed = [lax.psum_scatter(speed[0], "col", scatter_dimension=0, tiled=True)]

    outgoing = pack_call(places, home_speed, n, capacity, devices)
    arrived = lax.all_to_all(outgoing, ("row", "col"), split_axis=0, concat_axis=0, tiled=True)
    result = unpack_call(places, arrived, n)
    return jnp.transpose(result.reshape(3, n, slots), (1, 0, 2))


def solution(mesh):
    in_specs = (
        P(("groups", "row", "col"), None, None),
        P(("groups", "row", "col"), None, None),
        P(("groups", "row", "col"), None),
        P(("groups", "row", "col"), None),
        P(("groups", "row", "col"), None),
        P(("groups", "row", "col")),
        P("groups", None),
        P("groups", None),
        P("groups"),
    )
    out_specs = P(("groups", "row", "col"), None, None)
    return jax.shard_map(
        per_device, mesh=mesh, in_specs=in_specs, out_specs=out_specs, check_vma=False
    )
```

```python
import functools
import math

import jax
import jax.numpy as jnp
from jax import lax
from jax.experimental import pallas as pl
from jax.experimental.pallas import tpu as pltpu
from jax.sharding import PartitionSpec as P

f32 = jnp.float32
bf16 = jnp.bfloat16
i32 = jnp.int32
regular_sq = 0.0025
length_scale = 1.0 / math.sqrt(regular_sq)
force_scale = length_scale / (8.0 * math.pi)
unroll = 8
levels = 2
vmem_limit = 24 * 2**20
kernel_flops = 8 * 10**9
whole_vmem = 60 * 2**20
vmem = pl.BlockSpec(memory_space=pltpu.VMEM)
smem = pl.BlockSpec(memory_space=pltpu.SMEM)
hbm = pl.BlockSpec(memory_space=pltpu.HBM)


def split3(value):
    high = value.astype(bf16)
    rest = value - high.astype(f32)
    mid = rest.astype(bf16)
    low = (rest - mid.astype(f32)).astype(bf16)
    return high.astype(f32), mid.astype(f32), low.astype(f32)


def rows16(upper, lower):
    return jnp.concatenate([upper, lower], axis=0).astype(bf16)


def transposed_left(y, f, slots):
    row = lax.broadcasted_iota(i32, (8, slots), 0)
    dot = -(y[0] * f[0] + y[1] * f[1] + y[2] * f[2])
    tile = jnp.where(row == 7, dot, 0.0)
    for k in range(3):
        tile = jnp.where(row == k, y[k], jnp.where(row == 3 + k, f[k], tile))
    high, mid, low = split3(tile)
    first = row < 3
    high_one = jnp.where(first, 1.0, high)
    left = jnp.concatenate(
        [rows16(high, mid), rows16(low, high_one), rows16(high_one, jnp.where(first, 1.0, mid))], axis=0
    )
    return left.T


def products(left, x, slots):
    row = lax.broadcasted_iota(i32, (8, slots), 0)
    zero = jnp.zeros((8, slots), f32)
    tile = jnp.where(row == 7, 1.0, zero)
    for k in range(3):
        tile = jnp.where((row == k) | (row == 3 + k), x[k], tile)
    high, mid, low = split3(tile)
    columns = []
    for k in range(3):
        mine = row == k
        minus = jnp.where(mine, -1.0, zero)
        columns.append(
            [
                rows16(minus, minus),
                rows16(minus, jnp.where(mine, high, 0.0)),
                rows16(jnp.where(mine, mid, 0.0), jnp.where(mine, low, 0.0)),
            ]
        )
    first = row < 3
    high, mid, low = [jnp.where(first, 0.0, part) for part in (high, mid, low)]
    columns.append([rows16(high, high), rows16(high, mid), rows16(low, mid)])
    for k in range(2):
        pick = jnp.where(row == 3 + k, 1.0, zero)
        columns.append([rows16(pick, pick), rows16(pick, zero), rows16(zero, zero)])
    right = jnp.concatenate([jnp.concatenate(column, axis=0) for column in columns], axis=1)
    return lax.dot_general(left, right, (((1,), (0,)), ((), ())), preferred_element_type=f32)


def node_sums(product, force_z, slots):
    row = lax.broadcasted_iota(i32, (8, slots), 0)
    total = None
    for g in range(product.shape[0] // 8):
        part = product[8 * g : 8 * g + 8]
        wx, wy, wz, dot, fx, fy = [part[:, slots * k : slots * (k + 1)] for k in range(6)]
        fz = force_z[8 * g : 8 * g + 8]
        inverse = lax.rsqrt(wx * wx + wy * wy + (wz * wz + 1.0))
        cube = inverse * inverse * inverse
        isotropic = inverse + cube
        project = dot * cube
        terms = (isotropic * fx + project * wx, isotropic * fy + project * wy, isotropic * fz + project * wz)
        total = terms if total is None else tuple(a + b for a, b in zip(total, terms))
    sums = [jnp.broadcast_to(jnp.sum(part, axis=0, keepdims=True), (8, slots)) for part in total]
    return jnp.where(row == 0, sums[0], jnp.where(row == 1, sums[1], jnp.where(row == 2, sums[2], 0.0)))


def hop_kernel(spec, list_ref, mate_list_ref, *refs):
    n, slots, hop, homes, own, mate, first, last, split = spec
    refs = list(refs)
    if first:
        target_refs = [refs.pop(0) for _ in range(homes)]
    else:
        target_ref, _, _ = refs.pop(0), refs.pop(0), refs.pop(0)
    own_refs = [refs.pop(0) for _ in range(own)]
    mate_refs = [refs.pop(0) for _ in range(mate)]
    if first:
        total_ref, token_ref, target_ref = refs.pop(0), refs.pop(0), refs.pop(0)
    else:
        total_ref, token_ref = refs.pop(0), refs.pop(0)
        out_refs = [refs.pop(0) for _ in range((2 if split else 1) if last else 0)]
    source_ref, left_ref = refs
    token_ref[...] = jnp.zeros_like(token_ref)
    clusters = homes * n
    shift = n.bit_length() - 1
    if first:
        for h in range(homes):
            target_ref[3 * n * h : 3 * n * (h + 1), :] = target_refs[h][: 3 * n, :]
        total_ref[...] = jnp.zeros_like(total_ref)
    for place, block in list(enumerate(own_refs)) + [(2 + b, block) for b, block in enumerate(mate_refs)]:
        source_ref[6 * n * place : 6 * n * (place + 1), :] = block[...]

    bound_row = list_ref.shape[0] - 1

    def wide(value):
        return jnp.broadcast_to(value, (8, slots))

    def run(level):
        groups = slots // 8 * (levels - level) // levels
        lane = hop * levels + level
        own_start, own_end = list_ref[bound_row, lane], list_ref[bound_row, lane + 1]
        mate_start, mate_end = mate_list_ref[bound_row, lane], mate_list_ref[bound_row, lane + 1]
        own_count = (own_end - own_start + 1) >> 1
        count = own_count + ((mate_end - mate_start) >> 1)
        after_own = mate_start + 1 - 2 * own_count

        def entry(index):
            live = index < count
            mine = index < own_count
            place = jnp.where(live, 2 * index + jnp.where(mine, own_start, after_own), 0)
            row, column_of = place >> 7, place & 127
            packed = jnp.where(mine, list_ref[row, column_of], mate_list_ref[row, column_of])
            packed = jnp.where(live, packed, 0)
            target = (packed & 0xFFF) ^ jnp.where(mine, 0, n if split else 0)
            source = (packed >> 12) + jnp.where(mine, 0, 2 * n)
            return live, target, jnp.where(live, source, 0)

        def fetch(index, u):
            _, _, source = entry(index)
            base = source + (source >> shift) * (5 * n)
            values = [wide(source_ref[pl.ds(base + n * k, 1), :]) for k in range(6)]
            left_ref[u] = transposed_left(values[:3], values[3:], slots)

        @pl.when(count > 0)
        def _():
            for u in range(unroll):
                fetch(u, u)

        def step(i, carry):
            results = []
            lefts = [left_ref[u, : 8 * groups] for u in range(unroll)]
            for u in range(unroll):
                live, target, source = entry(i * unroll + u)
                base = target + (target >> shift) * (2 * n)
                x = [wide(target_ref[pl.ds(base + n * k, 1), :]) for k in range(3)]
                product = products(lefts[u], x, slots)
                force_z = source_ref[pl.ds(source + (source >> shift) * (5 * n) + 5 * n, 1), :]
                force_z = jnp.broadcast_to(force_z, (slots, slots)).T
                results.append((jnp.where(live, target, clusters), node_sums(product, force_z, slots)))
            for u in range(unroll):
                fetch((i + 1) * unroll + u, u)
            for target, result in results:
                total_ref[pl.ds(target * 4, 4), :] += result[:4]
            return carry

        lax.fori_loop(0, (count + unroll - 1) // unroll, step, 0)

    for level in range(levels):
        run(level)
    if last:
        for h in range(homes):
            out_ref = out_refs[h % 2] if split else out_refs[0]
            first_row = 3 * n * (h // 2 if split else h)

            def move(i, carry, h=h, out_ref=out_ref, first_row=first_row):
                for u in range(8):
                    tile = total_ref[pl.ds((n * h + i * 8 + u) * 4, 4), :]
                    out_ref[pl.ds(first_row + i * 24 + 3 * u, 3), :] = tile[:3]
                return carry

            lax.fori_loop(0, n // 8, move, 0)


def hop_call(n, hop, hops, lists, targets, token, total, own, mate, split):
    first, last = hop == 0, hop == hops - 1
    slots = own[0].shape[1]
    homes = len(targets) if first else targets[0].shape[0] // (3 * n)
    total_shape = jax.ShapeDtypeStruct((homes * n * 4 + 8, slots), f32)
    aliases = {}
    operands = [*lists, *targets]
    if not first:
        operands += [token, total]
    out_shape = [total_shape, jax.ShapeDtypeStruct((8, 128), f32)]
    if first:
        out_shape += [jax.ShapeDtypeStruct((homes * 3 * n, slots), f32)]
    elif last:
        parts = 2 if split else 1
        out_shape += [jax.ShapeDtypeStruct((homes * 3 * n // parts, slots), f32)] * parts
    if not first:
        aliases = {len(operands) - 1: 0}
    operands += [*own, *mate]
    spec = (n, slots, hop, homes, len(own), len(mate), first, last, split)
    return pl.pallas_call(
        functools.partial(hop_kernel, spec),
        out_shape=out_shape,
        in_specs=[smem, smem] + [vmem] * (len(operands) - 2),
        out_specs=[vmem] * len(out_shape),
        scratch_shapes=[
            pltpu.VMEM((4 * 6 * n, slots), f32),
            pltpu.VMEM((unroll, slots, 48), bf16),
        ],
        input_output_aliases=aliases,
        compiler_params=pltpu.CompilerParams(vmem_limit_bytes=vmem_limit),
        cost_estimate=pl.CostEstimate(flops=kernel_flops if hop else kernel_flops // 8, bytes_accessed=10**6, transcendentals=10**6),
        name=f"pairs_hop{hop}",
    )(*operands)


def column(row, rows):
    return jnp.broadcast_to(row, (rows, 128)).T


def prep_kernel(n, base_ref, *refs):
    ins, (out_ref, own_ref, small_ref), held, sems = refs[:8], refs[8:11], refs[11:19], refs[19]
    copies = [pltpu.make_async_copy(a, b, sems.at[k]) for k, (a, b) in enumerate(zip(ins, held))]
    for copy in copies:
        copy.start()
    for copy in copies:
        copy.wait()
    position_ref, normal_ref, curvature_ref, cluster_ref, count_ref, owner_ref, target_ref, source_ref = held
    slots = position_ref.shape[1]
    scaled = position_ref[...] * length_scale
    out_ref[: 3 * n, :] = scaled
    own_ref[...] = scaled
    mine = base_ref[0] + lax.broadcasted_iota(i32, (n, 128), 0)
    total = jnp.zeros((n, 128), f32)
    for k in range(cluster_ref.shape[0]):
        for j in range(cluster_ref.shape[1] // 128):
            part = slice(128 * j, 128 * (j + 1))
            cluster = jnp.broadcast_to(cluster_ref[k : k + 1, part], (n, 128))
            count = jnp.broadcast_to(count_ref[k : k + 1, part].astype(f32), (n, 128))
            total = total + jnp.where(cluster == mine, count, 0.0)
    live_count = jnp.sum(total, axis=1, keepdims=True)
    lane = lax.broadcasted_iota(i32, (n, slots), 1).astype(f32)
    strength = jnp.where(lane < live_count, curvature_ref[...] * force_scale, 0.0)
    for k in range(3):
        out_ref[n * (3 + k) : n * (4 + k), :] = normal_ref[n * k : n * (k + 1), :] * strength
    per_drop, drops = cluster_ref.shape
    pairs = target_ref.shape[1]
    small_ref[:per_drop, :drops] = cluster_ref[...] + (count_ref[...] << 14)
    small_ref[per_drop : per_drop + 1, :drops] = owner_ref[...]
    small_ref[per_drop + 1 : per_drop + 2, :pairs] = target_ref[...]
    small_ref[per_drop + 2 : per_drop + 3, :pairs] = source_ref[...]


def prep_call(base, *operands):
    n, slots = operands[2].shape
    per_drop, drops = operands[3].shape
    small = (per_drop + 8, max(drops, operands[6].shape[1]))
    shapes = [((6 * n, slots), f32), ((3 * n, slots), f32), (small, i32)]
    return pl.pallas_call(
        functools.partial(prep_kernel, n),
        out_shape=[jax.ShapeDtypeStruct(*shape) for shape in shapes],
        in_specs=[smem] + [hbm] * 8,
        out_specs=[vmem] * 3,
        scratch_shapes=[pltpu.VMEM(x.shape, x.dtype) for x in operands] + [pltpu.SemaphoreType.DMA((8,))],
        compiler_params=pltpu.CompilerParams(vmem_limit_bytes=whole_vmem),
        name="prep_sources",
    )(base, *operands)


def index_kernel(spec, facts_ref, *refs):
    n, rows, cols, capacity, per_drop, drops, pair_slots, split = spec
    small_ref, list_ref, place_ref = refs
    my_row, my_col, device, live_pairs = [facts_ref[k] for k in range(4)]
    shift = n.bit_length() - 1
    wide = (128, 128)
    lane_row = lax.broadcasted_iota(i32, (1, 128), 1)
    sub = lax.broadcasted_iota(i32, wide, 0)
    lane = lax.broadcasted_iota(i32, wide, 1)

    blocks = pair_slots // 128
    wide_source = []
    for b in range(blocks):
        source = small_ref[per_drop + 2 : per_drop + 3, 128 * b : 128 * (b + 1)]
        cluster = ((source >> shift) * cols + my_col) * n + (source & (n - 1))
        wide_source.append(jnp.broadcast_to(cluster, wide))

    def look_up(j, counts):
        part = pl.ds(pl.multiple_of(j * 128, 128), 128)
        for k in range(per_drop):
            fact = column(small_ref[k : k + 1, part], 128)
            cluster, count = fact & 16383, (fact >> 14).astype(f32)
            counts = [c + jnp.where(cluster == w, count, 0.0) for c, w in zip(counts, wide_source)]
        return counts

    counts = lax.fori_loop(0, drops // 128, look_up, [jnp.zeros(wide, f32)] * blocks)
    keys, packs = [], []
    for b in range(blocks):
        target = small_ref[per_drop + 1 : per_drop + 2, 128 * b : 128 * (b + 1)]
        source = small_ref[per_drop + 2 : per_drop + 3, 128 * b : 128 * (b + 1)]
        ahead = ((source >> shift) - my_row) & (rows - 1)
        hop = jnp.minimum(ahead, rows - ahead)
        index = lane_row + 128 * b
        key = jnp.where(index < live_pairs, hop, rows)
        count = jnp.sum(counts[b], axis=0, keepdims=True)
        level = jnp.zeros((1, 128), i32)
        for k in range(1, levels):
            level = level + jnp.where(count <= n * k / levels, 1, 0)
        keys.append((key * levels + level) * (128 * blocks) + index)
        home = target >> shift
        if split:
            home = home ^ my_col
        side = jnp.where((ahead > 0) & (ahead * 2 < rows), n, 0)
        packs.append((home * n + (target & (n - 1)) + (side + (source & (n - 1))) * 4096).astype(f32))
    key_columns = [column(key, 128) for key in keys]
    order_columns = []
    for b in range(blocks):
        before = jnp.zeros(wide, f32)
        for c in range(blocks):
            before = before + jnp.where(key_columns[c] < jnp.broadcast_to(keys[b], wide), 1.0, 0.0)
        order_columns.append(column(jnp.sum(before, axis=0, keepdims=True), 128))
    pack_columns = [column(pack, 128) for pack in packs]
    lanes = lane.astype(f32)
    for b in range(blocks):
        ordered = jnp.zeros(wide, f32)
        for c in range(blocks):
            ordered = ordered + jnp.where(order_columns[c] == lanes + 128.0 * b, pack_columns[c], 0.0)
        list_ref[b : b + 1, :] = jnp.sum(ordered, axis=0, keepdims=True).astype(i32)
    below = jnp.zeros(wide, f32)
    for c in range(blocks):
        below = below + jnp.where(key_columns[c] < lane * (128 * blocks), 1.0, 0.0)
    list_ref[blocks : blocks + 1, :] = jnp.sum(below, axis=0, keepdims=True).astype(i32)

    mine = device * n + sub

    def scan(j, carry):
        owner_sum, chosen, owned_before = carry
        part = pl.ds(pl.multiple_of(j * 128, 128), 128)
        owner = small_ref[per_drop : per_drop + 1, part]
        is_mine = jnp.where(owner == device, 1.0, 0.0)
        mine_column = column(is_mine, 128)
        rank = jnp.sum(jnp.where(sub < lane, mine_column, 0.0), axis=0, keepdims=True) + owned_before
        slot = jnp.where(owner == device, rank, -1.0)
        picked = column(slot, 128) == (lane // per_drop).astype(f32)
        for k in range(per_drop):
            fact = small_ref[k : k + 1, part]
            cluster = fact & 16383
            chosen = chosen + jnp.where(picked & (lane % per_drop == k), column(fact.astype(f32), 128), 0.0)
            wide_owner = jnp.broadcast_to(owner.astype(f32), wide)
            owner_sum = owner_sum + jnp.where(jnp.broadcast_to(cluster, wide) == mine, wide_owner, 0.0)
        return owner_sum, chosen, owned_before + jnp.sum(is_mine, axis=1, keepdims=True)

    start = (jnp.zeros(wide, f32), jnp.zeros(wide, f32), jnp.zeros((1, 1), f32))
    owner_sum, chosen, _ = lax.fori_loop(0, drops // 128, scan, start)
    home_owner = jnp.broadcast_to(jnp.sum(owner_sum, axis=1, keepdims=True), wide)
    owner_lanes = home_owner.T
    rank = jnp.sum(jnp.where((home_owner == owner_lanes) & (sub < lane), 1.0, 0.0), axis=0, keepdims=True)
    place_ref[0:1, :] = ((owner_lanes[0:1] * capacity + rank) * 3.0).astype(i32)
    fact = jnp.sum(chosen, axis=0, keepdims=True).astype(i32)
    cluster = fact & 16383
    anchor = cluster >> shift
    cluster_column = column(cluster, 128)
    cluster_wide = jnp.broadcast_to(cluster, wide)
    same = (cluster_column >> shift) == (cluster_wide >> shift)
    rank = jnp.sum(jnp.where(same & (cluster_column < cluster_wide), 1.0, 0.0), axis=0, keepdims=True)
    place_ref[1:2, :] = (anchor * capacity + rank.astype(i32)) * 3
    place_ref[2:3, :] = fact >> 14


def index_call(spec, facts, small):
    return pl.pallas_call(
        functools.partial(index_kernel, spec),
        out_shape=[jax.ShapeDtypeStruct((spec[6] // 128 + 1, 128), i32), jax.ShapeDtypeStruct((3, 128), i32)],
        in_specs=[smem, vmem],
        out_specs=[vmem, vmem],
        compiler_params=pltpu.CompilerParams(vmem_limit_bytes=vmem_limit),
        name="index_work",
    )(facts, small)


def pack_kernel(n, place_ref, *refs):
    *speed_refs, out_ref, speed_ref = refs
    total = speed_refs[0][: 3 * n, :]
    for part in speed_refs[1:]:
        total = total + part[: 3 * n, :]
    speed_ref[...] = total
    out_ref[...] = jnp.zeros_like(out_ref)

    def step(i, carry):
        for u in range(16):
            cluster = i * 16 + u
            out_ref[pl.ds(place_ref[0, cluster], 3), :] = speed_ref[pl.ds(3 * cluster, 3), :]
        return carry

    lax.fori_loop(0, n // 16, step, 0)


def pack_call(places, speeds, n, capacity, devices):
    slots = speeds[0].shape[1]
    return pl.pallas_call(
        functools.partial(pack_kernel, n),
        out_shape=jax.ShapeDtypeStruct((devices * capacity * 3, slots), f32),
        in_specs=[smem] + [vmem] * len(speeds),
        out_specs=vmem,
        scratch_shapes=[pltpu.VMEM((3 * n, slots), f32)],
        compiler_params=pltpu.CompilerParams(vmem_limit_bytes=vmem_limit),
        name="pack_owners",
    )(places, *speeds)


def unpack_kernel(n, place_ref, arrived_ref, out_ref, tile_ref):
    slots = arrived_ref.shape[1]
    lane = lax.broadcasted_iota(i32, (3, slots), 1)

    def step(i, carry):
        for u in range(16):
            cluster = i * 16 + u
            value = arrived_ref[pl.ds(place_ref[1, cluster], 3), :]
            tile_ref[cluster, :3, :] = jnp.where(lane < place_ref[2, cluster], value, 0.0)
        return carry

    lax.fori_loop(0, n // 16, step, 0)
    for k in range(3):
        out_ref[n * k : n * (k + 1), :] = tile_ref[:, k, :]


def unpack_call(places, arrived, n):
    slots = arrived.shape[1]
    return pl.pallas_call(
        functools.partial(unpack_kernel, n),
        out_shape=jax.ShapeDtypeStruct((3 * n, slots), f32),
        in_specs=[smem, vmem],
        out_specs=vmem,
        scratch_shapes=[pltpu.VMEM((n, 8, slots), f32)],
        compiler_params=pltpu.CompilerParams(vmem_limit_bytes=vmem_limit),
        name="unpack_drops",
    )(places, arrived)


def per_device(
    positions,
    normals,
    curvature,
    pair_targets,
    pair_sources,
    pair_count,
    node_counts,
    drop_clusters,
    drop_owner,
):
    n, slots = curvature.shape
    rows = lax.axis_size("row")
    cols = lax.axis_size("col")
    devices = rows * cols
    my_row = lax.axis_index("row")
    my_col = lax.axis_index("col")
    device = my_row * cols + my_col
    capacity = max(2, 2 * n // devices)
    hypercube = cols == 4
    hops = rows // 2 + 1

    def swap(value, bit):
        return lax.ppermute(value, "col", [(c, c ^ bit) for c in range(cols)])

    def component_major(value):
        return jnp.transpose(value, (1, 0, 2)).reshape(3 * n, slots)

    block, position, small = prep_call(
        (device * n).reshape(1),
        component_major(positions),
        component_major(normals),
        curvature,
        drop_clusters.T,
        node_counts.T,
        drop_owner.reshape(1, -1),
        pair_targets,
        pair_sources,
    )
    mate_block = swap(block, 1)
    if hypercube:
        across = swap(position, 2)
    to_right = [(r, (r + 1) % rows) for r in range(rows)]
    to_left = [((r + 1) % rows, r) for r in range(rows)]
    right = lax.ppermute(block, "row", to_right)
    left = lax.ppermute(block, "row", to_left)
    if hypercube:
        targets = [block, mate_block, across, swap(across, 1)]
    else:
        gathered = lax.all_gather(position, "col", axis=0, tiled=True)
        targets = [gathered[3 * n * h : 3 * n * (h + 1)] for h in range(cols)]
    listed, places = index_call(
        (n, rows, cols, capacity, *drop_clusters.shape[::-1], pair_targets.shape[1], hypercube),
        jnp.stack([my_row, my_col, device, pair_count[0]]),
        small,
    )
    lists = [listed, swap(listed, 1)]

    total, token, all_targets = hop_call(n, 0, hops, lists, targets, None, None, [block], [mate_block], hypercube)
    for hop in range(1, hops):
        if hop + 1 < hops:
            own = [right, left]
        *own, token = lax.optimization_barrier((*own, token))
        mates = [swap(part, 1) for part in own]
        if rows == 4 and hop == 1:
            passed = jnp.where(my_row % 2 == 0, own[0], own[1])
            opposite = [lax.ppermute(passed, "row", [(0, 1), (1, 0), (2, 3), (3, 2)])]
        elif hop + 1 < hops:
            right = lax.ppermute(own[0], "row", to_right)
            left = lax.ppermute(own[1], "row", to_left)
            opposite = [right]
        total, token, *speed = hop_call(n, hop, hops, lists, [all_targets], token, total, own, mates, hypercube)
        own = opposite

    if hypercube:
        kept, sent = speed
        from_mate = swap(sent, 1)
        across = swap(kept[3 * n :] + from_mate[3 * n :], 2)
        home_speed = [kept, from_mate, across]
    else:
        home_speed = [lax.psum_scatter(speed[0], "col", scatter_dimension=0, tiled=True)]

    outgoing = pack_call(places, home_speed, n, capacity, devices)
    arrived = lax.all_to_all(outgoing, ("row", "col"), split_axis=0, concat_axis=0, tiled=True)
    result = unpack_call(places, arrived, n)
    return jnp.transpose(result.reshape(3, n, slots), (1, 0, 2))


def solution(mesh):
    in_specs = (
        P(("groups", "row", "col"), None, None),
        P(("groups", "row", "col"), None, None),
        P(("groups", "row", "col"), None),
        P(("groups", "row", "col"), None),
        P(("groups", "row", "col"), None),
        P(("groups", "row", "col")),
        P("groups", None),
        P("groups", None),
        P("groups"),
    )
    out_specs = P(("groups", "row", "col"), None, None)
    return jax.shard_map(
        per_device, mesh=mesh, in_specs=in_specs, out_specs=out_specs, check_vma=False
    )
```

```python
import functools
import math

import jax
import jax.numpy as jnp
from jax import lax
from jax.experimental import pallas as pl
from jax.experimental.pallas import tpu as pltpu
from jax.sharding import PartitionSpec as P

f32 = jnp.float32
bf16 = jnp.bfloat16
i32 = jnp.int32
regular_sq = 0.0025
length_scale = 1.0 / math.sqrt(regular_sq)
force_scale = length_scale / (8.0 * math.pi)
unroll = 8
levels = 2
vmem_limit = 24 * 2**20
kernel_flops = 8 * 10**9
whole_vmem = 60 * 2**20
vmem = pl.BlockSpec(memory_space=pltpu.VMEM)
smem = pl.BlockSpec(memory_space=pltpu.SMEM)
hbm = pl.BlockSpec(memory_space=pltpu.HBM)


def split3(value):
    high = value.astype(bf16)
    rest = value - high.astype(f32)
    mid = rest.astype(bf16)
    low = (rest - mid.astype(f32)).astype(bf16)
    return high.astype(f32), mid.astype(f32), low.astype(f32)


def rows16(upper, lower):
    return jnp.concatenate([upper, lower], axis=0).astype(bf16)


def transposed_left(y, f, slots):
    row = lax.broadcasted_iota(i32, (8, slots), 0)
    dot = -(y[0] * f[0] + y[1] * f[1] + y[2] * f[2])
    tile = jnp.where(row == 7, dot, 0.0)
    for k in range(3):
        tile = jnp.where(row == k, y[k], jnp.where(row == 3 + k, f[k], tile))
    high, mid, low = split3(tile)
    first = row < 3
    high_one = jnp.where(first, 1.0, high)
    left = jnp.concatenate(
        [rows16(high, mid), rows16(low, high_one), rows16(high_one, jnp.where(first, 1.0, mid))], axis=0
    )
    return left.T


def products(left, x, slots):
    row = lax.broadcasted_iota(i32, (8, slots), 0)
    zero = jnp.zeros((8, slots), f32)
    tile = jnp.where(row == 7, 1.0, zero)
    for k in range(3):
        tile = jnp.where((row == k) | (row == 3 + k), x[k], tile)
    high, mid, low = split3(tile)
    columns = []
    for k in range(3):
        mine = row == k
        minus = jnp.where(mine, -1.0, zero)
        columns.append(
            [
                rows16(minus, minus),
                rows16(minus, jnp.where(mine, high, 0.0)),
                rows16(jnp.where(mine, mid, 0.0), jnp.where(mine, low, 0.0)),
            ]
        )
    first = row < 3
    high, mid, low = [jnp.where(first, 0.0, part) for part in (high, mid, low)]
    columns.append([rows16(high, high), rows16(high, mid), rows16(low, mid)])
    for k in range(2):
        pick = jnp.where(row == 3 + k, 1.0, zero)
        columns.append([rows16(pick, pick), rows16(pick, zero), rows16(zero, zero)])
    right = jnp.concatenate([jnp.concatenate(column, axis=0) for column in columns], axis=1)
    return lax.dot_general(left, right, (((1,), (0,)), ((), ())), preferred_element_type=f32)


def node_sums(product, force_z, slots):
    row = lax.broadcasted_iota(i32, (8, slots), 0)
    total = None
    for g in range(product.shape[0] // 8):
        part = product[8 * g : 8 * g + 8]
        wx, wy, wz, dot, fx, fy = [part[:, slots * k : slots * (k + 1)] for k in range(6)]
        fz = force_z[8 * g : 8 * g + 8]
        inverse = lax.rsqrt(wx * wx + wy * wy + (wz * wz + 1.0))
        cube = inverse * inverse * inverse
        isotropic = inverse + cube
        project = dot * cube
        terms = (isotropic * fx + project * wx, isotropic * fy + project * wy, isotropic * fz + project * wz)
        total = terms if total is None else tuple(a + b for a, b in zip(total, terms))
    sums = [jnp.broadcast_to(jnp.sum(part, axis=0, keepdims=True), (8, slots)) for part in total]
    return jnp.where(row == 0, sums[0], jnp.where(row == 1, sums[1], jnp.where(row == 2, sums[2], 0.0)))


def hop_kernel(spec, list_ref, mate_list_ref, *refs):
    n, slots, hop, homes, own, mate, first, emit, split = spec
    refs = list(refs)
    if first:
        target_refs = [refs.pop(0) for _ in range(homes)]
    else:
        target_ref, _, _ = refs.pop(0), refs.pop(0), refs.pop(0)
    own_refs = [refs.pop(0) for _ in range(own)]
    mate_refs = [refs.pop(0) for _ in range(mate)]
    if first:
        total_ref, token_ref, target_ref = refs.pop(0), refs.pop(0), refs.pop(0)
    else:
        total_ref, token_ref = refs.pop(0), refs.pop(0)
        out_refs = [refs.pop(0) for _ in emit]
    source_ref, left_ref = refs
    token_ref[...] = jnp.zeros_like(token_ref)
    clusters = homes * n
    shift = n.bit_length() - 1
    if first:
        for h in range(homes):
            target_ref[3 * n * h : 3 * n * (h + 1), :] = target_refs[h][: 3 * n, :]
        total_ref[...] = jnp.zeros_like(total_ref)
    for place, block in list(enumerate(own_refs)) + [(2 + b, block) for b, block in enumerate(mate_refs)]:
        source_ref[6 * n * place : 6 * n * (place + 1), :] = block[...]

    bound_row = list_ref.shape[0] - 1

    def wide(value):
        return jnp.broadcast_to(value, (8, slots))

    def run(level):
        groups = slots // 8 * (levels - level) // levels
        lane = hop * levels + level
        own_start, own_end = list_ref[bound_row, lane], list_ref[bound_row, lane + 1]
        mate_start, mate_end = mate_list_ref[bound_row, lane], mate_list_ref[bound_row, lane + 1]
        own_count = (own_end - own_start + 1) >> 1
        count = own_count + ((mate_end - mate_start) >> 1)
        after_own = mate_start + 1 - 2 * own_count

        def entry(index):
            live = index < count
            mine = index < own_count
            place = jnp.where(live, 2 * index + jnp.where(mine, own_start, after_own), 0)
            row, column_of = place >> 7, place & 127
            packed = jnp.where(mine, list_ref[row, column_of], mate_list_ref[row, column_of])
            packed = jnp.where(live, packed, 0)
            target = (packed & 0xFFF) ^ jnp.where(mine, 0, n if split else 0)
            source = (packed >> 12) + jnp.where(mine, 0, 2 * n)
            return live, target, jnp.where(live, source, 0)

        def fetch(index, u):
            _, _, source = entry(index)
            base = source + (source >> shift) * (5 * n)
            values = [wide(source_ref[pl.ds(base + n * k, 1), :]) for k in range(6)]
            left_ref[u] = transposed_left(values[:3], values[3:], slots)

        @pl.when(count > 0)
        def _():
            for u in range(unroll):
                fetch(u, u)

        def step(i, carry):
            results = []
            lefts = [left_ref[u, : 8 * groups] for u in range(unroll)]
            for u in range(unroll):
                live, target, source = entry(i * unroll + u)
                base = target + (target >> shift) * (2 * n)
                x = [wide(target_ref[pl.ds(base + n * k, 1), :]) for k in range(3)]
                product = products(lefts[u], x, slots)
                force_z = source_ref[pl.ds(source + (source >> shift) * (5 * n) + 5 * n, 1), :]
                force_z = jnp.broadcast_to(force_z, (slots, slots)).T
                results.append((jnp.where(live, target, clusters), node_sums(product, force_z, slots)))
            for u in range(unroll):
                fetch((i + 1) * unroll + u, u)
            for target, result in results:
                total_ref[pl.ds(target * 4, 4), :] += result[:4]
            return carry

        lax.fori_loop(0, (count + unroll - 1) // unroll, step, 0)

    for level in range(levels):
        run(level)
    for out_ref, out_homes in zip(out_refs if emit else [], emit):
        for place, h in enumerate(out_homes):

            def move(i, carry, h=h, out_ref=out_ref, first_row=3 * n * place):
                for u in range(8):
                    tile = total_ref[pl.ds((n * h + i * 8 + u) * 4, 4), :]
                    out_ref[pl.ds(first_row + i * 24 + 3 * u, 3), :] = tile[:3]
                return carry

            lax.fori_loop(0, n // 8, move, 0)


def hop_call(n, hop, emit, lists, targets, token, total, own, mate, split):
    first = hop == 0
    slots = own[0].shape[1]
    homes = len(targets) if first else targets[0].shape[0] // (3 * n)
    total_shape = jax.ShapeDtypeStruct((homes * n * 4 + 8, slots), f32)
    aliases = {}
    operands = [*lists, *targets]
    if not first:
        operands += [token, total]
    out_shape = [total_shape, jax.ShapeDtypeStruct((8, 128), f32)]
    if first:
        out_shape += [jax.ShapeDtypeStruct((homes * 3 * n, slots), f32)]
    out_shape += [jax.ShapeDtypeStruct((len(out_homes) * 3 * n, slots), f32) for out_homes in emit]
    if not first:
        aliases = {len(operands) - 1: 0}
    operands += [*own, *mate]
    spec = (n, slots, hop, homes, len(own), len(mate), first, emit, split)
    return pl.pallas_call(
        functools.partial(hop_kernel, spec),
        out_shape=out_shape,
        in_specs=[smem, smem] + [vmem] * (len(operands) - 2),
        out_specs=[vmem] * len(out_shape),
        scratch_shapes=[
            pltpu.VMEM((4 * 6 * n, slots), f32),
            pltpu.VMEM((unroll, slots, 48), bf16),
        ],
        input_output_aliases=aliases,
        compiler_params=pltpu.CompilerParams(vmem_limit_bytes=vmem_limit),
        cost_estimate=pl.CostEstimate(flops=kernel_flops if hop else kernel_flops // 8, bytes_accessed=10**6, transcendentals=10**6),
        name=f"pairs_hop{hop}",
    )(*operands)


def column(row, rows):
    return jnp.broadcast_to(row, (rows, 128)).T


def prep_kernel(n, base_ref, *refs):
    ins, (out_ref, own_ref, small_ref), held, sems = refs[:8], refs[8:11], refs[11:19], refs[19]
    copies = [pltpu.make_async_copy(a, b, sems.at[k]) for k, (a, b) in enumerate(zip(ins, held))]
    for copy in copies:
        copy.start()
    for copy in copies:
        copy.wait()
    position_ref, normal_ref, curvature_ref, cluster_ref, count_ref, owner_ref, target_ref, source_ref = held
    slots = position_ref.shape[1]
    scaled = position_ref[...] * length_scale
    out_ref[: 3 * n, :] = scaled
    own_ref[...] = scaled
    mine = base_ref[0] + lax.broadcasted_iota(i32, (n, 128), 0)
    total = jnp.zeros((n, 128), f32)
    for k in range(cluster_ref.shape[0]):
        for j in range(cluster_ref.shape[1] // 128):
            part = slice(128 * j, 128 * (j + 1))
            cluster = jnp.broadcast_to(cluster_ref[k : k + 1, part], (n, 128))
            count = jnp.broadcast_to(count_ref[k : k + 1, part].astype(f32), (n, 128))
            total = total + jnp.where(cluster == mine, count, 0.0)
    live_count = jnp.sum(total, axis=1, keepdims=True)
    lane = lax.broadcasted_iota(i32, (n, slots), 1).astype(f32)
    strength = jnp.where(lane < live_count, curvature_ref[...] * force_scale, 0.0)
    for k in range(3):
        out_ref[n * (3 + k) : n * (4 + k), :] = normal_ref[n * k : n * (k + 1), :] * strength
    per_drop, drops = cluster_ref.shape
    pairs = target_ref.shape[1]
    small_ref[:per_drop, :drops] = cluster_ref[...] + (count_ref[...] << 14)
    small_ref[per_drop : per_drop + 1, :drops] = owner_ref[...]
    small_ref[per_drop + 1 : per_drop + 2, :pairs] = target_ref[...]
    small_ref[per_drop + 2 : per_drop + 3, :pairs] = source_ref[...]


def prep_call(base, *operands):
    n, slots = operands[2].shape
    per_drop, drops = operands[3].shape
    small = (per_drop + 8, max(drops, operands[6].shape[1]))
    shapes = [((6 * n, slots), f32), ((3 * n, slots), f32), (small, i32)]
    return pl.pallas_call(
        functools.partial(prep_kernel, n),
        out_shape=[jax.ShapeDtypeStruct(*shape) for shape in shapes],
        in_specs=[smem] + [hbm] * 8,
        out_specs=[vmem] * 3,
        scratch_shapes=[pltpu.VMEM(x.shape, x.dtype) for x in operands] + [pltpu.SemaphoreType.DMA((8,))],
        compiler_params=pltpu.CompilerParams(vmem_limit_bytes=whole_vmem),
        name="prep_sources",
    )(base, *operands)


def index_kernel(spec, facts_ref, *refs):
    n, rows, cols, capacity, per_drop, drops, pair_slots, split = spec
    small_ref, list_ref, place_ref = refs
    my_row, my_col, device, live_pairs = [facts_ref[k] for k in range(4)]
    shift = n.bit_length() - 1
    wide = (128, 128)
    lane_row = lax.broadcasted_iota(i32, (1, 128), 1)
    sub = lax.broadcasted_iota(i32, wide, 0)
    lane = lax.broadcasted_iota(i32, wide, 1)

    blocks = pair_slots // 128
    wide_source = []
    for b in range(blocks):
        source = small_ref[per_drop + 2 : per_drop + 3, 128 * b : 128 * (b + 1)]
        cluster = ((source >> shift) * cols + my_col) * n + (source & (n - 1))
        wide_source.append(jnp.broadcast_to(cluster, wide))

    def look_up(j, counts):
        part = pl.ds(pl.multiple_of(j * 128, 128), 128)
        for k in range(per_drop):
            fact = column(small_ref[k : k + 1, part], 128)
            cluster, count = fact & 16383, (fact >> 14).astype(f32)
            counts = [c + jnp.where(cluster == w, count, 0.0) for c, w in zip(counts, wide_source)]
        return counts

    counts = lax.fori_loop(0, drops // 128, look_up, [jnp.zeros(wide, f32)] * blocks)
    keys, packs = [], []
    for b in range(blocks):
        target = small_ref[per_drop + 1 : per_drop + 2, 128 * b : 128 * (b + 1)]
        source = small_ref[per_drop + 2 : per_drop + 3, 128 * b : 128 * (b + 1)]
        ahead = ((source >> shift) - my_row) & (rows - 1)
        hop = jnp.minimum(ahead, rows - ahead)
        index = lane_row + 128 * b
        if split:
            hop = jnp.where((hop == rows // 2) & (((target >> shift) ^ my_col) < 2), hop + 1, hop)
        key = jnp.where(index < live_pairs, hop, rows)
        count = jnp.sum(counts[b], axis=0, keepdims=True)
        level = jnp.zeros((1, 128), i32)
        for k in range(1, levels):
            level = level + jnp.where(count <= n * k / levels, 1, 0)
        keys.append((key * levels + level) * (128 * blocks) + index)
        home = target >> shift
        if split:
            home = home ^ my_col
        side = jnp.where((ahead > 0) & (ahead * 2 < rows), n, 0)
        packs.append((home * n + (target & (n - 1)) + (side + (source & (n - 1))) * 4096).astype(f32))
    key_columns = [column(key, 128) for key in keys]
    order_columns = []
    for b in range(blocks):
        before = jnp.zeros(wide, f32)
        for c in range(blocks):
            before = before + jnp.where(key_columns[c] < jnp.broadcast_to(keys[b], wide), 1.0, 0.0)
        order_columns.append(column(jnp.sum(before, axis=0, keepdims=True), 128))
    pack_columns = [column(pack, 128) for pack in packs]
    lanes = lane.astype(f32)
    for b in range(blocks):
        ordered = jnp.zeros(wide, f32)
        for c in range(blocks):
            ordered = ordered + jnp.where(order_columns[c] == lanes + 128.0 * b, pack_columns[c], 0.0)
        list_ref[b : b + 1, :] = jnp.sum(ordered, axis=0, keepdims=True).astype(i32)
    below = jnp.zeros(wide, f32)
    for c in range(blocks):
        below = below + jnp.where(key_columns[c] < lane * (128 * blocks), 1.0, 0.0)
    list_ref[blocks : blocks + 1, :] = jnp.sum(below, axis=0, keepdims=True).astype(i32)

    mine = device * n + sub

    def scan(j, carry):
        owner_sum, chosen, owned_before = carry
        part = pl.ds(pl.multiple_of(j * 128, 128), 128)
        owner = small_ref[per_drop : per_drop + 1, part]
        is_mine = jnp.where(owner == device, 1.0, 0.0)
        mine_column = column(is_mine, 128)
        rank = jnp.sum(jnp.where(sub < lane, mine_column, 0.0), axis=0, keepdims=True) + owned_before
        slot = jnp.where(owner == device, rank, -1.0)
        picked = column(slot, 128) == (lane // per_drop).astype(f32)
        for k in range(per_drop):
            fact = small_ref[k : k + 1, part]
            cluster = fact & 16383
            chosen = chosen + jnp.where(picked & (lane % per_drop == k), column(fact.astype(f32), 128), 0.0)
            wide_owner = jnp.broadcast_to(owner.astype(f32), wide)
            owner_sum = owner_sum + jnp.where(jnp.broadcast_to(cluster, wide) == mine, wide_owner, 0.0)
        return owner_sum, chosen, owned_before + jnp.sum(is_mine, axis=1, keepdims=True)

    start = (jnp.zeros(wide, f32), jnp.zeros(wide, f32), jnp.zeros((1, 1), f32))
    owner_sum, chosen, _ = lax.fori_loop(0, drops // 128, scan, start)
    home_owner = jnp.broadcast_to(jnp.sum(owner_sum, axis=1, keepdims=True), wide)
    owner_lanes = home_owner.T
    rank = jnp.sum(jnp.where((home_owner == owner_lanes) & (sub < lane), 1.0, 0.0), axis=0, keepdims=True)
    place_ref[0:1, :] = ((owner_lanes[0:1] * capacity + rank) * 3.0).astype(i32)
    fact = jnp.sum(chosen, axis=0, keepdims=True).astype(i32)
    cluster = fact & 16383
    anchor = cluster >> shift
    cluster_column = column(cluster, 128)
    cluster_wide = jnp.broadcast_to(cluster, wide)
    same = (cluster_column >> shift) == (cluster_wide >> shift)
    rank = jnp.sum(jnp.where(same & (cluster_column < cluster_wide), 1.0, 0.0), axis=0, keepdims=True)
    place_ref[1:2, :] = (anchor * capacity + rank.astype(i32)) * 3
    place_ref[2:3, :] = fact >> 14


def index_call(spec, facts, small):
    return pl.pallas_call(
        functools.partial(index_kernel, spec),
        out_shape=[jax.ShapeDtypeStruct((spec[6] // 128 + 1, 128), i32), jax.ShapeDtypeStruct((3, 128), i32)],
        in_specs=[smem, vmem],
        out_specs=[vmem, vmem],
        compiler_params=pltpu.CompilerParams(vmem_limit_bytes=vmem_limit),
        name="index_work",
    )(facts, small)


def pack_kernel(n, place_ref, *refs):
    *speed_refs, out_ref, speed_ref = refs
    total = speed_refs[0][: 3 * n, :]
    for part in speed_refs[1:]:
        total = total + part[: 3 * n, :]
    speed_ref[...] = total
    out_ref[...] = jnp.zeros_like(out_ref)

    def step(i, carry):
        for u in range(16):
            cluster = i * 16 + u
            out_ref[pl.ds(place_ref[0, cluster], 3), :] = speed_ref[pl.ds(3 * cluster, 3), :]
        return carry

    lax.fori_loop(0, n // 16, step, 0)


def pack_call(places, speeds, n, capacity, devices):
    slots = speeds[0].shape[1]
    return pl.pallas_call(
        functools.partial(pack_kernel, n),
        out_shape=jax.ShapeDtypeStruct((devices * capacity * 3, slots), f32),
        in_specs=[smem] + [vmem] * len(speeds),
        out_specs=vmem,
        scratch_shapes=[pltpu.VMEM((3 * n, slots), f32)],
        compiler_params=pltpu.CompilerParams(vmem_limit_bytes=vmem_limit),
        name="pack_owners",
    )(places, *speeds)


def unpack_kernel(n, place_ref, arrived_ref, out_ref, tile_ref):
    slots = arrived_ref.shape[1]
    lane = lax.broadcasted_iota(i32, (3, slots), 1)

    def step(i, carry):
        for u in range(16):
            cluster = i * 16 + u
            value = arrived_ref[pl.ds(place_ref[1, cluster], 3), :]
            tile_ref[cluster, :3, :] = jnp.where(lane < place_ref[2, cluster], value, 0.0)
        return carry

    lax.fori_loop(0, n // 16, step, 0)
    for k in range(3):
        out_ref[n * k : n * (k + 1), :] = tile_ref[:, k, :]


def unpack_call(places, arrived, n):
    slots = arrived.shape[1]
    return pl.pallas_call(
        functools.partial(unpack_kernel, n),
        out_shape=jax.ShapeDtypeStruct((3 * n, slots), f32),
        in_specs=[smem, vmem],
        out_specs=vmem,
        scratch_shapes=[pltpu.VMEM((n, 8, slots), f32)],
        compiler_params=pltpu.CompilerParams(vmem_limit_bytes=vmem_limit),
        name="unpack_drops",
    )(places, arrived)


def per_device(
    positions,
    normals,
    curvature,
    pair_targets,
    pair_sources,
    pair_count,
    node_counts,
    drop_clusters,
    drop_owner,
):
    n, slots = curvature.shape
    rows = lax.axis_size("row")
    cols = lax.axis_size("col")
    devices = rows * cols
    my_row = lax.axis_index("row")
    my_col = lax.axis_index("col")
    device = my_row * cols + my_col
    capacity = max(2, 2 * n // devices)
    hypercube = cols == 4
    hops = rows // 2 + 1

    def swap(value, bit):
        return lax.ppermute(value, "col", [(c, c ^ bit) for c in range(cols)])

    def component_major(value):
        return jnp.transpose(value, (1, 0, 2)).reshape(3 * n, slots)

    block, position, small = prep_call(
        (device * n).reshape(1),
        component_major(positions),
        component_major(normals),
        curvature,
        drop_clusters.T,
        node_counts.T,
        drop_owner.reshape(1, -1),
        pair_targets,
        pair_sources,
    )
    mate_block = swap(block, 1)
    if hypercube:
        across = swap(position, 2)
    to_right = [(r, (r + 1) % rows) for r in range(rows)]
    to_left = [((r + 1) % rows, r) for r in range(rows)]
    right = lax.ppermute(block, "row", to_right)
    left = lax.ppermute(block, "row", to_left)
    listed, places = index_call(
        (n, rows, cols, capacity, *drop_clusters.shape[::-1], pair_targets.shape[1], hypercube),
        jnp.stack([my_row, my_col, device, pair_count[0]]),
        small,
    )
    if hypercube:
        across, listed = lax.optimization_barrier((across, listed))
        targets = [block, mate_block, across, swap(across, 1)]
    else:
        gathered = lax.all_gather(position, "col", axis=0, tiled=True)
        targets = [gathered[3 * n * h : 3 * n * (h + 1)] for h in range(cols)]
    lists = [listed, swap(listed, 1)]

    total, token, all_targets = hop_call(n, 0, (), lists, targets, None, None, [block], [mate_block], hypercube)
    for hop in range(1, hops):
        if hop + 1 < hops:
            own = [right, left]
        *own, token = lax.optimization_barrier((*own, token))
        mates = [swap(part, 1) for part in own]
        if rows == 4 and hop == 1:
            passed = jnp.where(my_row % 2 == 0, own[0], own[1])
            opposite = [lax.ppermute(passed, "row", [(0, 1), (1, 0), (2, 3), (3, 2)])]
        elif hop + 1 < hops:
            right = lax.ppermute(own[0], "row", to_right)
            left = lax.ppermute(own[1], "row", to_left)
            opposite = [right]
        final = hop + 1 == hops
        emit = () if not final else ((2,), (3,)) if hypercube else (tuple(range(cols)),)
        total, token, *speed = hop_call(n, hop, emit, lists, [all_targets], token, total, own, mates, hypercube)
        if final:
            break
        own = opposite

    if hypercube:
        kept, sent = speed
        crossing, token = lax.optimization_barrier((kept + swap(sent, 1), token))
        across = swap(crossing, 2)
        _, _, kept, sent = hop_call(
            n, hops, ((0,), (1,)), lists, [all_targets], token, total, own, mates, hypercube
        )
        sent, across = lax.optimization_barrier((sent, across))
        home_speed = [kept, swap(sent, 1), across]
    else:
        home_speed = [lax.psum_scatter(speed[0], "col", scatter_dimension=0, tiled=True)]

    outgoing = pack_call(places, home_speed, n, capacity, devices)
    arrived = lax.all_to_all(outgoing, ("row", "col"), split_axis=0, concat_axis=0, tiled=True)
    result = unpack_call(places, arrived, n)
    return jnp.transpose(result.reshape(3, n, slots), (1, 0, 2))


def solution(mesh):
    in_specs = (
        P(("groups", "row", "col"), None, None),
        P(("groups", "row", "col"), None, None),
        P(("groups", "row", "col"), None),
        P(("groups", "row", "col"), None),
        P(("groups", "row", "col"), None),
        P(("groups", "row", "col")),
        P("groups", None),
        P("groups", None),
        P("groups"),
    )
    out_specs = P(("groups", "row", "col"), None, None)
    return jax.shard_map(
        per_device, mesh=mesh, in_specs=in_specs, out_specs=out_specs, check_vma=False
    )
```

```python
import functools
import math

import jax
import jax.numpy as jnp
from jax import lax
from jax.experimental import pallas as pl
from jax.experimental.pallas import tpu as pltpu
from jax.sharding import PartitionSpec as P

f32 = jnp.float32
bf16 = jnp.bfloat16
i32 = jnp.int32
regular_sq = 0.0025
length_scale = 1.0 / math.sqrt(regular_sq)
force_scale = length_scale / (8.0 * math.pi)
unroll = 8
levels = 2
vmem_limit = 24 * 2**20
kernel_flops = 8 * 10**9
whole_vmem = 60 * 2**20
vmem = pl.BlockSpec(memory_space=pltpu.VMEM)
smem = pl.BlockSpec(memory_space=pltpu.SMEM)
hbm = pl.BlockSpec(memory_space=pltpu.HBM)


def split3(value):
    high = value.astype(bf16)
    rest = value - high.astype(f32)
    mid = rest.astype(bf16)
    low = (rest - mid.astype(f32)).astype(bf16)
    return high.astype(f32), mid.astype(f32), low.astype(f32)


def rows16(upper, lower):
    return jnp.concatenate([upper, lower], axis=0).astype(bf16)


def transposed_left(y, f, slots):
    row = lax.broadcasted_iota(i32, (8, slots), 0)
    dot = -(y[0] * f[0] + y[1] * f[1] + y[2] * f[2])
    tile = jnp.where(row == 7, dot, 0.0)
    for k in range(3):
        tile = jnp.where(row == k, y[k], jnp.where(row == 3 + k, f[k], tile))
    high, mid, low = split3(tile)
    first = row < 3
    high_one = jnp.where(first, 1.0, high)
    left = jnp.concatenate(
        [rows16(high, mid), rows16(low, high_one), rows16(high_one, jnp.where(first, 1.0, mid))], axis=0
    )
    return left.T


def products(left, x, slots):
    row = lax.broadcasted_iota(i32, (8, slots), 0)
    zero = jnp.zeros((8, slots), f32)
    tile = jnp.where(row == 7, 1.0, zero)
    for k in range(3):
        tile = jnp.where((row == k) | (row == 3 + k), x[k], tile)
    high, mid, low = split3(tile)
    columns = []
    for k in range(3):
        mine = row == k
        minus = jnp.where(mine, -1.0, zero)
        columns.append(
            [
                rows16(minus, minus),
                rows16(minus, jnp.where(mine, high, 0.0)),
                rows16(jnp.where(mine, mid, 0.0), jnp.where(mine, low, 0.0)),
            ]
        )
    first = row < 3
    high, mid, low = [jnp.where(first, 0.0, part) for part in (high, mid, low)]
    columns.append([rows16(high, high), rows16(high, mid), rows16(low, mid)])
    for k in range(2):
        pick = jnp.where(row == 3 + k, 1.0, zero)
        columns.append([rows16(pick, pick), rows16(pick, zero), rows16(zero, zero)])
    right = jnp.concatenate([jnp.concatenate(column, axis=0) for column in columns], axis=1)
    return lax.dot_general(left, right, (((1,), (0,)), ((), ())), preferred_element_type=f32)


def node_sums(product, force_z, slots):
    row = lax.broadcasted_iota(i32, (8, slots), 0)
    total = None
    for g in range(product.shape[0] // 8):
        part = product[8 * g : 8 * g + 8]
        wx, wy, wz, dot, fx, fy = [part[:, slots * k : slots * (k + 1)] for k in range(6)]
        fz = force_z[8 * g : 8 * g + 8]
        inverse = lax.rsqrt(wx * wx + wy * wy + (wz * wz + 1.0))
        cube = inverse * inverse * inverse
        isotropic = inverse + cube
        project = dot * cube
        terms = (isotropic * fx + project * wx, isotropic * fy + project * wy, isotropic * fz + project * wz)
        total = terms if total is None else tuple(a + b for a, b in zip(total, terms))
    sums = [jnp.broadcast_to(jnp.sum(part, axis=0, keepdims=True), (8, slots)) for part in total]
    return jnp.where(row == 0, sums[0], jnp.where(row == 1, sums[1], jnp.where(row == 2, sums[2], 0.0)))


def hop_kernel(spec, list_ref, mate_list_ref, *refs):
    n, slots, hop, homes, own, mate, first, emit, split = spec
    refs = list(refs)
    if first:
        target_refs = [refs.pop(0) for _ in range(homes)]
    else:
        target_ref, _, _ = refs.pop(0), refs.pop(0), refs.pop(0)
    own_refs = [refs.pop(0) for _ in range(own)]
    mate_refs = [refs.pop(0) for _ in range(mate)]
    if first:
        total_ref, token_ref, target_ref = refs.pop(0), refs.pop(0), refs.pop(0)
    else:
        total_ref, token_ref = refs.pop(0), refs.pop(0)
        out_refs = [refs.pop(0) for _ in emit]
    source_ref, left_ref = refs
    token_ref[...] = jnp.zeros_like(token_ref)
    clusters = homes * n
    shift = n.bit_length() - 1
    if first:
        for h in range(homes):
            target_ref[3 * n * h : 3 * n * (h + 1), :] = target_refs[h][: 3 * n, :]
        total_ref[...] = jnp.zeros_like(total_ref)
    for place, block in list(enumerate(own_refs)) + [(2 + b, block) for b, block in enumerate(mate_refs)]:
        source_ref[6 * n * place : 6 * n * (place + 1), :] = block[...]

    bound_row = list_ref.shape[0] - 1

    def wide(value):
        return jnp.broadcast_to(value, (8, slots))

    def run(level, until):
        groups = slots // 8 * (levels - level) // levels
        lane, end = hop * levels + level, hop * levels + until
        own_start, own_end = list_ref[bound_row, lane], list_ref[bound_row, end]
        mate_start, mate_end = mate_list_ref[bound_row, lane], mate_list_ref[bound_row, end]
        own_count = (own_end - own_start + 1) >> 1
        count = own_count + ((mate_end - mate_start) >> 1)
        after_own = mate_start + 1 - 2 * own_count

        def entry(index):
            live = index < count
            mine = index < own_count
            place = jnp.where(live, 2 * index + jnp.where(mine, own_start, after_own), 0)
            row, column_of = place >> 7, place & 127
            packed = jnp.where(mine, list_ref[row, column_of], mate_list_ref[row, column_of])
            packed = jnp.where(live, packed, 0)
            target = (packed & 0xFFF) ^ jnp.where(mine, 0, n if split else 0)
            source = (packed >> 12) + jnp.where(mine, 0, 2 * n)
            return live, target, jnp.where(live, source, 0)

        def fetch(index, u):
            _, _, source = entry(index)
            base = source + (source >> shift) * (5 * n)
            values = [wide(source_ref[pl.ds(base + n * k, 1), :]) for k in range(6)]
            left_ref[u] = transposed_left(values[:3], values[3:], slots)

        @pl.when(count > 0)
        def _():
            for u in range(unroll):
                fetch(u, u)

        def step(i, carry):
            results = []
            lefts = [left_ref[u, : 8 * groups] for u in range(unroll)]
            for u in range(unroll):
                live, target, source = entry(i * unroll + u)
                base = target + (target >> shift) * (2 * n)
                x = [wide(target_ref[pl.ds(base + n * k, 1), :]) for k in range(3)]
                product = products(lefts[u], x, slots)
                force_z = source_ref[pl.ds(source + (source >> shift) * (5 * n) + 5 * n, 1), :]
                force_z = jnp.broadcast_to(force_z, (slots, slots)).T
                results.append((jnp.where(live, target, clusters), node_sums(product, force_z, slots)))
            for u in range(unroll):
                fetch((i + 1) * unroll + u, u)
            for target, result in results:
                total_ref[pl.ds(target * 4, 4), :] += result[:4]
            return carry

        lax.fori_loop(0, (count + unroll - 1) // unroll, step, 0)

    if emit:
        run(0, levels)
    else:
        for level in range(levels):
            run(level, level + 1)
    for out_ref, out_homes in zip(out_refs if emit else [], emit):
        for place, h in enumerate(out_homes):

            def move(i, carry, h=h, out_ref=out_ref, first_row=3 * n * place):
                for u in range(8):
                    tile = total_ref[pl.ds((n * h + i * 8 + u) * 4, 4), :]
                    out_ref[pl.ds(first_row + i * 24 + 3 * u, 3), :] = tile[:3]
                return carry

            lax.fori_loop(0, n // 8, move, 0)


def hop_call(n, hop, emit, lists, targets, token, total, own, mate, split):
    first = hop == 0
    slots = own[0].shape[1]
    homes = len(targets) if first else targets[0].shape[0] // (3 * n)
    total_shape = jax.ShapeDtypeStruct((homes * n * 4 + 8, slots), f32)
    aliases = {}
    operands = [*lists, *targets]
    if not first:
        operands += [token, total]
    out_shape = [total_shape, jax.ShapeDtypeStruct((8, 128), f32)]
    if first:
        out_shape += [jax.ShapeDtypeStruct((homes * 3 * n, slots), f32)]
    out_shape += [jax.ShapeDtypeStruct((len(out_homes) * 3 * n, slots), f32) for out_homes in emit]
    if not first:
        aliases = {len(operands) - 1: 0}
    operands += [*own, *mate]
    spec = (n, slots, hop, homes, len(own), len(mate), first, emit, split)
    return pl.pallas_call(
        functools.partial(hop_kernel, spec),
        out_shape=out_shape,
        in_specs=[smem, smem] + [vmem] * (len(operands) - 2),
        out_specs=[vmem] * len(out_shape),
        scratch_shapes=[
            pltpu.VMEM((4 * 6 * n, slots), f32),
            pltpu.VMEM((unroll, slots, 48), bf16),
        ],
        input_output_aliases=aliases,
        compiler_params=pltpu.CompilerParams(vmem_limit_bytes=vmem_limit),
        cost_estimate=pl.CostEstimate(flops=kernel_flops if hop else kernel_flops // 8, bytes_accessed=10**6, transcendentals=10**6),
        name=f"pairs_hop{hop}",
    )(*operands)


def column(row, rows):
    return jnp.broadcast_to(row, (rows, 128)).T


def prep_kernel(n, base_ref, *refs):
    ins, (out_ref, own_ref, small_ref), held, sems = refs[:8], refs[8:11], refs[11:19], refs[19]
    copies = [pltpu.make_async_copy(a, b, sems.at[k]) for k, (a, b) in enumerate(zip(ins, held))]
    for copy in copies[3:5] + copies[:3] + copies[5:]:
        copy.start()
    position_ref, normal_ref, curvature_ref, cluster_ref, count_ref, owner_ref, target_ref, source_ref = held
    slots = position_ref.shape[1]
    for copy in copies[3:5]:
        copy.wait()
    mine = base_ref[0] + lax.broadcasted_iota(i32, (n, 128), 0)
    total = jnp.zeros((n, 128), f32)
    for k in range(cluster_ref.shape[0]):
        for j in range(cluster_ref.shape[1] // 128):
            part = slice(128 * j, 128 * (j + 1))
            cluster = jnp.broadcast_to(cluster_ref[k : k + 1, part], (n, 128))
            count = jnp.broadcast_to(count_ref[k : k + 1, part].astype(f32), (n, 128))
            total = total + jnp.where(cluster == mine, count, 0.0)
    live_count = jnp.sum(total, axis=1, keepdims=True)
    for copy in copies[:3] + copies[5:]:
        copy.wait()
    scaled = position_ref[...] * length_scale
    out_ref[: 3 * n, :] = scaled
    own_ref[...] = scaled
    lane = lax.broadcasted_iota(i32, (n, slots), 1).astype(f32)
    strength = jnp.where(lane < live_count, curvature_ref[...] * force_scale, 0.0)
    for k in range(3):
        out_ref[n * (3 + k) : n * (4 + k), :] = normal_ref[n * k : n * (k + 1), :] * strength
    per_drop, drops = cluster_ref.shape
    pairs = target_ref.shape[1]
    small_ref[:per_drop, :drops] = cluster_ref[...] + (count_ref[...] << 14)
    small_ref[per_drop : per_drop + 1, :drops] = owner_ref[...]
    small_ref[per_drop + 1 : per_drop + 2, :pairs] = target_ref[...]
    small_ref[per_drop + 2 : per_drop + 3, :pairs] = source_ref[...]


def prep_call(base, *operands):
    n, slots = operands[2].shape
    per_drop, drops = operands[3].shape
    small = (per_drop + 8, max(drops, operands[6].shape[1]))
    shapes = [((6 * n, slots), f32), ((3 * n, slots), f32), (small, i32)]
    return pl.pallas_call(
        functools.partial(prep_kernel, n),
        out_shape=[jax.ShapeDtypeStruct(*shape) for shape in shapes],
        in_specs=[smem] + [hbm] * 8,
        out_specs=[vmem] * 3,
        scratch_shapes=[pltpu.VMEM(x.shape, x.dtype) for x in operands] + [pltpu.SemaphoreType.DMA((8,))],
        compiler_params=pltpu.CompilerParams(vmem_limit_bytes=whole_vmem),
        name="prep_sources",
    )(base, *operands)


def index_kernel(spec, facts_ref, *refs):
    n, rows, cols, capacity, per_drop, drops, pair_slots, split = spec
    small_ref, list_ref, place_ref = refs
    my_row, my_col, device, live_pairs = [facts_ref[k] for k in range(4)]
    shift = n.bit_length() - 1
    wide = (128, 128)
    lane_row = lax.broadcasted_iota(i32, (1, 128), 1)
    sub = lax.broadcasted_iota(i32, wide, 0)
    lane = lax.broadcasted_iota(i32, wide, 1)

    blocks = pair_slots // 128
    wide_source = []
    for b in range(blocks):
        source = small_ref[per_drop + 2 : per_drop + 3, 128 * b : 128 * (b + 1)]
        cluster = ((source >> shift) * cols + my_col) * n + (source & (n - 1))
        wide_source.append(jnp.broadcast_to(cluster, wide))

    def look_up(j, counts):
        part = pl.ds(pl.multiple_of(j * 128, 128), 128)
        for k in range(per_drop):
            fact = column(small_ref[k : k + 1, part], 128)
            cluster, count = fact & 16383, (fact >> 14).astype(f32)
            counts = [c + jnp.where(cluster == w, count, 0.0) for c, w in zip(counts, wide_source)]
        return counts

    counts = lax.fori_loop(0, drops // 128, look_up, [jnp.zeros(wide, f32)] * blocks)
    keys, packs = [], []
    for b in range(blocks):
        target = small_ref[per_drop + 1 : per_drop + 2, 128 * b : 128 * (b + 1)]
        source = small_ref[per_drop + 2 : per_drop + 3, 128 * b : 128 * (b + 1)]
        ahead = ((source >> shift) - my_row) & (rows - 1)
        hop = jnp.minimum(ahead, rows - ahead)
        index = lane_row + 128 * b
        if split:
            hop = jnp.where((hop == rows // 2) & (((target >> shift) ^ my_col) < 2), hop + 1, hop)
        key = jnp.where(index < live_pairs, hop, rows)
        count = jnp.sum(counts[b], axis=0, keepdims=True)
        level = jnp.zeros((1, 128), i32)
        for k in range(1, levels):
            level = level + jnp.where(count <= n * k / levels, 1, 0)
        keys.append((key * levels + level) * (128 * blocks) + index)
        home = target >> shift
        if split:
            home = home ^ my_col
        side = jnp.where((ahead > 0) & (ahead * 2 < rows), n, 0)
        packs.append((home * n + (target & (n - 1)) + (side + (source & (n - 1))) * 4096).astype(f32))
    key_columns = [column(key, 128) for key in keys]
    order_columns = []
    for b in range(blocks):
        before = jnp.zeros(wide, f32)
        for c in range(blocks):
            before = before + jnp.where(key_columns[c] < jnp.broadcast_to(keys[b], wide), 1.0, 0.0)
        order_columns.append(column(jnp.sum(before, axis=0, keepdims=True), 128))
    pack_columns = [column(pack, 128) for pack in packs]
    lanes = lane.astype(f32)
    for b in range(blocks):
        ordered = jnp.zeros(wide, f32)
        for c in range(blocks):
            ordered = ordered + jnp.where(order_columns[c] == lanes + 128.0 * b, pack_columns[c], 0.0)
        list_ref[b : b + 1, :] = jnp.sum(ordered, axis=0, keepdims=True).astype(i32)
    below = jnp.zeros(wide, f32)
    for c in range(blocks):
        below = below + jnp.where(key_columns[c] < lane * (128 * blocks), 1.0, 0.0)
    list_ref[blocks : blocks + 1, :] = jnp.sum(below, axis=0, keepdims=True).astype(i32)

    mine = device * n + sub

    def scan(j, carry):
        owner_sum, chosen, owned_before = carry
        part = pl.ds(pl.multiple_of(j * 128, 128), 128)
        owner = small_ref[per_drop : per_drop + 1, part]
        is_mine = jnp.where(owner == device, 1.0, 0.0)
        mine_column = column(is_mine, 128)
        rank = jnp.sum(jnp.where(sub < lane, mine_column, 0.0), axis=0, keepdims=True) + owned_before
        slot = jnp.where(owner == device, rank, -1.0)
        picked = column(slot, 128) == (lane // per_drop).astype(f32)
        for k in range(per_drop):
            fact = small_ref[k : k + 1, part]
            cluster = fact & 16383
            chosen = chosen + jnp.where(picked & (lane % per_drop == k), column(fact.astype(f32), 128), 0.0)
            wide_owner = jnp.broadcast_to(owner.astype(f32), wide)
            owner_sum = owner_sum + jnp.where(jnp.broadcast_to(cluster, wide) == mine, wide_owner, 0.0)
        return owner_sum, chosen, owned_before + jnp.sum(is_mine, axis=1, keepdims=True)

    start = (jnp.zeros(wide, f32), jnp.zeros(wide, f32), jnp.zeros((1, 1), f32))
    owner_sum, chosen, _ = lax.fori_loop(0, drops // 128, scan, start)
    home_owner = jnp.broadcast_to(jnp.sum(owner_sum, axis=1, keepdims=True), wide)
    owner_lanes = home_owner.T
    rank = jnp.sum(jnp.where((home_owner == owner_lanes) & (sub < lane), 1.0, 0.0), axis=0, keepdims=True)
    place_ref[0:1, :] = ((owner_lanes[0:1] * capacity + rank) * 3.0).astype(i32)
    fact = jnp.sum(chosen, axis=0, keepdims=True).astype(i32)
    cluster = fact & 16383
    anchor = cluster >> shift
    cluster_column = column(cluster, 128)
    cluster_wide = jnp.broadcast_to(cluster, wide)
    same = (cluster_column >> shift) == (cluster_wide >> shift)
    rank = jnp.sum(jnp.where(same & (cluster_column < cluster_wide), 1.0, 0.0), axis=0, keepdims=True)
    place_ref[1:2, :] = (anchor * capacity + rank.astype(i32)) * 3
    place_ref[2:3, :] = fact >> 14


def index_call(spec, facts, small):
    return pl.pallas_call(
        functools.partial(index_kernel, spec),
        out_shape=[jax.ShapeDtypeStruct((spec[6] // 128 + 1, 128), i32), jax.ShapeDtypeStruct((3, 128), i32)],
        in_specs=[smem, vmem],
        out_specs=[vmem, vmem],
        compiler_params=pltpu.CompilerParams(vmem_limit_bytes=vmem_limit),
        name="index_work",
    )(facts, small)


def pack_kernel(n, place_ref, *refs):
    *speed_refs, out_ref, speed_ref = refs
    total = speed_refs[0][: 3 * n, :]
    for part in speed_refs[1:]:
        total = total + part[: 3 * n, :]
    speed_ref[...] = total
    out_ref[...] = jnp.zeros_like(out_ref)

    def step(i, carry):
        for u in range(16):
            cluster = i * 16 + u
            out_ref[pl.ds(place_ref[0, cluster], 3), :] = speed_ref[pl.ds(3 * cluster, 3), :]
        return carry

    lax.fori_loop(0, n // 16, step, 0)


def pack_call(places, speeds, n, capacity, devices):
    slots = speeds[0].shape[1]
    return pl.pallas_call(
        functools.partial(pack_kernel, n),
        out_shape=jax.ShapeDtypeStruct((devices * capacity * 3, slots), f32),
        in_specs=[smem] + [vmem] * len(speeds),
        out_specs=vmem,
        scratch_shapes=[pltpu.VMEM((3 * n, slots), f32)],
        compiler_params=pltpu.CompilerParams(vmem_limit_bytes=vmem_limit),
        name="pack_owners",
    )(places, *speeds)


def unpack_kernel(n, place_ref, arrived_ref, out_ref, tile_ref):
    slots = arrived_ref.shape[1]
    lane = lax.broadcasted_iota(i32, (3, slots), 1)

    def step(i, carry):
        for u in range(16):
            cluster = i * 16 + u
            value = arrived_ref[pl.ds(place_ref[1, cluster], 3), :]
            tile_ref[cluster, :3, :] = jnp.where(lane < place_ref[2, cluster], value, 0.0)
        return carry

    lax.fori_loop(0, n // 16, step, 0)
    for k in range(3):
        out_ref[n * k : n * (k + 1), :] = tile_ref[:, k, :]


def unpack_call(places, arrived, n):
    slots = arrived.shape[1]
    return pl.pallas_call(
        functools.partial(unpack_kernel, n),
        out_shape=jax.ShapeDtypeStruct((3 * n, slots), f32),
        in_specs=[smem, vmem],
        out_specs=vmem,
        scratch_shapes=[pltpu.VMEM((n, 8, slots), f32)],
        compiler_params=pltpu.CompilerParams(vmem_limit_bytes=vmem_limit),
        name="unpack_drops",
    )(places, arrived)


def per_device(
    positions,
    normals,
    curvature,
    pair_targets,
    pair_sources,
    pair_count,
    node_counts,
    drop_clusters,
    drop_owner,
):
    n, slots = curvature.shape
    rows = lax.axis_size("row")
    cols = lax.axis_size("col")
    devices = rows * cols
    my_row = lax.axis_index("row")
    my_col = lax.axis_index("col")
    device = my_row * cols + my_col
    capacity = max(2, 2 * n // devices)
    hypercube = cols == 4
    hops = rows // 2 + 1

    def swap(value, bit):
        return lax.ppermute(value, "col", [(c, c ^ bit) for c in range(cols)])

    def component_major(value):
        return jnp.transpose(value, (1, 0, 2)).reshape(3 * n, slots)

    block, position, small = prep_call(
        (device * n).reshape(1),
        component_major(positions),
        component_major(normals),
        curvature,
        drop_clusters.T,
        node_counts.T,
        drop_owner.reshape(1, -1),
        pair_targets,
        pair_sources,
    )
    mate_block = swap(block, 1)
    if hypercube:
        across = swap(position, 2)
    to_right = [(r, (r + 1) % rows) for r in range(rows)]
    to_left = [((r + 1) % rows, r) for r in range(rows)]
    right = lax.ppermute(block, "row", to_right)
    left = lax.ppermute(block, "row", to_left)
    listed, places = index_call(
        (n, rows, cols, capacity, *drop_clusters.shape[::-1], pair_targets.shape[1], hypercube),
        jnp.stack([my_row, my_col, device, pair_count[0]]),
        small,
    )
    if hypercube:
        across, listed = lax.optimization_barrier((across, listed))
        targets = [block, mate_block, across, swap(across, 1)]
    else:
        gathered = lax.all_gather(position, "col", axis=0, tiled=True)
        targets = [gathered[3 * n * h : 3 * n * (h + 1)] for h in range(cols)]
    lists = [listed, swap(listed, 1)]

    total, token, all_targets = hop_call(n, 0, (), lists, targets, None, None, [block], [mate_block], hypercube)
    for hop in range(1, hops):
        if hop + 1 < hops:
            own = [right, left]
        *own, token = lax.optimization_barrier((*own, token))
        mates = [swap(part, 1) for part in own]
        if rows == 4 and hop == 1:
            passed = jnp.where(my_row % 2 == 0, own[0], own[1])
            opposite = [lax.ppermute(passed, "row", [(0, 1), (1, 0), (2, 3), (3, 2)])]
        elif hop + 1 < hops:
            right = lax.ppermute(own[0], "row", to_right)
            left = lax.ppermute(own[1], "row", to_left)
            opposite = [right]
        final = hop + 1 == hops
        emit = () if not final else ((2,), (3,)) if hypercube else (tuple(range(cols)),)
        total, token, *speed = hop_call(n, hop, emit, lists, [all_targets], token, total, own, mates, hypercube)
        if final:
            break
        own = opposite

    if hypercube:
        kept, sent = speed
        crossing, token = lax.optimization_barrier((kept + swap(sent, 1), token))
        across = swap(crossing, 2)
        _, _, kept, sent = hop_call(
            n, hops, ((0,), (1,)), lists, [all_targets], token, total, own, mates, hypercube
        )
        sent, across = lax.optimization_barrier((sent, across))
        home_speed = [kept, swap(sent, 1), across]
    else:
        home_speed = [lax.psum_scatter(speed[0], "col", scatter_dimension=0, tiled=True)]

    outgoing = pack_call(places, home_speed, n, capacity, devices)
    arrived = lax.all_to_all(outgoing, ("row", "col"), split_axis=0, concat_axis=0, tiled=True)
    result = unpack_call(places, arrived, n)
    return jnp.transpose(result.reshape(3, n, slots), (1, 0, 2))


def solution(mesh):
    in_specs = (
        P(("groups", "row", "col"), None, None),
        P(("groups", "row", "col"), None, None),
        P(("groups", "row", "col"), None),
        P(("groups", "row", "col"), None),
        P(("groups", "row", "col"), None),
        P(("groups", "row", "col")),
        P("groups", None),
        P("groups", None),
        P("groups"),
    )
    out_specs = P(("groups", "row", "col"), None, None)
    return jax.shard_map(
        per_device, mesh=mesh, in_specs=in_specs, out_specs=out_specs, check_vma=False
    )
```
